256 devices in a mesh: dp: 8 (over x_hi, y), patch: 32 (over x_lo, z, core).
Axes of the slice: x: 4 (x_hi: 2, x_lo: 2; x = x_hi * 2 + x_lo), y: 4, z: 8, core: 2. Of those that a mesh axis runs over, the one named last changes fastest.
Arguments:
- latent: bfloat16 [8, 64, 64, 640], P('dp', 'patch'), may hold values from -6 to 6
- cotangent: bfloat16 [8, 64, 64, 640], P('dp', 'patch'), may hold values from -6 to 6
- conv_weight: bfloat16 [3, 3, 640, 640], replicated, may hold values from -0.078125 to 0.078125
- query_weight: bfloat16 [640, 320], replicated, may hold values from -0.25 to 0.25
- key_weight: bfloat16 [640, 320], replicated, may hold values from -0.25 to 0.25
- value_weight: bfloat16 [640, 320], replicated, may hold values from -0.25 to 0.25
- out_weight: bfloat16 [320, 640], replicated, may hold values from -0.3125 to 0.3125
Outputs:
- grad_latent: bfloat16 [8, 64, 64, 640], P('dp', 'patch')
- grad_conv: float32 [3, 3, 640, 640], P(None, None, 'patch')
- grad_query: float32 [640, 320], replicated
- grad_key: float32 [640, 320], replicated
- grad_value: float32 [640, 320], replicated
- grad_out: float32 [320, 640], replicated
The draws below stay inside these ranges and needn't reach their ends.
All inputs are finite; a program needn't handle non-finite values.
Results may differ from the reference program's by a relative error of at most 0.018.
Values may be sent and summed in bfloat16 or wider, within the bound.
A program may use at most 128 MiB of HBM per device.

```python
import jax
import jax.numpy as jnp
from jax import lax

C = 640
NH = 5
HD = 64
COLS = 64
AW = 320
ROWS = 64
IMAGES = 8


def block_scale(own_key, extent, shards, smallest, largest):
    def one(axis_at, blocks):
        steps = jax.random.uniform(jax.random.fold_in(jax.random.fold_in(own_key, 6), axis_at), (blocks,), jnp.float32, smallest / len(shards), largest / len(shards))
        return jnp.repeat(jnp.exp(steps), extent[axis_at] // blocks).reshape((-1,) + (1,) * (len(extent) - axis_at - 1))

    gain = one(*shards[0])
    for cut in shards[1:]:
        gain = gain * one(*cut)
    return gain


def noise(stream_key, shape, deviation, reach, split=(), kind=jnp.bfloat16):
    level = block_scale(stream_key, shape, split, -0.22, 0.18) if split else 1.0
    drawn = jax.random.normal(stream_key, shape, jnp.float32) * deviation * level
    return jnp.minimum(jnp.maximum(drawn, -reach), reach).astype(kind)


def setup_inputs(seed: int = 0) -> dict:
    arg_keys = jax.random.split(jax.random.key(seed), 8)
    return {
        "latent": noise(arg_keys[0], (IMAGES, ROWS, COLS, C), 1.0, 6.0, ((0, 8), (1, 32))),
        "cotangent": noise(arg_keys[1], (IMAGES, ROWS, COLS, C), 1.0, 6.0, ((0, 8), (1, 32))),
        "conv_weight": noise(arg_keys[2], (3, 3, C, C), (9 * C) ** -0.5, 0.078125),
        "query_weight": noise(arg_keys[3], (C, AW), C ** -0.5, 0.25),
        "key_weight": noise(arg_keys[4], (C, AW), C ** -0.5, 0.25),
        "value_weight": noise(arg_keys[5], (C, AW), C ** -0.5, 0.25),
        "out_weight": noise(arg_keys[6], (AW, C), AW ** -0.5, 0.3125),
    }


def conv_rows(padded, weight, rows, cols, backward):
    total = jnp.zeros((rows * cols, weight.shape[3]), jnp.float32)
    for first in range(3):
        for second in range(3):
            window = padded[first:first + rows, second:second + cols].reshape(rows * cols, -1)
            if backward:
                tap = weight[2 - first, 2 - second]
                dims = (((1,), (1,)), ((), ()))
            else:
                tap = weight[first, second]
                dims = (((1,), (0,)), ((), ()))
            total = total + lax.dot_general(window, tap, dims, preferred_element_type=jnp.float32)
    return total


def outer_sum(left, right):
    return lax.dot_general(left, right, (((0,), (0,)), ((), ())), preferred_element_type=jnp.float32)


def one_image(latent, cotangent, conv_weight, query_weight, key_weight, value_weight, out_weight):
    rows, cols, chans = latent.shape
    count = rows * cols
    scale = HD ** -0.5
    padded = jnp.pad(latent, ((1, 1), (1, 1), (0, 0)))
    hidden = conv_rows(padded, conv_weight, rows, cols, False).astype(jnp.bfloat16)
    query = jnp.dot(hidden, query_weight, preferred_element_type=jnp.float32).astype(jnp.bfloat16)
    key = jnp.dot(hidden, key_weight, preferred_element_type=jnp.float32).astype(jnp.bfloat16)
    value = jnp.dot(hidden, value_weight, preferred_element_type=jnp.float32).astype(jnp.bfloat16)
    qh = query.reshape(count, NH, HD).astype(jnp.float32)
    kh = key.reshape(count, NH, HD).astype(jnp.float32)
    vh = value.reshape(count, NH, HD).astype(jnp.float32)
    scores = jnp.einsum('qhd,khd->hqk', qh, kh) * scale
    top = jnp.max(scores, axis=2, keepdims=True)
    lse = top + jnp.log(jnp.sum(jnp.exp(scores - top), axis=2, keepdims=True))
    probs = jnp.exp(scores - lse)
    probs_b = probs.astype(jnp.bfloat16)
    attended = jnp.einsum('hqk,khd->qhd', probs_b.astype(jnp.float32), vh)
    attended_b = attended.reshape(count, AW).astype(jnp.bfloat16)
    grad_flat = cotangent.reshape(count, chans)
    grad_att = lax.dot_general(grad_flat, out_weight, (((1,), (1,)), ((), ())), preferred_element_type=jnp.float32).astype(jnp.bfloat16)
    grad_out = outer_sum(attended_b, grad_flat)
    gh = grad_att.reshape(count, NH, HD).astype(jnp.float32)
    delta = jnp.sum(gh * attended, axis=2).T
    grad_probs = jnp.einsum('qhd,khd->hqk', gh, vh)
    grad_scores_b = (probs * (grad_probs - delta[:, :, None])).astype(jnp.bfloat16).astype(jnp.float32)
    grad_q = (jnp.einsum('hqk,khd->qhd', grad_scores_b, kh) * scale).reshape(count, AW).astype(jnp.bfloat16)
    grad_k = (jnp.einsum('hqk,qhd->khd', grad_scores_b, qh) * scale).reshape(count, AW).astype(jnp.bfloat16)
    grad_v = jnp.einsum('hqk,qhd->khd', probs_b.astype(jnp.float32), gh).reshape(count, AW).astype(jnp.bfloat16)
    grad_query = outer_sum(hidden, grad_q)
    grad_key = outer_sum(hidden, grad_k)
    grad_value = outer_sum(hidden, grad_v)
    back = (((1,), (1,)), ((), ()))
    grad_hidden = grad_flat.astype(jnp.float32)
    grad_hidden = grad_hidden + lax.dot_general(grad_q, query_weight, back, preferred_element_type=jnp.float32)
    grad_hidden = grad_hidden + lax.dot_general(grad_k, key_weight, back, preferred_element_type=jnp.float32)
    grad_hidden = grad_hidden + lax.dot_general(grad_v, value_weight, back, preferred_element_type=jnp.float32)
    grad_hidden = grad_hidden.astype(jnp.bfloat16)
    grad_pad = jnp.pad(grad_hidden.reshape(rows, cols, chans), ((1, 1), (1, 1), (0, 0)))
    grad_latent = conv_rows(grad_pad, conv_weight, rows, cols, True).reshape(rows, cols, chans).astype(jnp.bfloat16)
    taps = []
    for first in range(3):
        for second in range(3):
            window = padded[first:first + rows, second:second + cols].reshape(count, chans)
            taps.append(outer_sum(window, grad_hidden))
    grad_conv = jnp.stack(taps).reshape(3, 3, chans, chans)
    return grad_latent, grad_conv, grad_query, grad_key, grad_value, grad_out


def reference(latent, cotangent, conv_weight, query_weight, key_weight, value_weight, out_weight):
    def single(pair):
        return one_image(pair[0], pair[1], conv_weight, query_weight, key_weight, value_weight, out_weight)

    grad_latent, grad_conv, grad_query, grad_key, grad_value, grad_out = lax.map(single, (latent, cotangent))
    return (grad_latent, jnp.sum(grad_conv, axis=0), jnp.sum(grad_query, axis=0), jnp.sum(grad_key, axis=0), jnp.sum(grad_value, axis=0), jnp.sum(grad_out, axis=0))
```

```python
import functools
import jax
import jax.numpy as jnp
from jax import lax
from jax.experimental import pallas as pl
from jax.experimental.pallas import tpu as pltpu
from jax.sharding import PartitionSpec as P

NH = 5
HD = 64
AW = 320
MESH = pl.DeviceIdType.MESH
F32 = jnp.float32
BF16 = jnp.bfloat16


def place():
    p = lax.axis_index("patch")
    return lax.axis_index("dp"), p // 16, lax.rem(p, 16) // 2, lax.rem(p, 2)


def send(src, dst, send_sem, recv_sem, device):
    copy = pltpu.make_async_remote_copy(
        src_ref=src, dst_ref=dst, send_sem=send_sem, recv_sem=recv_sem,
        device_id=device, device_id_type=MESH,
    )
    copy.start()
    return copy


def greet(devices):
    barrier = pltpu.get_barrier_semaphore()
    for device in devices:
        pl.semaphore_signal(barrier, inc=1, device_id=device, device_id_type=MESH)
    pl.semaphore_wait(barrier, len(devices))


NT = (((1,), (1,)), ((), ()))
LOG2E = 1.4426950408889634


def remote(src, dst, send_sem, recv_sem, device):
    return pltpu.make_async_remote_copy(
        src_ref=src, dst_ref=dst, send_sem=send_sem, recv_sem=recv_sem,
        device_id=device, device_id_type=MESH,
    )


def attend_kernel(x_ref, out_ref, kv, qd, qs, gs, qt, gt, scores, slope, pb, sb, top, low, att, delta, dq,
                  part, box_up, box_down, ahead, behind, stage, res, kv_s, kv_r, qd_s, qd_r, up_s, up_r, down_s, down_r,
                  rup_s, rup_r, rdown_s, rdown_r, o_s, o_r, g_s, g_r):
    dp, xlo, z, core = place()
    j = xlo * 2 + core

    def at_z(step):
        return (dp, xlo * 16 + lax.rem(z + step + 8, 8) * 2 + core)

    def in_quad(step):
        m = lax.rem(j + step, 4)
        return m, (dp, (m // 2) * 16 + z * 2 + lax.rem(m, 2))

    def rows(m):
        return pl.ds(pl.multiple_of(m * 128, 128), 128)

    greet([at_z(1), at_z(-1)] + [in_quad(s)[1] for s in range(1, 4)])

    first, second = [], []
    for s in range(1, 4):
        m, device = in_quad(s)
        first.append(send(x_ref.at[m, 0:2], kv.at[z, :, rows(j), :], kv_s.at[s], kv_r.at[s], device))
    for s in range(1, 4):
        m, device = in_quad(s)
        second.append(send(x_ref.at[m, 2:4], qd.at[:, rows(j), :], qd_s.at[s], qd_r.at[s], device))
    for t in range(2):
        kv[z, t, rows(j), :] = x_ref[j, t]
        qd[t, rows(j), :] = x_ref[j, 2 + t]
    lane = lax.broadcasted_iota(jnp.int32, (128, 128), 1)
    left = lane < 64
    own = x_ref[j, 2:4].astype(F32)
    qs[512:640] = jnp.where(left, 0.0, own[0]).astype(BF16)
    gs[512:640] = jnp.where(left, 0.0, own[1]).astype(BF16)
    top[...] = jnp.full(top.shape, -jnp.inf, F32)
    low[...] = jnp.zeros(low.shape, F32)
    att[...] = jnp.zeros(att.shape, F32)
    dq[...] = jnp.zeros(dq.shape, F32)

    def ring_up(s):
        k = lax.rem(z + 8 - s, 8)
        return remote(kv.at[k], kv.at[k], up_s.at[s], up_r.at[s], at_z(1))

    def ring_down(s):
        k = lax.rem(z + s, 8)
        return remote(kv.at[k], kv.at[k], down_s.at[s], down_r.at[s], at_z(-1))

    for copy in first:
        copy.wait()
    ring_up(0).start()
    ring_down(0).start()
    for copy in second:
        copy.wait()
    for m in range(4):
        pair = qd[:, m * 128 : m * 128 + 128, :].astype(F32)
        qs[m * 128 : m * 128 + 128] = jnp.where(left, pair[0], 0.0).astype(BF16)
        gs[m * 128 : m * 128 + 128] = jnp.where(left, pair[1], 0.0).astype(BF16)
    qt[...] = qs[...].astype(F32).T.astype(BF16)
    gt[...] = gs[...].astype(F32).T.astype(BF16)

    def pass_one(t, carry):
        for s in range(4):
            @pl.when(t == 2 * s + 1)
            def _():
                ring_up(s).wait_recv()
                if s < 3:
                    ring_up(s + 1).start()

            if s < 3:
                @pl.when(t == 2 * s + 2)
                def _():
                    ring_down(s).wait_recv()
                    if s < 2:
                        ring_down(s + 1).start()

        offset = jnp.where(lax.rem(t, 2) == 1, 8 - (t + 1) // 2, t // 2)
        b = lax.rem(z + offset, 8)
        scores[b] = lax.dot_general(qs[...], kv[b, 0], NT, preferred_element_type=F32) * LOG2E
        for i in range(5):
            r = slice(128 * i, 128 * i + 128)
            s = scores[b, r]
            old = top[r]
            new = jnp.maximum(old, jnp.max(s, axis=1, keepdims=True))
            p = jnp.exp2(s - new)
            fade = jnp.exp2(old - new)
            low[r] = low[r] * fade + jnp.sum(p, axis=1, keepdims=True)
            top[r] = new
            att[r] = att[r] * fade
            pb[r] = p.astype(BF16)
        att[...] += jnp.dot(pb[...], kv[b, 1], preferred_element_type=F32)
        return carry

    lax.fori_loop(0, 8, pass_one, 0)
    for i in range(5):
        r = slice(128 * i, 128 * i + 128)
        value = att[r] / low[r]
        top[r] = top[r] + jnp.log2(low[r])
        att[r] = value
        delta[r] = jnp.sum(value * gs[r].astype(F32), axis=1, keepdims=True)
    stage[0] = att[0:512].astype(BF16)
    early = []
    for s in range(1, 4):
        m, device = in_quad(s)
        early.append(send(stage.at[0, rows(m), :], res.at[j, 0], o_s.at[s], o_r.at[s], device))

    def sum_up(s):
        return remote(box_up.at[s], ahead.at[s], rup_s.at[s], rup_r.at[s], at_z(1))

    def sum_down(s):
        return remote(
            box_down.at[s], behind.at[s], rdown_s.at[s], rdown_r.at[s], at_z(-1),
        )

    def pass_two(t, carry):
        offset = jnp.where(lax.rem(t, 2) == 0, 4 + t // 2, 4 - (t + 1) // 2)
        b = lax.rem(z + offset, 8)
        slope[...] = lax.dot_general(gs[...], kv[b, 1], NT, preferred_element_type=F32)
        for i in range(5):
            r = slice(128 * i, 128 * i + 128)
            p = jnp.exp2(scores[b, r] - top[r])
            pb[r] = p.astype(BF16)
            sb[r] = (p * (slope[r] - delta[r])).astype(BF16)
        dq[...] += jnp.dot(sb[...], kv[b, 0], preferred_element_type=F32)
        part[0] = jnp.dot(qt[...], sb[...], preferred_element_type=F32)
        part[1] = jnp.dot(gt[...], pb[...], preferred_element_type=F32)

        @pl.when(t == 0)
        def _():
            box_up[0] = part[...].astype(BF16)
            sum_up(0).start()

        @pl.when(t == 2)
        def _():
            box_down[0] = part[...].astype(BF16)
            sum_down(0).start()

        for s in range(3):
            @pl.when(t == 2 * s + 1)
            def _():
                sum_up(s).wait_recv()
                box_up[s + 1] = (part[...] + ahead[s].astype(F32)).astype(BF16)
                sum_up(s + 1).start()

        for s in range(2):
            @pl.when(t == 2 * s + 4)
            def _():
                sum_down(s).wait_recv()
                box_down[s + 1] = (part[...] + behind[s].astype(F32)).astype(BF16)
                sum_down(s + 1).start()

        return carry

    lax.fori_loop(0, 8, pass_two, 0)
    stage[1] = (dq[0:512] * HD ** -0.5).astype(BF16)
    sum_up(3).wait_recv()
    sum_down(2).wait_recv()
    for t in range(2):
        whole = part[t] + ahead[3, t].astype(F32) + behind[2, t].astype(F32)
        stage[2 + t] = whole.T.astype(BF16)
    late = []
    for s in range(1, 4):
        m, device = in_quad(s)
        late.append(send(stage.at[1:4, rows(m), :], res.at[j, 1:4], g_s.at[s], g_r.at[s], device))
    for t in range(4):
        res[j, t] = stage[t, rows(j), :]
    for s in range(4):
        ring_up(s).wait_send()
        sum_up(s).wait_send()
    for s in range(3):
        ring_down(s).wait_send()
        sum_down(s).wait_send()
    for copy in early + late:
        copy.wait()

    def swap(a):
        return pltpu.roll(a, 64, axis=1)

    last = [att[512:640], dq[512:640] * HD ** -0.5]
    for t in range(2, 4):
        last.append(sum(res[m, t].astype(F32) for m in range(4)))
    for t in range(4):
        for i in range(2):
            pair = jnp.where(left, res[2 * i, t].astype(F32), swap(res[2 * i + 1, t].astype(F32)))
            out_ref[t, :, 128 * i : 128 * i + 128] = pair.astype(BF16)
        out_ref[t, :, 256:384] = jnp.where(left, swap(last[t]), 0.0).astype(BF16)


def attend(x):
    dma = pltpu.SemaphoreType.DMA
    vmem = pl.BlockSpec(memory_space=pltpu.VMEM)
    return pl.pallas_call(
        attend_kernel,
        out_shape=jax.ShapeDtypeStruct((4, 128, 384), BF16),
        in_specs=[vmem],
        out_specs=vmem,
        scratch_shapes=[
            pltpu.VMEM((8, 2, 512, 128), BF16),
            pltpu.VMEM((2, 512, 128), BF16),
            pltpu.VMEM((640, 128), BF16),
            pltpu.VMEM((640, 128), BF16),
            pltpu.VMEM((128, 640), BF16),
            pltpu.VMEM((128, 640), BF16),
            pltpu.VMEM((8, 640, 512), F32),
            pltpu.VMEM((640, 512), F32),
            pltpu.VMEM((640, 512), BF16),
            pltpu.VMEM((640, 512), BF16),
            pltpu.VMEM((640, 1), F32),
            pltpu.VMEM((640, 1), F32),
            pltpu.VMEM((640, 128), F32),
            pltpu.VMEM((640, 1), F32),
            pltpu.VMEM((640, 128), F32),
            pltpu.VMEM((2, 128, 512), F32),
            pltpu.VMEM((4, 2, 128, 512), BF16),
            pltpu.VMEM((3, 2, 128, 512), BF16),
            pltpu.VMEM((4, 2, 128, 512), BF16),
            pltpu.VMEM((3, 2, 128, 512), BF16),
            pltpu.VMEM((4, 512, 128), BF16),
            pltpu.VMEM((4, 4, 128, 128), BF16),
            dma((4,)), dma((4,)), dma((4,)), dma((4,)),
            dma((4,)), dma((4,)), dma((3,)), dma((3,)),
            dma((4,)), dma((4,)), dma((3,)), dma((3,)),
            dma((4,)), dma((4,)), dma((4,)), dma((4,)),
        ],
        compiler_params=pltpu.CompilerParams(
            collective_id=1, has_side_effects=True, vmem_limit_bytes=48 * 1024 * 1024
        ),
        name="attend",
    )(x)


def shifted(rows, j):
    before = jnp.where(j == 0, 0.0, pltpu.roll(rows, 1, axis=0))
    after = jnp.where(j == 63, 0.0, pltpu.roll(rows, 63, axis=0))
    return before, rows, after


def first_kernel(lat_ref, cot_ref, wq_ref, wk_ref, wv_ref, wo_ref, w_ref, hid_ref, x_ref, lhs_ref,
                 w, w_sem, halo, turned, sbuf, share, sh, acc, tmp, halo_s, halo_r, share_s, share_r):
    dp = lax.axis_index("dp")
    p = lax.axis_index("patch")

    def at(step):
        other = lax.rem(p + step + 32, 32)
        return other, (dp, other)

    loads = []
    for t in range(9):
        copy = pltpu.make_async_copy(w_ref.at[t], w.at[t], w_sem.at[t])
        copy.start()
        loads.append(copy)
    barrier = pltpu.get_barrier_semaphore()

    def hello(s, carry):
        pl.semaphore_signal(barrier, inc=1, device_id=at(s)[1], device_id_type=MESH)
        return carry

    lax.fori_loop(1, 32, hello, 0)
    turned[0:640] = lat_ref[...].astype(F32).T
    turned[640:656] = jnp.zeros((16, 128), F32)
    for k in range(32):
        sbuf[k] = turned[20 * k : 20 * k + 32].astype(BF16)
    share[0] = jnp.zeros((32, 128), BF16)
    share[33] = jnp.zeros((32, 128), BF16)
    share[p + 1] = sbuf[p]
    pl.semaphore_wait(barrier, 31)
    near = [
        send(lat_ref.at[64:128], halo.at[0], halo_s.at[0], halo_r.at[0], at(1)[1]),
        send(lat_ref.at[0:64], halo.at[1], halo_s.at[1], halo_r.at[1], at(-1)[1]),
    ]

    def share_copy(s):
        other, device = at(s)
        return remote(sbuf.at[other], share.at[p + 1], share_s.at[s], share_r.at[s], device)

    def share_start(s, carry):
        share_copy(s).start()
        return carry

    lax.fori_loop(1, 32, share_start, 0)

    lane = lax.broadcasted_iota(jnp.int32, (128, 128), 1)
    left = lane < 64

    def pack(value, t):
        tmp[:, 0:320] = value.astype(BF16).astype(F32)
        low, mid = tmp[:, 0:128], tmp[:, 128:256]
        last = pltpu.roll(tmp[:, 256:384], 64, axis=1)
        heads = (low, pltpu.roll(low, 64, axis=1), mid, pltpu.roll(mid, 64, axis=1))
        for m in range(4):
            x_ref[m, t] = jnp.where(left, heads[m], last).astype(BF16)

    tmp[:, 256:384] = jnp.zeros((128, 128), F32)
    pack(lax.dot_general(cot_ref[...], wo_ref[...], NT, preferred_element_type=F32), 3)
    for copy in near:
        copy.wait()
    j = lax.broadcasted_iota(jnp.int32, (64, 640), 0)
    rows = (
        jnp.where(p > 0, halo[0].astype(F32), 0.0),
        lat_ref[0:64].astype(F32),
        lat_ref[64:128].astype(F32),
        jnp.where(p < 31, halo[1].astype(F32), 0.0),
    )
    for r in range(4):
        moved = shifted(rows[r], j)
        for b in range(3):
            sh[b, 64 * r : 64 * r + 64] = moved[b].astype(BF16)
    for t in range(9):
        a, b = t // 3, t % 3
        loads[t].wait()
        term = jnp.dot(sh[b, 64 * a : 64 * a + 128], w[t], preferred_element_type=F32)
        if t:
            acc[...] += term
        else:
            acc[...] = term
    hid_ref[...] = acc[...].astype(BF16)
    pack(jnp.dot(hid_ref[...], wk_ref[...], preferred_element_type=F32), 0)
    pack(jnp.dot(hid_ref[...], wv_ref[...], preferred_element_type=F32), 1)
    pack(jnp.dot(hid_ref[...], wq_ref[...], preferred_element_type=F32), 2)
    for m in range(4):
        x_ref[m, 2] = (x_ref[m, 2].astype(F32) * HD ** -0.5).astype(BF16)

    def share_end(s, carry):
        share_copy(s).wait()
        return carry

    lax.fori_loop(1, 32, share_end, 0)
    col = lax.broadcasted_iota(jnp.int32, (32, 128), 1)
    side = col < 64
    col = lax.rem(col, 64)

    def windows(q, carry):
        here = share[q + 1].astype(F32)
        turn = pltpu.roll(here, 64, axis=1)
        above = jnp.where(side, pltpu.roll(share[q].astype(F32), 64, axis=1), turn)
        below = jnp.where(side, turn, pltpu.roll(share[q + 2].astype(F32), 64, axis=1))
        place = pl.ds(pl.multiple_of(lax.rem(q, 2) * 128, 128), 128)
        for a, value in enumerate((above, here, below)):
            three = (
                jnp.where(col == 0, 0.0, pltpu.roll(value, 1, axis=1)),
                value,
                jnp.where(col == 63, 0.0, pltpu.roll(value, 127, axis=1)),
            )
            for b in range(3):
                t = 3 * a + b
                lhs_ref[q // 2, 32 * t : 32 * t + 32, place] = three[b].astype(BF16)
        return carry

    lax.fori_loop(0, 32, windows, 0)


def first(latent, cotangent, wq, wk, wv, wo, taps):
    dma = pltpu.SemaphoreType.DMA
    vmem = pl.BlockSpec(memory_space=pltpu.VMEM)
    return pl.pallas_call(
        first_kernel,
        out_shape=(
            jax.ShapeDtypeStruct((128, 640), BF16),
            jax.ShapeDtypeStruct((4, 4, 128, 128), BF16),
            jax.ShapeDtypeStruct((16, 288, 256), BF16),
        ),
        in_specs=[vmem] * 6 + [pl.BlockSpec(memory_space=pl.ANY)],
        out_specs=(vmem,) * 3,
        scratch_shapes=[
            pltpu.VMEM((9, 640, 640), BF16),
            dma((9,)),
            pltpu.VMEM((2, 64, 640), BF16),
            pltpu.VMEM((656, 128), F32),
            pltpu.VMEM((32, 32, 128), BF16),
            pltpu.VMEM((34, 32, 128), BF16),
            pltpu.VMEM((3, 256, 640), BF16),
            pltpu.VMEM((128, 640), F32),
            pltpu.VMEM((128, 384), F32),
            dma((2,)), dma((2,)), dma((32,)), dma((32,)),
        ],
        compiler_params=pltpu.CompilerParams(
            collective_id=2, has_side_effects=True, vmem_limit_bytes=48 * 1024 * 1024
        ),
        name="first",
    )(latent, cotangent, wq, wk, wv, wo, taps)


def finish_kernel(parts_ref, hid_ref, cot_ref, wq_ref, wk_ref, wv_ref, lhs_ref, w_ref, out_ref, taps_ref, lat_ref,
                  w, w_sem, gh, halo, sh, acc, prod, small, dqk, dva, dvb, turned, aturned, xs, half, ya, yb, yc, yd,
                  plane, xin, xsum, zin, zfull, pfull, ob, tb, tin, halo_s, halo_r, up_s, down_s, over_s, sib_s, own_r, sib_r,
                  pair_s, pair_r, y_s, y_r, x_s, x_r, z_s, z_r, zb_s, zb_r, xb_s, xb_r, yb_s, yb_r, fin_s, fin_r,
                  t_s, t_r, u_s, u_r):
    dp, xlo, z, core = place()
    p = lax.axis_index("patch")
    xhi, y = dp // 4, lax.rem(dp, 4)
    x = xhi * 2 + xlo
    sib = (dp, xlo * 16 + z * 2 + 1 - core)
    over = (dp, (1 - xlo) * 16 + z * 2 + core)

    def at_z(s):
        other = lax.rem(z + s + 8, 8)
        return other, (dp, xlo * 16 + other * 2 + core)

    def at_y(s):
        other = lax.rem(y + s + 4, 4)
        return other, (xhi * 4 + other, p)

    def at_x(s):
        other = lax.rem(x + s, 4)
        return other, (other // 2 * 4 + y, lax.rem(other, 2) * 16 + z * 2 + core)

    def at_dp(s):
        other = lax.rem(dp + s, 8)
        return other, (other, p)

    def at_p(s):
        return (dp, lax.rem(p + s + 32, 32))

    loads = []
    for t in range(9):
        copy = pltpu.make_async_copy(w_ref.at[t], w.at[t], w_sem.at[t])
        copy.start()
        loads.append(copy)
    greet(
        [sib, at_p(1), at_p(-1)]
        + [at_z(s)[1] for s in range(1, 8)]
        + [at_x(s)[1] for s in range(1, 4)]
        + [at_dp(s)[1] for s in range(1, 8)]
    )
    mine = pl.ds(pl.multiple_of(core * 128, 128), 128)
    sent = []

    value = cot_ref[...].astype(F32)
    for t, ref in ((1, wq_ref), (2, wk_ref), (3, wv_ref)):
        value = value + lax.dot_general(parts_ref[t, :, 0:AW], ref[...], NT, preferred_element_type=F32)
    here = xlo * 8 + z
    gh[here, mine, :] = value.astype(BF16)

    ways = {"up": (up_s, at_z(1)[1]), "down": (down_s, at_z(-1)[1]), "over": (over_s, over), "sib": (sib_s, sib)}
    count = {way: 0 for way in ways}

    def block(kind, dz):
        return (xlo if kind == "o" else 1 - xlo) * 8 + lax.rem(z + dz + 8, 8)

    def ship(u, *names):
        for way in names:
            sem, device = ways[way]
            ref = gh.at[u, mine, :]
            recv = sib_r if way == "sib" else own_r
            sent.append(send(ref, ref, sem.at[count[way]], recv.at[u], device))
            count[way] += 1

    def arrive(kind, dz, *names):
        u = block(kind, dz)
        ref = gh.at[u, mine, :]
        remote(ref, ref, up_s.at[0], own_r.at[u], sib).wait_recv()
        ship(u, *names)

    edge = gh.at[here]
    low = pl.ds(pl.multiple_of(core * 128, 64), 64)
    high = pl.ds(pl.multiple_of(core * 128 + 64, 64), 64)
    near = [
        send(edge.at[high, :], halo.at[0], halo_s.at[0], halo_r.at[0], at_p(1)),
        send(edge.at[low, :], halo.at[1], halo_s.at[1], halo_r.at[1], at_p(-1)),
    ]
    ship(here, "up", "down", "over", "sib")

    lane = lax.broadcasted_iota(jnp.int32, (128, 128), 1)
    left = lane < 64

    def chunk(t, n):
        return parts_ref[t, :, 128 * n : 128 * n + 128].astype(F32)

    def swap(a):
        return pltpu.roll(a, 64, axis=1)

    def put(ref, n, a):
        ref[:, 128 * n : 128 * n + 128] = a.astype(BF16)

    k0, k1, k2 = (swap(chunk(2, n)) for n in range(3))
    v0, v1, v2 = (swap(chunk(3, n)) for n in range(3))
    zero = jnp.zeros((128, 128), F32)
    for n, a in enumerate((chunk(1, 0), chunk(1, 1), jnp.where(left, chunk(1, 2), k0), jnp.where(left, k0, k1),
                           jnp.where(left, k1, k2))):
        put(dqk, n, a)
    for n, a in enumerate((chunk(3, 0), chunk(3, 1), chunk(3, 2), zero, zero)):
        put(dva, n, a)
    for n, a in enumerate((zero, zero, jnp.where(left, 0.0, v0), jnp.where(left, v0, v1), jnp.where(left, v1, v2))):
        put(dvb, n, a)
    turned[...] = hid_ref[...].astype(F32).T.astype(BF16)
    aturned[...] = parts_ref[0].astype(F32).T.astype(BF16)

    def keep(first_row, value):
        for n in range(5):
            start = 1280 * n + first_row
            xs[start : start + value.shape[0]] = value[:, 128 * n : 128 * n + 128].astype(BF16)

    def mm(a, b):
        return jnp.dot(a, b, preferred_element_type=F32)

    keep(0, mm(turned[0:320], dqk[...]))
    keep(320, mm(turned[320:640], dqk[...]))
    keep(640, mm(aturned[0:320], cot_ref[...]))
    keep(960, mm(turned[0:320], dva[...]) + mm(turned[320:640], dvb[...]))

    def part(c, k):
        return pl.ds(pl.multiple_of(c * 3200 + k * 800, 16), 800)

    pair = [send(xs.at[part(1 - core, k)], half.at[k], pair_s.at[k], pair_r.at[k], sib) for k in range(4)]
    arrive("o", -1, "up", "over", "sib")
    arrive("o", 1, "down", "over", "sib")
    arrive("p", 0, "sib")

    for copy in near:
        copy.wait()
    j = lax.broadcasted_iota(jnp.int32, (64, 640), 0)
    rows = (
        jnp.where(p > 0, halo[0].astype(F32), 0.0),
        gh[here, low, :].astype(F32),
        gh[here, high, :].astype(F32),
        jnp.where(p < 31, halo[1].astype(F32), 0.0),
    )
    for r in range(4):
        moved = shifted(rows[r], j)
        for b in range(3):
            sh[2 - b, 64 * r : 64 * r + 64] = moved[b].astype(BF16)

    def tap(t):
        a, b = t // 3, t % 3
        loads[t].wait()
        start = 64 * (2 - a)
        term = lax.dot_general(sh[b, start : start + 128], w[t], NT, preferred_element_type=F32)
        if t:
            acc[...] += term
        else:
            acc[...] = term

    for copy in pair:
        copy.wait()
    for k in range(4):
        half[k] = (half[k].astype(F32) + xs[part(core, k)].astype(F32)).astype(BF16)
    far = lax.rem(y + 2, 4)
    y_up, y_down = at_y(1), at_y(-1)
    sent.append(send(half.at[far, 0:400], ya, y_s.at[0], y_r.at[0], y_up[1]))
    sent.append(send(half.at[far, 400:800], yb, y_s.at[1], y_r.at[1], y_down[1]))
    tap(0)
    tap(1)
    arrive("o", -2, "up", "over", "sib")
    arrive("o", 2, "down", "over", "sib")
    remote(half.at[far, 0:400], ya, y_s.at[0], y_r.at[0], sib).wait_recv()
    remote(half.at[far, 400:800], yb, y_s.at[1], y_r.at[1], sib).wait_recv()
    half[y_up[0], 0:400] = (half[y_up[0], 0:400].astype(F32) + ya[...].astype(F32)).astype(BF16)
    half[y_down[0], 400:800] = (half[y_down[0], 400:800].astype(F32) + yb[...].astype(F32)).astype(BF16)
    sent.append(send(half.at[y_up[0]], yc, y_s.at[2], y_r.at[2], y_up[1]))
    sent.append(send(half.at[y_down[0]], yd, y_s.at[3], y_r.at[3], y_down[1]))
    tap(2)
    tap(3)
    arrive("p", -1, "sib")
    arrive("p", 1, "sib")
    tap(4)
    arrive("o", -3, "up", "sib")
    arrive("o", 3, "sib")
    remote(half.at[0], yc, y_s.at[2], y_r.at[2], sib).wait_recv()
    remote(half.at[0], yd, y_s.at[3], y_r.at[3], sib).wait_recv()
    plane[0:800] = (half[y].astype(F32) + yc[...].astype(F32) + yd[...].astype(F32)).astype(BF16)
    plane[800:1024] = jnp.zeros((224, 128), BF16)

    def quarter(k):
        return pl.ds(pl.multiple_of(k * 256, 256), 256)

    def slot(k):
        return pl.ds(pl.multiple_of(k * 32, 32), 32)

    crossing = []
    for s in range(1, 4):
        other, device = at_x(s)
        crossing.append(send(plane.at[quarter(other)], xin.at[s], x_s.at[s], x_r.at[s], device))
    tap(5)
    tap(6)
    arrive("p", -2, "up", "sib")
    arrive("p", 2, "down", "sib")
    whole = plane[quarter(x)].astype(F32)
    for s in range(1, 4):
        crossing[s - 1].wait()
        whole = whole + xin[s].astype(F32)
    xsum[...] = whole.astype(BF16)
    along = []
    for s in range(1, 8):
        other, device = at_z(s)
        along.append(send(xsum.at[slot(other)], zin.at[s], z_s.at[s], z_r.at[s], device))
    tap(7)
    tap(8)
    lat_ref[...] = acc[...].astype(BF16)
    arrive("o", 4, "sib")
    whole = xsum[slot(z)].astype(F32)
    for s in range(1, 8):
        along[s - 1].wait()
        whole = whole + zin[s].astype(F32)
    zfull[slot(z)] = whole.astype(BF16)
    zback = []
    for s in range(1, 8):
        ref = zfull.at[slot(z)]
        zback.append(send(ref, ref, zb_s.at[s], zb_r.at[s], at_z(s)[1]))

    def gain(kind, dz, start=False):
        u = block(kind, dz)
        ref = gh.at[u, pl.ds(pl.multiple_of((1 - core) * 128, 128), 128), :]
        remote(ref, ref, up_s.at[0], sib_r.at[u], sib).wait_recv()
        term = jnp.dot(lhs_ref[u], gh[u], preferred_element_type=F32)
        if start:
            prod[...] = term
        else:
            prod[...] += term

    gain("o", 0, True)
    gain("p", 0)
    arrive("p", -3, "sib")
    arrive("p", 3, "down", "sib")
    gain("o", -1)
    gain("o", 1)
    for copy in zback:
        copy.wait()
    pfull[quarter(x)] = zfull[...]
    xback = []
    for s in range(1, 4):
        ref = pfull.at[quarter(x)]
        xback.append(send(ref, ref, xb_s.at[s], xb_r.at[s], at_x(s)[1]))
    gain("p", -1)
    gain("p", 1)
    gain("o", -2)
    gain("o", 2)
    arrive("p", 4, "sib")
    for copy in xback:
        copy.wait()
    ob[part(core, y)] = pfull[0:800]

    def whole_part(k, send_sem, recv_sem, device):
        ref = ob.at[part(core, k)]
        return send(ref, ref, send_sem, recv_sem, device)

    def half_part(k, first, send_sem, recv_sem, device):
        start = core * 3200 + k * 800 + (0 if first else 400)
        ref = ob.at[pl.ds(pl.multiple_of(start, 16), 400)]
        return send(ref, ref, send_sem, recv_sem, device)

    sent.append(whole_part(y, yb_s.at[0], yb_r.at[0], y_up[1]))
    sent.append(whole_part(y, yb_s.at[1], yb_r.at[1], y_down[1]))
    fin = [whole_part(y, fin_s.at[0], fin_r.at[0], sib)]
    gain("o", -3)
    gain("o", 3)
    gain("p", -2)
    gain("p", 2)
    ref = ob.at[part(core, y_down[0])]
    remote(ref, ref, yb_s.at[0], yb_r.at[0], sib).wait_recv()
    ref = ob.at[part(core, y_up[0])]
    remote(ref, ref, yb_s.at[1], yb_r.at[1], sib).wait_recv()
    sent.append(half_part(y_down[0], True, yb_s.at[2], yb_r.at[2], y_up[1]))
    sent.append(half_part(y_up[0], False, yb_s.at[3], yb_r.at[3], y_down[1]))
    fin.append(whole_part(y_down[0], fin_s.at[1], fin_r.at[1], sib))
    fin.append(whole_part(y_up[0], fin_s.at[2], fin_r.at[2], sib))
    gain("o", 4)
    gain("p", -3)
    gain("p", 3)
    gain("p", 4)

    for t in range(9):
        small[20 * t : 20 * t + 20] = prod[32 * t : 32 * t + 20]
    small[180:192] = jnp.zeros((12, 640), F32)
    for n in range(5):
        piece = small[:, 128 * n : 128 * n + 128].astype(BF16)
        for i in range(12):
            f = 192 * n + 16 * i
            tb[f // 128, f % 128 : f % 128 + 16] = piece[16 * i : 16 * i + 16]
    tb[7, 64:128] = jnp.zeros((64, 128), BF16)
    there = []
    for s in range(1, 8):
        other, device = at_dp(s)
        there.append(send(tb.at[other], tin.at[s], t_s.at[s], t_r.at[s], device))
    ref = ob.at[pl.ds(pl.multiple_of(core * 3200 + far * 800, 16), 400)]
    remote(ref, ref, yb_s.at[2], yb_r.at[2], sib).wait_recv()
    ref = ob.at[pl.ds(pl.multiple_of(core * 3200 + far * 800 + 400, 16), 400)]
    remote(ref, ref, yb_s.at[3], yb_r.at[3], sib).wait_recv()
    fin.append(whole_part(far, fin_s.at[3], fin_r.at[3], sib))
    whole = tb[dp].astype(F32)
    for s in range(1, 8):
        there[s - 1].wait()
        whole = whole + tin[s].astype(F32)
    taps_ref[dp] = whole.astype(BF16)
    tback = []
    for s in range(1, 8):
        ref = taps_ref.at[dp]
        tback.append(send(ref, ref, u_s.at[s], u_r.at[s], at_dp(s)[1]))
    for copy in fin:
        copy.wait()
    for n in range(5):
        out_ref[:, 128 * n : 128 * n + 128] = ob[1280 * n : 1280 * n + 1280]
    for copy in sent:
        copy.wait_send()
    for copy in tback:
        copy.wait()


def finish(parts, hidden, cotangent, wq, wk, wv, lhs, taps):
    dma = pltpu.SemaphoreType.DMA
    vmem = pl.BlockSpec(memory_space=pltpu.VMEM)

    def b16(*shape):
        return pltpu.VMEM(shape, BF16)

    def f32(*shape):
        return pltpu.VMEM(shape, F32)

    return pl.pallas_call(
        finish_kernel,
        out_shape=(
            jax.ShapeDtypeStruct((1280, 640), BF16),
            jax.ShapeDtypeStruct((8, 128, 128), BF16),
            jax.ShapeDtypeStruct((128, 640), BF16),
        ),
        in_specs=[vmem] * 7 + [pl.BlockSpec(memory_space=pl.ANY)],
        out_specs=(vmem,) * 3,
        scratch_shapes=[
            b16(9, 640, 640), dma((9,)), b16(16, 256, 640), b16(2, 64, 640), b16(3, 256, 640), f32(128, 640),
            f32(288, 640), f32(192, 640), b16(128, 640), b16(128, 640), b16(128, 640), b16(640, 128), b16(384, 128),
            b16(6400, 128), b16(4, 800, 128), b16(400, 128), b16(400, 128), b16(800, 128), b16(800, 128),
            b16(1024, 128), b16(4, 256, 128), b16(256, 128), b16(8, 32, 128), b16(256, 128), b16(1024, 128),
            b16(6400, 128), b16(8, 128, 128), b16(8, 128, 128),
            dma((2,)), dma((2,)), dma((5,)), dma((5,)), dma((5,)), dma((16,)), dma((16,)), dma((16,)),
            dma((4,)), dma((4,)), dma((4,)), dma((4,)), dma((4,)), dma((4,)), dma((8,)), dma((8,)),
            dma((8,)), dma((8,)), dma((4,)), dma((4,)), dma((4,)), dma((4,)), dma((4,)), dma((4,)),
            dma((8,)), dma((8,)), dma((8,)), dma((8,)),
        ],
        compiler_params=pltpu.CompilerParams(
            collective_id=0, has_side_effects=True, vmem_limit_bytes=52 * 1024 * 1024
        ),
        name="finish",
    )(parts, hidden, cotangent, wq, wk, wv, lhs, taps)


def body(latent, cotangent, conv_weight, query_weight, key_weight, value_weight, out_weight):
    lat = latent.reshape(128, 640)
    cot = cotangent.reshape(128, 640)
    w = conv_weight.reshape(9, 640, 640)
    hidden, packed, lhs = first(lat, cot, query_weight, key_weight, value_weight, out_weight, w)
    parts = attend(packed)
    rows, taps, grad_latent = finish(parts, hidden, cot, query_weight, key_weight, value_weight, lhs, w)
    taps = taps.reshape(1024, 128)[:960].reshape(5, 192, 128)[:, :180].transpose(1, 0, 2)
    grad_conv = taps.reshape(3, 3, 20, 640).astype(F32)
    grad_value = jnp.concatenate([rows[960:, :320], rows[960:, 320:]], axis=0).astype(F32)
    return (
        grad_latent.reshape(latent.shape),
        grad_conv,
        rows[:640, :320].astype(F32),
        rows[:640, 320:].astype(F32),
        grad_value,
        rows[640:960].astype(F32),
    )


def solution(mesh):
    placed = (P("dp", "patch", None, None), P("dp", "patch", None, None), P(), P(), P(), P(), P())
    return jax.shard_map(
        body,
        mesh=mesh,
        in_specs=placed,
        out_specs=(P("dp", "patch", None, None), P(None, None, "patch", None), P(), P(), P(), P()),
        check_vma=False,
    )
```

```python
import functools
import jax
import jax.numpy as jnp
from jax import lax
from jax.experimental import pallas as pl
from jax.experimental.pallas import tpu as pltpu
from jax.sharding import PartitionSpec as P

NH = 5
HD = 64
AW = 320
MESH = pl.DeviceIdType.MESH
F32 = jnp.float32
BF16 = jnp.bfloat16


def place():
    p = lax.axis_index("patch")
    return lax.axis_index("dp"), p // 16, lax.rem(p, 16) // 2, lax.rem(p, 2)


def send(src, dst, send_sem, recv_sem, device):
    copy = pltpu.make_async_remote_copy(
        src_ref=src, dst_ref=dst, send_sem=send_sem, recv_sem=recv_sem,
        device_id=device, device_id_type=MESH,
    )
    copy.start()
    return copy


NT = (((1,), (1,)), ((), ()))
LOG2E = 1.4426950408889634


def remote(src, dst, send_sem, recv_sem, device):
    return pltpu.make_async_remote_copy(
        src_ref=src, dst_ref=dst, send_sem=send_sem, recv_sem=recv_sem,
        device_id=device, device_id_type=MESH,
    )


def attend_kernel(windows, lhs_ref, x_ref, out_ref, kv, kvt, qd, qs, gs, q4, g4, gt, gt4, scores, slope, pb, sb,
                  top, low, att, delta, dq, top4, low4, att4, delta4, dq4, part, box_up, box_down, ahead, behind,
                  mix, mix_in, stat, own4, stage, res,
                  kv_s, kv_r, qd_s, qd_r, up_s, up_r, down_s, down_r, rup_s, rup_r, rdown_s, rdown_r,
                  mix_s, mix_r, stat_s, stat_r, g_s, g_r):
    dp, xlo, z, core = place()
    j = xlo * 2 + core

    def at_z(step):
        return (dp, xlo * 16 + lax.rem(z + step + 8, 8) * 2 + core)

    def in_quad(step):
        m = lax.rem(j + step, 4)
        return m, (dp, (m // 2) * 16 + z * 2 + lax.rem(m, 2))

    def rows(m):
        return pl.ds(pl.multiple_of(m * 128, 128), 128)

    first, second = [], []
    for s in range(1, 4):
        m, device = in_quad(s)
        first.append(send(x_ref.at[2 * m], kv.at[z, rows(j), :], kv_s.at[s], kv_r.at[s], device))
    for s in range(1, 4):
        m, device = in_quad(s)
        second.append(send(x_ref.at[2 * m + 1], qd.at[0, rows(j), :], qd_s.at[0, s], qd_r.at[0, s], device))
        second.append(send(x_ref.at[8], qd.at[1, rows(j), :], qd_s.at[1, s], qd_r.at[1, s], device))
    kv[z, rows(j), :] = x_ref[2 * j]
    kv[z, 512:640] = x_ref[9]
    qd[0, rows(j), :] = x_ref[2 * j + 1]
    qd[1, rows(j), :] = x_ref[8]
    lane = lax.broadcasted_iota(jnp.int32, (128, 128), 1)
    left = lane < 64
    for ref in (top, top4):
        ref[...] = jnp.full(ref.shape, -jnp.inf, F32)
    for ref in (low, low4, att, att4, dq, dq4):
        ref[...] = jnp.zeros(ref.shape, F32)

    def ring_up(s):
        k = lax.rem(z + 8 - s, 8)
        ref = kv.at[k] if s < 3 else kv.at[k, 0:320]
        return remote(ref, ref, up_s.at[s], up_r.at[s], at_z(1))

    def ring_down(s):
        k = lax.rem(z + s, 8)
        ref = kv.at[k] if s < 3 else kv.at[k, 320:640]
        return remote(ref, ref, down_s.at[s], down_r.at[s], at_z(-1))

    for copy in first:
        copy.wait()
    ring_up(0).start()
    ring_down(0).start()
    windows(lhs_ref)
    for copy in second:
        copy.wait()
    for m in range(4):
        r = slice(m * 128, m * 128 + 128)
        for i, (a, b, bt) in enumerate(((qs, gs, gt), (q4, g4, gt4))):
            pair = qd[i, r].astype(F32)
            a[r] = jnp.where(left, pair, 0.0).astype(BF16)
            b[r] = jnp.where(left, 0.0, pair).astype(BF16)
            bt[:, r] = pair.T[64:128]

    def soften(b, keys, q, top, low, att):
        s = scores[b, keys, q]
        old = top[:, q]
        new = jnp.maximum(old, jnp.max(s, axis=0, keepdims=True))
        p = jnp.exp2(s - new)
        fade = jnp.exp2(old - new)
        low[:, q] = low[:, q] * fade + jnp.sum(p, axis=0, keepdims=True)
        top[:, q] = new
        att[:, q] = att[:, q] * fade
        pb[keys, q] = p.astype(BF16)

    main, side = slice(0, 512), slice(512, 640)
    quarters = [slice(128 * i, 128 * i + 128) for i in range(4)]

    def pass_one(t, carry):
        for s in range(3):
            @pl.when(t == 2 * s + 1)
            def _():
                ring_up(s).wait_recv()
                ring_up(s + 1).start()

            @pl.when(t == 2 * s + 2)
            def _():
                ring_down(s).wait_recv()
                ring_down(s + 1).start()

        @pl.when(t == 7)
        def _():
            ring_up(3).wait_recv()
            ring_down(3).wait_recv()

        offset = jnp.where(lax.rem(t, 2) == 1, 8 - (t + 1) // 2, t // 2)
        b = lax.rem(z + offset, 8)
        scores[b, main] = lax.dot_general(kv[b, main], qs[...], NT, preferred_element_type=F32) * LOG2E
        scores[b, side] = lax.dot_general(kv[b, side], q4[...], NT, preferred_element_type=F32) * LOG2E
        for i in range(5):
            c = slice(128 * i, 128 * i + 128)
            kvt[b, :, c] = kv[b, c].astype(F32).T.astype(BF16)
        for q in quarters:
            soften(b, main, q, top, low, att)
            soften(b, side, q, top4, low4, att4)
        att[...] += jnp.dot(kvt[b, 64:128, main], pb[main], preferred_element_type=F32)
        att4[...] += jnp.dot(kvt[b, 64:128, side], pb[side], preferred_element_type=F32)
        return carry

    lax.fori_loop(0, 8, pass_one, 0)
    for m in range(4):
        q = quarters[m]
        mix[m, 0:64] = att4[:, q]
        mix[m, 64:65] = top4[:, q]
        mix[m, 65:66] = low4[:, q]
        mix[m, 66:72] = jnp.zeros((6, 128), F32)
    mixing = []
    for s in range(1, 4):
        m, device = in_quad(s)
        mixing.append(send(mix.at[m], mix_in.at[s], mix_s.at[s], mix_r.at[s], device))
    mix_in[0] = mix[j]
    att[...] = att[...] / low[...]
    top[...] = top[...] + jnp.log2(low[...])
    delta[...] = jnp.sum(att[...] * gt[...], axis=0, keepdims=True)

    def stat_copy(s):
        return remote(stat.at[j], stat.at[j], stat_s.at[s], stat_r.at[s], in_quad(s)[1])

    for copy in mixing:
        copy.wait()
    tops = [mix_in[s, 64:65] for s in range(4)]
    best = jnp.maximum(jnp.maximum(tops[0], tops[1]), jnp.maximum(tops[2], tops[3]))
    total, blend = jnp.zeros((1, 128), F32), jnp.zeros((64, 128), F32)
    for s in range(4):
        weight = jnp.exp2(tops[s] - best)
        total = total + mix_in[s, 65:66] * weight
        blend = blend + mix_in[s, 0:64] * weight
    blend = blend / total
    own4[0:64] = blend
    own4[64:128] = jnp.zeros((64, 128), F32)
    stat[j, 0:1] = best + jnp.log2(total)
    stat[j, 1:2] = jnp.sum(blend * gt4[:, rows(j)], axis=0, keepdims=True)
    stat[j, 2:8] = jnp.zeros((6, 128), F32)
    for s in range(1, 4):
        stat_copy(s).start()

    def sum_up(s):
        r = slice(0, 320) if s == 0 else slice(0, 640)
        return remote(box_up.at[s, r], ahead.at[s, r], rup_s.at[s], rup_r.at[s], at_z(1))

    def sum_down(s):
        r = slice(320, 640) if s == 0 else slice(0, 640)
        return remote(box_down.at[s, r], behind.at[s, r], rdown_s.at[s], rdown_r.at[s], at_z(-1))

    def slopes(b, keys, q, top, delta):
        p = jnp.exp2(scores[b, keys, q] - top[:, q])
        pb[keys, q] = p.astype(BF16)
        sb[keys, q] = (p * (slope[keys, q] - delta[:, q])).astype(BF16)

    def pass_two(t, carry):
        offset = jnp.where(lax.rem(t, 2) == 0, 4 + t // 2, 4 - (t + 1) // 2)
        b = lax.rem(z + offset, 8)
        slope[main] = lax.dot_general(kv[b, main], gs[...], NT, preferred_element_type=F32)
        slope[side] = lax.dot_general(kv[b, side], g4[...], NT, preferred_element_type=F32)
        for q in quarters:
            slopes(b, main, q, top, delta)
        dq[...] += jnp.dot(kvt[b, 0:64, main], sb[main], preferred_element_type=F32)
        part[main] = jnp.dot(sb[main], qs[...], preferred_element_type=F32) + jnp.dot(
            pb[main], gs[...], preferred_element_type=F32
        )

        @pl.when(t == 0)
        def _():
            for s in range(1, 4):
                stat_copy(s).wait()
            for m in range(4):
                top4[:, quarters[m]] = stat[m, 0:1]
                delta4[:, quarters[m]] = stat[m, 1:2]

        for q in quarters:
            slopes(b, side, q, top4, delta4)
        dq4[...] += jnp.dot(kvt[b, 0:64, side], sb[side], preferred_element_type=F32)
        part[side] = jnp.dot(sb[side], q4[...], preferred_element_type=F32) + jnp.dot(
            pb[side], g4[...], preferred_element_type=F32
        )

        @pl.when(t == 0)
        def _():
            box_up[0, 0:320] = part[0:320].astype(BF16)
            sum_up(0).start()
            box_down[0, 320:640] = part[320:640].astype(BF16)
            sum_down(0).start()

        @pl.when(t == 1)
        def _():
            sum_up(0).wait_recv()
            box_up[1, 0:320] = (part[0:320] + ahead[0, 0:320].astype(F32)).astype(BF16)
            box_up[1, 320:640] = part[320:640].astype(BF16)
            sum_up(1).start()

        @pl.when(t == 2)
        def _():
            sum_down(0).wait_recv()
            box_down[1, 0:320] = part[0:320].astype(BF16)
            box_down[1, 320:640] = (part[320:640] + behind[0, 320:640].astype(F32)).astype(BF16)
            sum_down(1).start()

        for s in range(1, 3):
            @pl.when(t == 2 * s + 1)
            def _():
                sum_up(s).wait_recv()
                box_up[s + 1] = (part[...] + ahead[s].astype(F32)).astype(BF16)
                sum_up(s + 1).start()

            @pl.when(t == 2 * s + 2)
            def _():
                sum_down(s).wait_recv()
                box_down[s + 1] = (part[...] + behind[s].astype(F32)).astype(BF16)
                sum_down(s + 1).start()

        return carry

    lax.fori_loop(0, 8, pass_two, 0)
    for q in quarters:
        both = jnp.concatenate([dq[:, q] * HD ** -0.5, att[:, q]], axis=0)
        stage[0, q] = both.T.astype(BF16)
        both = jnp.concatenate([dq4[:, q] * HD ** -0.5, jnp.zeros((64, 128), F32)], axis=0)
        stage[1, q] = both.T.astype(BF16)
    late = []
    for s in range(1, 4):
        m, device = in_quad(s)
        late.append(send(stage.at[0:2, rows(m), :], res.at[j, 0:2], g_s.at[0, s], g_r.at[0, s], device))
    sum_up(3).wait_recv()
    sum_down(3).wait_recv()
    stage[2] = (part[main] + ahead[3, main].astype(F32) + behind[3, main].astype(F32)).astype(BF16)
    for s in range(1, 4):
        m, device = in_quad(s)
        late.append(send(stage.at[2, rows(m), :], res.at[j, 2], g_s.at[1, s], g_r.at[1, s], device))
    own = part[side] + ahead[3, side].astype(F32) + behind[3, side].astype(F32)
    for t in range(3):
        res[j, t] = stage[t, rows(j), :]
    for s in range(4):
        ring_up(s).wait_send()
        ring_down(s).wait_send()
        sum_up(s).wait_send()
        sum_down(s).wait_send()
    for copy in late:
        copy.wait()

    def swap(a):
        return pltpu.roll(a, 64, axis=1)

    for t, source, high in ((0, 0, True), (1, 0, False), (2, 2, False), (3, 2, True)):
        for i in range(2):
            a, b = res[2 * i, source].astype(F32), res[2 * i + 1, source].astype(F32)
            pair = jnp.where(left, swap(a), b) if high else jnp.where(left, a, swap(b))
            out_ref[t, :, 128 * i : 128 * i + 128] = pair.astype(BF16)
    last4 = (
        own4[...].T,
        sum(res[m, 1].astype(F32) for m in range(4)),
        own,
        swap(own),
    )
    for t in range(4):
        out_ref[t, :, 256:384] = jnp.where(left, last4[t], 0.0).astype(BF16)


def shifted(rows, j):
    before = jnp.where(j == 0, 0.0, pltpu.roll(rows, 1, axis=0))
    after = jnp.where(j == 63, 0.0, pltpu.roll(rows, 63, axis=0))
    return before, rows, after


def first_kernel(hbm, lat_ref, cot_ref, wq_ref, wk_ref, wv_ref, wo_ref, w, hid_ref, x_ref, load_sem, w_sem,
                 halo, turned, sbuf, share, sh, acc, tmp, halo_s, halo_r, share_s, share_r, rim_s, rim_r):
    dp, xlo, z, core = place()
    p = lax.axis_index("patch")
    spot = dp * 2 + xlo
    index = lax.rem(p, 16)

    def at(step):
        other = lax.rem(p + step + 32, 32)
        return (dp, other)

    local = (lat_ref, cot_ref, wo_ref, wk_ref, wv_ref, wq_ref)
    inputs = []
    for i, ref in enumerate(local):
        copy = pltpu.make_async_copy(hbm[i], ref, load_sem.at[i])
        copy.start()
        inputs.append(copy)
    loads = []
    for t in range(9):
        copy = pltpu.make_async_copy(hbm[6].at[t], w.at[t], w_sem.at[t])
        copy.start()
        loads.append(copy)
    barrier = pltpu.get_barrier_semaphore()

    def hello(s, carry):
        pl.semaphore_signal(barrier, inc=1, device_id=at(s), device_id_type=MESH)
        return carry

    def hello_plane(s, carry):
        other = lax.rem(spot + s, 16)
        device = (other // 2, lax.rem(other, 2) * 16 + index)
        pl.semaphore_signal(barrier, inc=1, device_id=device, device_id_type=MESH)
        return carry

    lax.fori_loop(1, 32, hello, 0)
    lax.fori_loop(1, 16, hello_plane, 0)
    inputs[0].wait()
    turned[0:640] = lat_ref[...].astype(F32).T
    turned[640:656] = jnp.zeros((16, 128), F32)
    for k in range(32):
        sbuf[k % 16, k // 16] = turned[20 * k : 20 * k + 32].astype(BF16)
    share[jnp.where(xlo == 0, 0, 17)] = jnp.zeros((2, 32, 128), BF16)
    share[index + 1] = sbuf[index]
    pl.semaphore_wait(barrier, 46)
    near = [
        send(lat_ref.at[64:128], halo.at[0], halo_s.at[0], halo_r.at[0], at(1)),
        send(lat_ref.at[0:64], halo.at[1], halo_s.at[1], halo_r.at[1], at(-1)),
    ]

    def share_copy(s):
        other = lax.rem(index + s, 16)
        return remote(sbuf.at[other], share.at[index + 1], share_s.at[s], share_r.at[s], (dp, xlo * 16 + other))

    rim = index == jnp.where(xlo == 0, 15, 0)
    rim_slot = jnp.where(xlo == 0, 0, 17)

    def rim_copy(s):
        return remote(sbuf.at[s], share.at[rim_slot], rim_s.at[s], rim_r.at[0], (dp, (1 - xlo) * 16 + s))

    def share_start(s, carry):
        share_copy(s).start()
        return carry

    def rim_start(s, carry):
        rim_copy(s).start()
        return carry

    lax.fori_loop(1, 16, share_start, 0)

    @pl.when(rim)
    def _():
        lax.fori_loop(0, 16, rim_start, 0)

    lane = lax.broadcasted_iota(jnp.int32, (128, 128), 1)
    left = lane < 64

    def pack(low_value, high_value, first_slot, last_slot):
        for n in range(3):
            c = slice(128 * n, min(128 * n + 128, AW))
            width = c.stop - c.start
            tmp[0, :, 0:width] = low_value[:, c]
            tmp[1, :, 0:width] = high_value[:, c]
            a, b = tmp[0], tmp[1]
            even = jnp.where(left, a, pltpu.roll(b, 64, axis=1)).astype(BF16)
            if n == 2:
                x_ref[last_slot] = even
            else:
                x_ref[4 * n + first_slot] = even
                x_ref[4 * n + 2 + first_slot] = jnp.where(left, pltpu.roll(a, 64, axis=1), b).astype(BF16)

    inputs[1].wait()
    inputs[2].wait()
    out_grad = lax.dot_general(cot_ref[...], wo_ref[...], NT, preferred_element_type=F32)
    tmp[...] = jnp.zeros(tmp.shape, F32)
    for copy in near:
        copy.wait()
    j = lax.broadcasted_iota(jnp.int32, (64, 640), 0)
    rows = (
        jnp.where(p > 0, halo[0].astype(F32), 0.0),
        lat_ref[0:64].astype(F32),
        lat_ref[64:128].astype(F32),
        jnp.where(p < 31, halo[1].astype(F32), 0.0),
    )
    for r in range(4):
        moved = shifted(rows[r], j)
        for b in range(3):
            sh[b, 64 * r : 64 * r + 64] = moved[b].astype(BF16)
    for t in range(9):
        a, b = t // 3, t % 3
        loads[t].wait()
        term = jnp.dot(sh[b, 64 * a : 64 * a + 128], w[t], preferred_element_type=F32)
        if t:
            acc[...] += term
        else:
            acc[...] = term
    hid_ref[...] = acc[...].astype(BF16)
    for copy in inputs[3:]:
        copy.wait()

    def project(ref):
        value = lax.dot_general(hid_ref[...], ref[...], NT, preferred_element_type=F32)
        return value.astype(BF16).astype(F32)

    pack(project(wk_ref), project(wv_ref), 0, 9)
    pack(project(wq_ref) * HD ** -0.5, out_grad, 1, 8)

    def windows(lhs_ref):
        def share_end(s, carry):
            share_copy(s).wait()
            return carry

        def rim_end(s, carry):
            rim_copy(s).wait_send()
            return carry

        lax.fori_loop(1, 16, share_end, 0)
        rim_copy(0).wait_recv()

        @pl.when(rim)
        def _():
            lax.fori_loop(0, 16, rim_end, 0)

        col = lax.broadcasted_iota(jnp.int32, (32, 128), 1)
        near_side = col < 64
        col = lax.rem(col, 64)

        def one(q, carry):
            lanes = pl.ds(pl.multiple_of(lax.rem(q, 2) * 128, 128), 128)
            for c in range(2):
                here = share[q + 1, c].astype(F32)
                turn = pltpu.roll(here, 64, axis=1)
                above = jnp.where(near_side, pltpu.roll(share[q, c].astype(F32), 64, axis=1), turn)
                below = jnp.where(near_side, turn, pltpu.roll(share[q + 2, c].astype(F32), 64, axis=1))
                for a, value in enumerate((above, here, below)):
                    three = (
                        jnp.where(col == 0, 0.0, pltpu.roll(value, 1, axis=1)),
                        value,
                        jnp.where(col == 63, 0.0, pltpu.roll(value, 127, axis=1)),
                    )
                    for b in range(3):
                        row = 288 * c + 32 * (3 * a + b)
                        lhs_ref[q // 2, row : row + 32, lanes] = three[b].astype(BF16)
            return carry

        lax.fori_loop(0, 16, one, 0)

    return windows


def finish_kernel(parts_ref, hid_ref, cot_ref, wq_ref, wk_ref, wv_ref, lhs_ref, w, out_ref, taps_ref, lat_ref,
                  gh, halo, sh, acc, prod, small, turned, xs, half, ya, yb, yc, yd,
                  plane, xin, xsum, zin, zfull, pfull, tb, tin, tfull, halo_s, halo_r, up_s, down_s, sib_s, own_r, sib_r,
                  pair_s, pair_r, y_s, y_r, x_s, x_r, z_s, z_r, zb_s, zb_r, xb_s, xb_r, yb_s, yb_r, fin_s, fin_r,
                  t_s, t_r, u_s, u_r):
    dp, xlo, z, core = place()
    p = lax.axis_index("patch")
    xhi, y = dp // 4, lax.rem(dp, 4)
    x = xhi * 2 + xlo
    sib = (dp, xlo * 16 + z * 2 + 1 - core)

    def at_z(s):
        other = lax.rem(z + s + 8, 8)
        return other, (dp, xlo * 16 + other * 2 + core)

    def at_y(s):
        other = lax.rem(y + s + 4, 4)
        return other, (xhi * 4 + other, p)

    def at_x(s):
        other = lax.rem(x + s, 4)
        return other, (other // 2 * 4 + y, lax.rem(other, 2) * 16 + z * 2 + core)

    spot = dp * 2 + xlo

    def at_spot(s):
        other = lax.rem(spot + s, 16)
        return other, (other // 2, lax.rem(other, 2) * 16 + z * 2 + core)

    def at_dp(s):
        other = lax.rem(dp + s, 8)
        return other, (other, p)

    def at_p(s):
        return (dp, lax.rem(p + s + 32, 32))

    mine = pl.ds(pl.multiple_of(core * 128, 128), 128)
    sent = []

    value = cot_ref[...].astype(F32)
    for t, ref in ((1, wq_ref), (2, wk_ref), (3, wv_ref)):
        value = value + jnp.dot(parts_ref[t, :, 0:AW], ref[...], preferred_element_type=F32)
    gh[z, mine, :] = value.astype(BF16)

    ways = {"up": (up_s, at_z(1)[1]), "down": (down_s, at_z(-1)[1]), "sib": (sib_s, sib)}
    count = {way: 0 for way in ways}
    low = pl.ds(pl.multiple_of(core * 128, 64), 64)
    high = pl.ds(pl.multiple_of(core * 128 + 64, 64), 64)

    def block(dz):
        return lax.rem(z + dz + 8, 8)

    def ship(dz, *names):
        u = block(dz)
        for way in names:
            sem, device = ways[way]
            ref = gh.at[u, mine, :]
            recv = (sib_r if way == "sib" else own_r).at[u]
            if dz == -3 and way == "up":
                ref, recv = gh.at[u, low, :], own_r.at[8]
            if dz == 3 and way == "down":
                ref, recv = gh.at[u, high, :], own_r.at[9]
            sent.append(send(ref, ref, sem.at[count[way]], recv, device))
            count[way] += 1

    def arrive(dz, *names):
        u = block(dz)
        if dz == 4:
            ref = gh.at[u, low, :]
            remote(ref, ref, up_s.at[0], own_r.at[8], sib).wait_recv()
            ref = gh.at[u, high, :]
            remote(ref, ref, up_s.at[0], own_r.at[9], sib).wait_recv()
        else:
            ref = gh.at[u, mine, :]
            remote(ref, ref, up_s.at[0], own_r.at[u], sib).wait_recv()
        ship(dz, *names)

    edge = gh.at[z]
    near = [
        send(edge.at[high, :], halo.at[0], halo_s.at[0], halo_r.at[0], at_p(1)),
        send(edge.at[low, :], halo.at[1], halo_s.at[1], halo_r.at[1], at_p(-1)),
    ]
    ship(0, "up", "down", "sib")

    for i, t in enumerate((1, 2, 3, 0)):
        turned[...] = parts_ref[t].astype(F32).T.astype(BF16)
        right = hid_ref if t else cot_ref
        xs[AW * i : AW * i + AW] = jnp.dot(turned[0:AW], right[...], preferred_element_type=F32).astype(BF16)

    def part(c, k):
        return pl.ds(pl.multiple_of(c * 640 + k * 160, 16), 160)

    pair = [send(xs.at[part(1 - core, k)], half.at[k], pair_s.at[k], pair_r.at[k], sib) for k in range(4)]
    arrive(-1, "up", "sib")
    arrive(1, "down", "sib")

    for copy in near:
        copy.wait()
    j = lax.broadcasted_iota(jnp.int32, (64, 640), 0)
    rows = (
        jnp.where(p > 0, halo[0].astype(F32), 0.0),
        gh[z, low, :].astype(F32),
        gh[z, high, :].astype(F32),
        jnp.where(p < 31, halo[1].astype(F32), 0.0),
    )
    for r in range(4):
        moved = shifted(rows[r], j)
        for b in range(3):
            sh[2 - b, 64 * r : 64 * r + 64] = moved[b].astype(BF16)

    def tap(t):
        a, b = t // 3, t % 3
        start = 64 * (2 - a)
        term = lax.dot_general(sh[b, start : start + 128], w[t], NT, preferred_element_type=F32)
        if t:
            acc[...] += term
        else:
            acc[...] = term

    def gain(dz, start=False):
        u = block(dz)
        ref = gh.at[u, pl.ds(pl.multiple_of((1 - core) * 128, 128), 128), :]
        remote(ref, ref, up_s.at[0], sib_r.at[u], sib).wait_recv()
        term = jnp.dot(lhs_ref[u], gh[u], preferred_element_type=F32)
        if start:
            prod[...] = term
        else:
            prod[...] += term

    tap(0)
    for copy in pair:
        copy.wait()
    for k in range(4):
        half[k] = (half[k].astype(F32) + xs[part(core, k)].astype(F32)).astype(BF16)
    far = lax.rem(y + 2, 4)
    y_up, y_down = at_y(1), at_y(-1)
    sent.append(send(half.at[far, 0:80], ya, y_s.at[0], y_r.at[0], y_up[1]))
    sent.append(send(half.at[far, 80:160], yb, y_s.at[1], y_r.at[1], y_down[1]))
    tap(1)
    arrive(-2, "up", "sib")
    arrive(2, "down", "sib")
    remote(half.at[far, 0:80], ya, y_s.at[0], y_r.at[0], sib).wait_recv()
    remote(half.at[far, 80:160], yb, y_s.at[1], y_r.at[1], sib).wait_recv()
    half[y_up[0], 0:80] = (half[y_up[0], 0:80].astype(F32) + ya[...].astype(F32)).astype(BF16)
    half[y_down[0], 80:160] = (half[y_down[0], 80:160].astype(F32) + yb[...].astype(F32)).astype(BF16)
    sent.append(send(half.at[y_up[0]], yc, y_s.at[2], y_r.at[2], y_up[1]))
    sent.append(send(half.at[y_down[0]], yd, y_s.at[3], y_r.at[3], y_down[1]))
    tap(2)
    gain(0, True)
    arrive(-3, "up", "sib")
    arrive(3, "down", "sib")
    gain(-1)
    remote(half.at[0], yc, y_s.at[2], y_r.at[2], sib).wait_recv()
    remote(half.at[0], yd, y_s.at[3], y_r.at[3], sib).wait_recv()
    for n in range(5):
        c = slice(128 * n, 128 * n + 128)
        whole = half[y, :, c].astype(F32) + yc[:, c].astype(F32) + yd[:, c].astype(F32)
        plane[160 * n : 160 * n + 160] = whole.astype(BF16)
    plane[800:1024] = jnp.zeros((224, 128), BF16)

    def quarter(k):
        return pl.ds(pl.multiple_of(k * 256, 256), 256)

    def slot(k):
        return pl.ds(pl.multiple_of(k * 32, 32), 32)

    crossing = []
    for s in range(1, 4):
        other, device = at_x(s)
        crossing.append(send(plane.at[quarter(other)], xin.at[s], x_s.at[s], x_r.at[s], device))
    gain(1)
    arrive(4, "sib")
    whole = plane[quarter(x)].astype(F32)
    for s in range(1, 4):
        crossing[s - 1].wait()
        whole = whole + xin[s].astype(F32)
    xsum[...] = whole.astype(BF16)
    along = []
    for s in range(1, 8):
        other, device = at_z(s)
        along.append(send(xsum.at[slot(other)], zin.at[s], z_s.at[s], z_r.at[s], device))
    gain(-2)
    whole = xsum[slot(z)].astype(F32)
    for s in range(1, 8):
        along[s - 1].wait()
        whole = whole + zin[s].astype(F32)
    zfull[slot(z)] = whole.astype(BF16)
    zback = []
    for s in range(1, 8):
        ref = zfull.at[slot(z)]
        zback.append(send(ref, ref, zb_s.at[s], zb_r.at[s], at_z(s)[1]))
    gain(2)
    for copy in zback:
        copy.wait()
    pfull[quarter(x)] = zfull[...]
    xback = []
    for s in range(1, 4):
        ref = pfull.at[quarter(x)]
        xback.append(send(ref, ref, xb_s.at[s], xb_r.at[s], at_x(s)[1]))
    gain(-3)
    gain(3)
    for copy in xback:
        copy.wait()
    for n in range(5):
        out_ref[part(core, y), 128 * n : 128 * n + 128] = pfull[160 * n : 160 * n + 160]

    def whole_part(k, send_sem, recv_sem, device):
        ref = out_ref.at[part(core, k)]
        return send(ref, ref, send_sem, recv_sem, device)

    def half_of(k, low_half):
        start = core * 640 + k * 160 + (0 if low_half else 80)
        return out_ref.at[pl.ds(pl.multiple_of(start, 16), 80)]

    def half_part(k, low_half, send_sem, recv_sem, device):
        ref = half_of(k, low_half)
        return send(ref, ref, send_sem, recv_sem, device)

    sent.append(whole_part(y, yb_s.at[0], yb_r.at[0], y_up[1]))
    sent.append(whole_part(y, yb_s.at[1], yb_r.at[1], y_down[1]))
    fin = [whole_part(y, fin_s.at[0], fin_r.at[0], sib)]
    gain(4)

    places = [(n, i, 192 * n + 16 * i) for n in range(5) for i in range(12)]
    small[180:192] = jnp.zeros((12, 640), F32)
    for c in range(2):
        for t in range(9):
            small[20 * t : 20 * t + 20] = prod[288 * c + 32 * t : 288 * c + 32 * t + 20]
        for n, i, f in places:
            piece = small[16 * i : 16 * i + 16, 128 * n : 128 * n + 128].astype(BF16)
            tb[c, f // 128, f % 128 : f % 128 + 16] = piece
        tb[c, 7, 64:128] = jnp.zeros((64, 128), BF16)
    there = []
    for s in range(1, 16):
        other, device = at_spot(s)
        there.append(send(tb.at[lax.rem(other, 2), other // 2], tin.at[s], t_s.at[s], t_r.at[s], device))
    tap(3)
    ref = out_ref.at[part(core, y_down[0])]
    remote(ref, ref, yb_s.at[0], yb_r.at[0], sib).wait_recv()
    ref = out_ref.at[part(core, y_up[0])]
    remote(ref, ref, yb_s.at[1], yb_r.at[1], sib).wait_recv()
    sent.append(half_part(y_down[0], True, yb_s.at[2], yb_r.at[2], y_up[1]))
    sent.append(half_part(y_up[0], False, yb_s.at[3], yb_r.at[3], y_down[1]))
    fin.append(whole_part(y_down[0], fin_s.at[1], fin_r.at[1], sib))
    fin.append(whole_part(y_up[0], fin_s.at[2], fin_r.at[2], sib))
    tap(4)
    tap(5)
    ref = half_of(far, True)
    remote(ref, ref, yb_s.at[2], yb_r.at[2], sib).wait_recv()
    ref = half_of(far, False)
    remote(ref, ref, yb_s.at[3], yb_r.at[3], sib).wait_recv()
    fin.append(whole_part(far, fin_s.at[3], fin_r.at[3], sib))
    tap(6)
    whole = tb[xlo, dp].astype(F32)
    for s in range(1, 16):
        there[s - 1].wait()
        whole = whole + tin[s].astype(F32)
    tfull[dp] = whole.astype(BF16)
    tback = []
    for s in range(1, 8):
        ref = tfull.at[dp]
        tback.append(send(ref, ref, u_s.at[s], u_r.at[s], at_dp(s)[1]))
    tap(7)
    tap(8)
    lat_ref[...] = acc[...].astype(BF16)
    for copy in tback:
        copy.wait()
    for n, i, f in places:
        small[16 * i : 16 * i + 16, 128 * n : 128 * n + 128] = tfull[f // 128, f % 128 : f % 128 + 16].astype(F32)
    for t in range(9):
        taps_ref[t] = small[20 * t : 20 * t + 20]
    for copy in fin:
        copy.wait()
    for copy in sent:
        copy.wait_send()


ATTEND = 52


def whole_kernel(*refs):
    hbm, (rows_ref, taps_ref, lat_ref), scratch = refs[:7], refs[7:10], refs[10:]
    shared, scratch = scratch[:11], scratch[11:]
    latent, cot, wq, wk, wv, wo, w, hidden, packed, lhs, parts = shared
    one, two, three = scratch[:15], scratch[15:15 + ATTEND], scratch[15 + ATTEND :]
    windows = first_kernel(hbm, latent, cot, wq, wk, wv, wo, w, hidden, packed, *one)
    attend_kernel(windows, lhs, packed, parts, *two)
    finish_kernel(parts, hidden, cot, wq, wk, wv, lhs, w, rows_ref, taps_ref, lat_ref, *three)


def whole(*args):
    dma = pltpu.SemaphoreType.DMA
    vmem = pl.BlockSpec(memory_space=pltpu.VMEM)

    def b16(*shape):
        return pltpu.VMEM(shape, BF16)

    def f32(*shape):
        return pltpu.VMEM(shape, F32)

    shared = [
        b16(128, 640), b16(128, 640), b16(320, 640), b16(320, 640), b16(320, 640), b16(320, 640),
        b16(9, 640, 640), b16(128, 640), b16(10, 128, 128), b16(8, 576, 256), b16(4, 128, 384),
    ]
    one = [
        dma((6,)), dma((9,)), b16(2, 64, 640), f32(656, 128), b16(16, 2, 32, 128), b16(18, 2, 32, 128),
        b16(3, 256, 640), f32(128, 640), f32(2, 128, 128),
        dma((2,)), dma((2,)), dma((16,)), dma((16,)), dma((16,)), dma((1,)),
    ]
    two = [
        b16(8, 640, 128), b16(8, 128, 640), b16(2, 512, 128), b16(512, 128), b16(512, 128), b16(512, 128), b16(512, 128),
        f32(64, 512), f32(64, 512),
        f32(8, 640, 512), f32(640, 512), b16(640, 512), b16(640, 512),
        f32(1, 512), f32(1, 512), f32(64, 512), f32(1, 512), f32(64, 512),
        f32(1, 512), f32(1, 512), f32(64, 512), f32(1, 512), f32(64, 512),
        f32(640, 128), b16(4, 640, 128), b16(4, 640, 128), b16(4, 640, 128), b16(4, 640, 128),
        f32(4, 72, 128), f32(4, 72, 128), f32(4, 8, 128), f32(128, 128), b16(3, 512, 128), b16(4, 3, 128, 128),
        dma((4,)), dma((4,)), dma((2, 4)), dma((2, 4)),
        dma((4,)), dma((4,)), dma((4,)), dma((4,)), dma((4,)), dma((4,)), dma((4,)), dma((4,)),
        dma((4,)), dma((4,)), dma((4,)), dma((4,)), dma((2, 4)), dma((2, 4)),
    ]
    three = [
        b16(8, 256, 640), b16(2, 64, 640), b16(3, 256, 640), f32(128, 640),
        f32(576, 640), f32(192, 640), b16(384, 128),
        b16(1280, 640), b16(4, 160, 640), b16(80, 640), b16(80, 640), b16(160, 640), b16(160, 640),
        b16(1024, 128), b16(4, 256, 128), b16(256, 128), b16(8, 32, 128), b16(256, 128), b16(1024, 128),
        b16(2, 8, 128, 128), b16(16, 128, 128), b16(8, 128, 128),
        dma((2,)), dma((2,)), dma((4,)), dma((4,)), dma((8,)), dma((10,)), dma((8,)),
        dma((4,)), dma((4,)), dma((4,)), dma((4,)), dma((4,)), dma((4,)), dma((8,)), dma((8,)),
        dma((8,)), dma((8,)), dma((4,)), dma((4,)), dma((4,)), dma((4,)), dma((4,)), dma((4,)),
        dma((16,)), dma((16,)), dma((8,)), dma((8,)),
    ]
    return pl.pallas_call(
        whole_kernel,
        out_shape=(
            jax.ShapeDtypeStruct((1280, 640), BF16),
            jax.ShapeDtypeStruct((9, 20, 640), F32),
            jax.ShapeDtypeStruct((128, 640), BF16),
        ),
        in_specs=[pl.BlockSpec(memory_space=pl.ANY)] * 7,
        out_specs=(vmem,) * 3,
        scratch_shapes=shared + one + two + three,
        compiler_params=pltpu.CompilerParams(
            collective_id=0, has_side_effects=True, vmem_limit_bytes=60 * 1024 * 1024
        ),
        name="whole",
    )(*args)


def hand_kernel(rows_ref, taps_ref, lat_ref, taps_out, lat_out, *rest):
    outs, (rows, wide, in_sem, out_sem) = rest[:4], rest[4:]
    direct = [
        pltpu.make_async_copy(taps_ref, taps_out, out_sem.at[4]),
        pltpu.make_async_copy(lat_ref, lat_out, out_sem.at[5]),
    ]
    loads = [
        pltpu.make_async_copy(rows_ref.at[AW * i : AW * i + AW], rows.at[i], in_sem.at[i]) for i in range(4)
    ]
    for copy in loads + direct:
        copy.start()
    stores = []
    for i in range(4):
        loads[i].wait()
        wide[i] = rows[i].astype(F32)
        copy = pltpu.make_async_copy(wide.at[i], outs[i], out_sem.at[i])
        copy.start()
        stores.append(copy)
    for copy in stores + direct:
        copy.wait()


def hand_out(rows, taps, grad_latent):
    anywhere = pl.BlockSpec(memory_space=pl.ANY)
    return pl.pallas_call(
        hand_kernel,
        out_shape=(
            jax.ShapeDtypeStruct(taps.shape, F32),
            jax.ShapeDtypeStruct(grad_latent.shape, BF16),
        )
        + (jax.ShapeDtypeStruct((AW, 640), F32),) * 4,
        in_specs=[anywhere] * 3,
        out_specs=(anywhere,) * 6,
        scratch_shapes=[
            pltpu.VMEM((4, AW, 640), BF16),
            pltpu.VMEM((4, AW, 640), F32),
            pltpu.SemaphoreType.DMA((4,)),
            pltpu.SemaphoreType.DMA((6,)),
        ],
        compiler_params=pltpu.CompilerParams(vmem_limit_bytes=60 * 1024 * 1024),
        name="hand_out",
    )(rows, taps, grad_latent)


def body(latent, cotangent, conv_weight, query_weight, key_weight, value_weight, out_weight):
    sums = whole(
        latent.reshape(128, 640), cotangent.reshape(128, 640), out_weight, key_weight.T, value_weight.T,
        query_weight.T, conv_weight.reshape(9, 640, 640),
    )
    taps, grad_latent, query, key, value, out = hand_out(*sums)
    return (grad_latent.reshape(latent.shape), taps.reshape(3, 3, 20, 640), query.T, key.T, value.T, out)


def solution(mesh):
    placed = (P("dp", "patch", None, None), P("dp", "patch", None, None), P(), P(), P(), P(), P())
    return jax.shard_map(
        body,
        mesh=mesh,
        in_specs=placed,
        out_specs=(P("dp", "patch", None, None), P(None, None, "patch", None), P(), P(), P(), P()),
        check_vma=False,
    )
```

```python
import functools
import jax
import jax.numpy as jnp
from jax import lax
from jax.experimental import pallas as pl
from jax.experimental.pallas import tpu as pltpu
from jax.sharding import PartitionSpec as P

NH = 5
HD = 64
AW = 320
MESH = pl.DeviceIdType.MESH
F32 = jnp.float32
BF16 = jnp.bfloat16


def place():
    p = lax.axis_index("patch")
    return lax.axis_index("dp"), p // 16, lax.rem(p, 16) // 2, lax.rem(p, 2)


def send(src, dst, send_sem, recv_sem, device):
    copy = pltpu.make_async_remote_copy(
        src_ref=src, dst_ref=dst, send_sem=send_sem, recv_sem=recv_sem,
        device_id=device, device_id_type=MESH,
    )
    copy.start()
    return copy


NT = (((1,), (1,)), ((), ()))
LOG2E = 1.4426950408889634


def remote(src, dst, send_sem, recv_sem, device):
    return pltpu.make_async_remote_copy(
        src_ref=src, dst_ref=dst, send_sem=send_sem, recv_sem=recv_sem,
        device_id=device, device_id_type=MESH,
    )


def attend_kernel(windows, lhs_ref, x_ref, out_ref, kv, kvt, qd, qs, gs, q4, g4, gt, gt4, scores, slope, pb, sb,
                  top, low, att, delta, dq, top4, low4, att4, delta4, dq4, part, box_up, box_down, ahead, behind,
                  mix, mix_in, stat, own4, stage, res,
                  kv_s, kv_r, qd_s, qd_r, up_s, up_r, down_s, down_r, rup_s, rup_r, rdown_s, rdown_r,
                  mix_s, mix_r, stat_s, stat_r, g_s, g_r):
    dp, xlo, z, core = place()
    j = xlo * 2 + core

    def at_z(step):
        return (dp, xlo * 16 + lax.rem(z + step + 8, 8) * 2 + core)

    def in_quad(step):
        m = lax.rem(j + step, 4)
        return m, (dp, (m // 2) * 16 + z * 2 + lax.rem(m, 2))

    def rows(m):
        return pl.ds(pl.multiple_of(m * 128, 128), 128)

    first, second = [], []
    for s in range(1, 4):
        m, device = in_quad(s)
        first.append(send(x_ref.at[2 * m], kv.at[z, rows(j), :], kv_s.at[s], kv_r.at[s], device))
    for s in range(1, 4):
        m, device = in_quad(s)
        second.append(send(x_ref.at[2 * m + 1], qd.at[0, rows(j), :], qd_s.at[0, s], qd_r.at[0, s], device))
        second.append(send(x_ref.at[8], qd.at[1, rows(j), :], qd_s.at[1, s], qd_r.at[1, s], device))
    kv[z, rows(j), :] = x_ref[2 * j]
    kv[z, 512:640] = x_ref[9]
    qd[0, rows(j), :] = x_ref[2 * j + 1]
    qd[1, rows(j), :] = x_ref[8]
    lane = lax.broadcasted_iota(jnp.int32, (128, 128), 1)
    left = lane < 64
    for ref in (top, top4):
        ref[...] = jnp.full(ref.shape, -jnp.inf, F32)
    for ref in (low, low4, att, att4, dq, dq4):
        ref[...] = jnp.zeros(ref.shape, F32)

    def ring_up(s):
        k = lax.rem(z + 8 - s, 8)
        ref = kv.at[k] if s < 3 else kv.at[k, 0:320]
        return remote(ref, ref, up_s.at[s], up_r.at[s], at_z(1))

    def ring_down(s):
        k = lax.rem(z + s, 8)
        ref = kv.at[k] if s < 3 else kv.at[k, 320:640]
        return remote(ref, ref, down_s.at[s], down_r.at[s], at_z(-1))

    for copy in first:
        copy.wait()
    ring_up(0).start()
    ring_down(0).start()
    windows(lhs_ref)
    for copy in second:
        copy.wait()
    for m in range(4):
        r = slice(m * 128, m * 128 + 128)
        for i, (a, b, bt) in enumerate(((qs, gs, gt), (q4, g4, gt4))):
            pair = qd[i, r].astype(F32)
            a[r] = jnp.where(left, pair, 0.0).astype(BF16)
            b[r] = jnp.where(left, 0.0, pair).astype(BF16)
            bt[:, r] = pair.T[64:128]

    def soften(b, keys, q, top, low, att):
        s = scores[b, keys, q]
        old = top[:, q]
        new = jnp.maximum(old, jnp.max(s, axis=0, keepdims=True))
        p = jnp.exp2(s - new)
        fade = jnp.exp2(old - new)
        low[:, q] = low[:, q] * fade + jnp.sum(p, axis=0, keepdims=True)
        top[:, q] = new
        att[:, q] = att[:, q] * fade
        pb[keys, q] = p.astype(BF16)

    main, side = slice(0, 512), slice(512, 640)
    quarters = [slice(128 * i, 128 * i + 128) for i in range(4)]

    def pass_one(t, carry):
        for s in range(3):
            @pl.when(t == 2 * s + 1)
            def _():
                ring_up(s).wait_recv()
                ring_up(s + 1).start()
                ring_down(s).wait_recv()
                ring_down(s + 1).start()

        @pl.when(t == 7)
        def _():
            ring_up(3).wait_recv()
            ring_down(3).wait_recv()

        offset = jnp.where(lax.rem(t, 2) == 1, 8 - (t + 1) // 2, t // 2)
        b = lax.rem(z + offset, 8)
        scores[b, main] = lax.dot_general(kv[b, main], qs[...], NT, preferred_element_type=F32) * LOG2E
        scores[b, side] = lax.dot_general(kv[b, side], q4[...], NT, preferred_element_type=F32) * LOG2E
        for i in range(5):
            c = slice(128 * i, 128 * i + 128)
            kvt[b, :, c] = kv[b, c].astype(F32).T.astype(BF16)
        for q in quarters:
            soften(b, main, q, top, low, att)
            soften(b, side, q, top4, low4, att4)
        att[...] += jnp.dot(kvt[b, 64:128, main], pb[main], preferred_element_type=F32)
        att4[...] += jnp.dot(kvt[b, 64:128, side], pb[side], preferred_element_type=F32)
        return carry

    lax.fori_loop(0, 8, pass_one, 0)
    for m in range(4):
        q = quarters[m]
        mix[m, 0:64] = att4[:, q]
        mix[m, 64:65] = top4[:, q]
        mix[m, 65:66] = low4[:, q]
        mix[m, 66:72] = jnp.zeros((6, 128), F32)
    mixing = []
    for s in range(1, 4):
        m, device = in_quad(s)
        mixing.append(send(mix.at[m], mix_in.at[s], mix_s.at[s], mix_r.at[s], device))
    mix_in[0] = mix[j]
    att[...] = att[...] / low[...]
    top[...] = top[...] + jnp.log2(low[...])
    delta[...] = jnp.sum(att[...] * gt[...], axis=0, keepdims=True)

    def stat_copy(s):
        return remote(stat.at[j], stat.at[j], stat_s.at[s], stat_r.at[s], in_quad(s)[1])

    for copy in mixing:
        copy.wait()
    tops = [mix_in[s, 64:65] for s in range(4)]
    best = jnp.maximum(jnp.maximum(tops[0], tops[1]), jnp.maximum(tops[2], tops[3]))
    total, blend = jnp.zeros((1, 128), F32), jnp.zeros((64, 128), F32)
    for s in range(4):
        weight = jnp.exp2(tops[s] - best)
        total = total + mix_in[s, 65:66] * weight
        blend = blend + mix_in[s, 0:64] * weight
    blend = blend / total
    own4[0:64] = blend
    own4[64:128] = jnp.zeros((64, 128), F32)
    stat[j, 0:1] = best + jnp.log2(total)
    stat[j, 1:2] = jnp.sum(blend * gt4[:, rows(j)], axis=0, keepdims=True)
    stat[j, 2:8] = jnp.zeros((6, 128), F32)
    for s in range(1, 4):
        stat_copy(s).start()

    def sum_up(s):
        r = slice(0, 320) if s == 0 else slice(0, 640)
        return remote(box_up.at[s, r], ahead.at[s, r], rup_s.at[s], rup_r.at[s], at_z(1))

    def sum_down(s):
        r = slice(320, 640) if s == 0 else slice(0, 640)
        return remote(box_down.at[s, r], behind.at[s, r], rdown_s.at[s], rdown_r.at[s], at_z(-1))

    def slopes(b, keys, q, top, delta):
        p = jnp.exp2(scores[b, keys, q] - top[:, q])
        pb[keys, q] = p.astype(BF16)
        sb[keys, q] = (p * (slope[keys, q] - delta[:, q])).astype(BF16)

    def pass_two(t, carry):
        offset = jnp.where(lax.rem(t, 2) == 0, 4 + t // 2, 4 - (t + 1) // 2)
        b = lax.rem(z + offset, 8)
        slope[main] = lax.dot_general(kv[b, main], gs[...], NT, preferred_element_type=F32)
        slope[side] = lax.dot_general(kv[b, side], g4[...], NT, preferred_element_type=F32)
        for q in quarters:
            slopes(b, main, q, top, delta)
        dq[...] += jnp.dot(kvt[b, 0:64, main], sb[main], preferred_element_type=F32)
        part[main] = jnp.dot(sb[main], qs[...], preferred_element_type=F32) + jnp.dot(
            pb[main], gs[...], preferred_element_type=F32
        )

        @pl.when(t == 0)
        def _():
            for s in range(1, 4):
                stat_copy(s).wait()
            for m in range(4):
                top4[:, quarters[m]] = stat[m, 0:1]
                delta4[:, quarters[m]] = stat[m, 1:2]

        for q in quarters:
            slopes(b, side, q, top4, delta4)
        dq4[...] += jnp.dot(kvt[b, 0:64, side], sb[side], preferred_element_type=F32)
        part[side] = jnp.dot(sb[side], q4[...], preferred_element_type=F32) + jnp.dot(
            pb[side], g4[...], preferred_element_type=F32
        )

        @pl.when(t == 0)
        def _():
            box_up[0, 0:320] = part[0:320].astype(BF16)
            sum_up(0).start()
            box_down[0, 320:640] = part[320:640].astype(BF16)
            sum_down(0).start()

        @pl.when(t == 1)
        def _():
            sum_up(0).wait_recv()
            box_up[1, 0:320] = (part[0:320] + ahead[0, 0:320].astype(F32)).astype(BF16)
            box_up[1, 320:640] = part[320:640].astype(BF16)
            sum_up(1).start()

        @pl.when(t == 2)
        def _():
            sum_down(0).wait_recv()
            box_down[1, 0:320] = part[0:320].astype(BF16)
            box_down[1, 320:640] = (part[320:640] + behind[0, 320:640].astype(F32)).astype(BF16)
            sum_down(1).start()

        for s in range(1, 3):
            @pl.when(t == 2 * s + 1)
            def _():
                sum_up(s).wait_recv()
                box_up[s + 1] = (part[...] + ahead[s].astype(F32)).astype(BF16)
                sum_up(s + 1).start()

            @pl.when(t == 2 * s + 2)
            def _():
                sum_down(s).wait_recv()
                box_down[s + 1] = (part[...] + behind[s].astype(F32)).astype(BF16)
                sum_down(s + 1).start()

        return carry

    lax.fori_loop(0, 8, pass_two, 0)
    for q in quarters:
        both = jnp.concatenate([dq[:, q] * HD ** -0.5, att[:, q]], axis=0)
        stage[0, q] = both.T.astype(BF16)
        both = jnp.concatenate([dq4[:, q] * HD ** -0.5, jnp.zeros((64, 128), F32)], axis=0)
        stage[1, q] = both.T.astype(BF16)
    late = []
    for s in range(1, 4):
        m, device = in_quad(s)
        late.append(send(stage.at[0:2, rows(m), :], res.at[j, 0:2], g_s.at[0, s], g_r.at[0, s], device))
    sum_up(3).wait_recv()
    sum_down(3).wait_recv()
    stage[2] = (part[main] + ahead[3, main].astype(F32) + behind[3, main].astype(F32)).astype(BF16)
    for s in range(1, 4):
        m, device = in_quad(s)
        late.append(send(stage.at[2, rows(m), :], res.at[j, 2], g_s.at[1, s], g_r.at[1, s], device))
    own = part[side] + ahead[3, side].astype(F32) + behind[3, side].astype(F32)
    for t in range(3):
        res[j, t] = stage[t, rows(j), :]
    for s in range(4):
        ring_up(s).wait_send()
        ring_down(s).wait_send()
        sum_up(s).wait_send()
        sum_down(s).wait_send()
    for copy in late:
        copy.wait()

    def swap(a):
        return pltpu.roll(a, 64, axis=1)

    for t, source, high in ((0, 0, True), (1, 0, False), (2, 2, False), (3, 2, True)):
        for i in range(2):
            a, b = res[2 * i, source].astype(F32), res[2 * i + 1, source].astype(F32)
            pair = jnp.where(left, swap(a), b) if high else jnp.where(left, a, swap(b))
            out_ref[t, :, 128 * i : 128 * i + 128] = pair.astype(BF16)
    last4 = (
        own4[...].T,
        sum(res[m, 1].astype(F32) for m in range(4)),
        own,
        swap(own),
    )
    for t in range(4):
        out_ref[t, :, 256:384] = jnp.where(left, last4[t], 0.0).astype(BF16)


def shifted(rows, j):
    before = jnp.where(j == 0, 0.0, pltpu.roll(rows, 1, axis=0))
    after = jnp.where(j == 63, 0.0, pltpu.roll(rows, 63, axis=0))
    return before, rows, after


def first_kernel(hbm, lat_ref, cot_ref, wq_ref, wk_ref, wv_ref, wo_ref, w, hid_ref, x_ref, load_sem, w_sem,
                 halo, turned, sbuf, share, sh, acc, tmp, halo_s, halo_r, share_s, share_r, rim_s, rim_r):
    dp, xlo, z, core = place()
    p = lax.axis_index("patch")
    spot = dp * 2 + xlo
    index = lax.rem(p, 16)

    def at(step):
        other = lax.rem(p + step + 32, 32)
        return (dp, other)

    local = (lat_ref, cot_ref, wo_ref, wk_ref, wv_ref, wq_ref)
    inputs = []
    for i, ref in enumerate(local):
        copy = pltpu.make_async_copy(hbm[i], ref, load_sem.at[i])
        copy.start()
        inputs.append(copy)
    loads = []
    for t in range(9):
        copy = pltpu.make_async_copy(hbm[6].at[t], w.at[t], w_sem.at[t])
        copy.start()
        loads.append(copy)
    barrier = pltpu.get_barrier_semaphore()

    def hello(s, carry):
        pl.semaphore_signal(barrier, inc=1, device_id=at(s), device_id_type=MESH)
        return carry

    def hello_plane(s, carry):
        other = lax.rem(spot + s, 16)
        device = (other // 2, lax.rem(other, 2) * 16 + index)
        pl.semaphore_signal(barrier, inc=1, device_id=device, device_id_type=MESH)
        return carry

    lax.fori_loop(1, 32, hello, 0)
    lax.fori_loop(1, 16, hello_plane, 0)
    inputs[0].wait()
    turned[0:640] = lat_ref[...].astype(F32).T
    turned[640:656] = jnp.zeros((16, 128), F32)
    for k in range(32):
        sbuf[k % 16, k // 16] = turned[20 * k : 20 * k + 32].astype(BF16)
    share[jnp.where(xlo == 0, 0, 17)] = jnp.zeros((2, 32, 128), BF16)
    share[index + 1] = sbuf[index]
    pl.semaphore_wait(barrier, 46)
    near = [
        send(lat_ref.at[64:128], halo.at[0], halo_s.at[0], halo_r.at[0], at(1)),
        send(lat_ref.at[0:64], halo.at[1], halo_s.at[1], halo_r.at[1], at(-1)),
    ]

    def share_copy(s):
        other = lax.rem(index + s, 16)
        return remote(sbuf.at[other], share.at[index + 1], share_s.at[s], share_r.at[s], (dp, xlo * 16 + other))

    rim = index == jnp.where(xlo == 0, 15, 0)
    rim_slot = jnp.where(xlo == 0, 0, 17)

    def rim_copy(s):
        return remote(sbuf.at[s], share.at[rim_slot], rim_s.at[s], rim_r.at[0], (dp, (1 - xlo) * 16 + s))

    def share_start(s, carry):
        share_copy(s).start()
        return carry

    def rim_start(s, carry):
        rim_copy(s).start()
        return carry

    lax.fori_loop(1, 16, share_start, 0)

    @pl.when(rim)
    def _():
        lax.fori_loop(0, 16, rim_start, 0)

    lane = lax.broadcasted_iota(jnp.int32, (128, 128), 1)
    left = lane < 64

    def pack(low_value, high_value, first_slot, last_slot):
        for n in range(3):
            c = slice(128 * n, min(128 * n + 128, AW))
            width = c.stop - c.start
            tmp[0, :, 0:width] = low_value[:, c]
            tmp[1, :, 0:width] = high_value[:, c]
            a, b = tmp[0], tmp[1]
            even = jnp.where(left, a, pltpu.roll(b, 64, axis=1)).astype(BF16)
            if n == 2:
                x_ref[last_slot] = even
            else:
                x_ref[4 * n + first_slot] = even
                x_ref[4 * n + 2 + first_slot] = jnp.where(left, pltpu.roll(a, 64, axis=1), b).astype(BF16)

    inputs[1].wait()
    inputs[2].wait()
    out_grad = lax.dot_general(cot_ref[...], wo_ref[...], NT, preferred_element_type=F32)
    tmp[...] = jnp.zeros(tmp.shape, F32)
    for copy in near:
        copy.wait()
    j = lax.broadcasted_iota(jnp.int32, (64, 640), 0)
    rows = (
        jnp.where(p > 0, halo[0].astype(F32), 0.0),
        lat_ref[0:64].astype(F32),
        lat_ref[64:128].astype(F32),
        jnp.where(p < 31, halo[1].astype(F32), 0.0),
    )
    for r in range(4):
        moved = shifted(rows[r], j)
        for b in range(3):
            sh[b, 64 * r : 64 * r + 64] = moved[b].astype(BF16)
    for t in range(9):
        a, b = t // 3, t % 3
        loads[t].wait()
        term = jnp.dot(sh[b, 64 * a : 64 * a + 128], w[t], preferred_element_type=F32)
        if t:
            acc[...] += term
        else:
            acc[...] = term
    hid_ref[...] = acc[...].astype(BF16)
    for copy in inputs[3:]:
        copy.wait()

    def project(ref):
        value = lax.dot_general(hid_ref[...], ref[...], NT, preferred_element_type=F32)
        return value.astype(BF16).astype(F32)

    pack(project(wk_ref), project(wv_ref), 0, 9)
    pack(project(wq_ref) * HD ** -0.5, out_grad, 1, 8)

    def windows(lhs_ref):
        def share_end(s, carry):
            share_copy(s).wait()
            return carry

        def rim_end(s, carry):
            rim_copy(s).wait_send()
            return carry

        lax.fori_loop(1, 16, share_end, 0)
        rim_copy(0).wait_recv()

        @pl.when(rim)
        def _():
            lax.fori_loop(0, 16, rim_end, 0)

        col = lax.broadcasted_iota(jnp.int32, (32, 128), 1)
        near_side = col < 64
        col = lax.rem(col, 64)

        def one(q, carry):
            lanes = pl.ds(pl.multiple_of(lax.rem(q, 2) * 128, 128), 128)
            for c in range(2):
                here = share[q + 1, c].astype(F32)
                turn = pltpu.roll(here, 64, axis=1)
                above = jnp.where(near_side, pltpu.roll(share[q, c].astype(F32), 64, axis=1), turn)
                below = jnp.where(near_side, turn, pltpu.roll(share[q + 2, c].astype(F32), 64, axis=1))
                for a, value in enumerate((above, here, below)):
                    three = (
                        jnp.where(col == 0, 0.0, pltpu.roll(value, 1, axis=1)),
                        value,
                        jnp.where(col == 63, 0.0, pltpu.roll(value, 127, axis=1)),
                    )
                    for b in range(3):
                        row = 288 * c + 32 * (3 * a + b)
                        lhs_ref[q // 2, row : row + 32, lanes] = three[b].astype(BF16)
            return carry

        lax.fori_loop(0, 16, one, 0)

    return windows


def finish_kernel(parts_ref, hid_ref, cot_ref, wq_ref, wk_ref, wv_ref, lhs_ref, w, out_ref, taps_ref, lat_ref,
                  gh, halo, sh, acc, prod, small, turned, xs, half, ra, rb, rc, rd,
                  plane, xin, xsum, zin, zfull, pfull, tb, tin, tfull, halo_s, halo_r, up_s, down_s, sib_s, own_r, sib_r,
                  pair_s, pair_r, y_s, y_r, x_s, x_r, z_s, z_r, zb_s, zb_r, xb_s, xb_r, yb_s, yb_r, fin_s, fin_r,
                  t_s, t_r, u_s, u_r):
    dp, xlo, z, core = place()
    p = lax.axis_index("patch")
    xhi, y = dp // 4, lax.rem(dp, 4)
    x = xhi * 2 + xlo
    sib = (dp, xlo * 16 + z * 2 + 1 - core)

    def at_z(s):
        other = lax.rem(z + s + 8, 8)
        return other, (dp, xlo * 16 + other * 2 + core)

    def at_y(s):
        other = lax.rem(y + s + 4, 4)
        return other, (xhi * 4 + other, p)

    def at_x(s):
        other = lax.rem(x + s + 4, 4)
        return other, (other // 2 * 4 + y, lax.rem(other, 2) * 16 + z * 2 + core)

    spot = dp * 2 + xlo

    def at_spot(s):
        other = lax.rem(spot + s, 16)
        return other, (other // 2, lax.rem(other, 2) * 16 + z * 2 + core)

    def at_dp(s):
        other = lax.rem(dp + s, 8)
        return other, (other, p)

    def at_p(s):
        return (dp, lax.rem(p + s + 32, 32))

    mine = pl.ds(pl.multiple_of(core * 128, 128), 128)
    sent = []

    value = cot_ref[...].astype(F32)
    for t, ref in ((1, wq_ref), (2, wk_ref), (3, wv_ref)):
        value = value + jnp.dot(parts_ref[t, :, 0:AW], ref[...], preferred_element_type=F32)
    gh[z, mine, :] = value.astype(BF16)

    ways = {"up": (up_s, at_z(1)[1]), "down": (down_s, at_z(-1)[1]), "sib": (sib_s, sib)}
    count = {way: 0 for way in ways}
    low = pl.ds(pl.multiple_of(core * 128, 64), 64)
    high = pl.ds(pl.multiple_of(core * 128 + 64, 64), 64)

    def block(dz):
        return lax.rem(z + dz + 8, 8)

    def ship(dz, *names):
        u = block(dz)
        for way in names:
            sem, device = ways[way]
            ref = gh.at[u, mine, :]
            recv = (sib_r if way == "sib" else own_r).at[u]
            if dz == -3 and way == "up":
                ref, recv = gh.at[u, low, :], own_r.at[8]
            if dz == 3 and way == "down":
                ref, recv = gh.at[u, high, :], own_r.at[9]
            sent.append(send(ref, ref, sem.at[count[way]], recv, device))
            count[way] += 1

    def arrive(dz, *names):
        u = block(dz)
        if dz == 4:
            ref = gh.at[u, low, :]
            remote(ref, ref, up_s.at[0], own_r.at[8], sib).wait_recv()
            ref = gh.at[u, high, :]
            remote(ref, ref, up_s.at[0], own_r.at[9], sib).wait_recv()
        else:
            ref = gh.at[u, mine, :]
            remote(ref, ref, up_s.at[0], own_r.at[u], sib).wait_recv()
        ship(dz, *names)

    edge = gh.at[z]
    near = [
        send(edge.at[high, :], halo.at[0], halo_s.at[0], halo_r.at[0], at_p(1)),
        send(edge.at[low, :], halo.at[1], halo_s.at[1], halo_r.at[1], at_p(-1)),
    ]
    ship(0, "up", "down", "sib")

    for i, t in enumerate((1, 2, 3, 0)):
        turned[...] = parts_ref[t].astype(F32).T.astype(BF16)
        right = hid_ref if t else cot_ref
        xs[AW * i : AW * i + AW] = jnp.dot(turned[0:AW], right[...], preferred_element_type=F32).astype(BF16)

    first_at, second_at = (at_y, at_x), (at_x, at_y)
    first_index, second_index = (y, x), (x, y)
    halves = range(2)

    def part(c, h, k):
        return pl.ds(pl.multiple_of(c * 640 + h * 320 + k * 80, 16), 80)

    def low_of(c, h, k):
        return pl.ds(pl.multiple_of(c * 640 + h * 320 + k * 80, 16), 48)

    def high_of(c, h, k):
        return pl.ds(pl.multiple_of(c * 640 + h * 320 + k * 80 + 48, 16), 32)

    pair = []
    for h in halves:
        theirs = pl.ds(pl.multiple_of((1 - core) * 640 + h * 320, 16), 320)
        there = pl.ds(320 * h, 320)
        pair.append(send(xs.at[theirs], half.at[there], pair_s.at[h], pair_r.at[h], sib))
    arrive(-1, "up", "sib")
    arrive(1, "down", "sib")

    for copy in near:
        copy.wait()
    j = lax.broadcasted_iota(jnp.int32, (64, 640), 0)
    rows = (
        jnp.where(p > 0, halo[0].astype(F32), 0.0),
        gh[z, low, :].astype(F32),
        gh[z, high, :].astype(F32),
        jnp.where(p < 31, halo[1].astype(F32), 0.0),
    )
    for r in range(4):
        moved = shifted(rows[r], j)
        for b in range(3):
            sh[2 - b, 64 * r : 64 * r + 64] = moved[b].astype(BF16)

    def tap(t):
        a, b = t // 3, t % 3
        start = 64 * (2 - a)
        term = lax.dot_general(sh[b, start : start + 128], w[t], NT, preferred_element_type=F32)
        if t:
            acc[...] += term
        else:
            acc[...] = term

    def gain(dz, start=False):
        u = block(dz)
        ref = gh.at[u, pl.ds(pl.multiple_of((1 - core) * 128, 128), 128), :]
        remote(ref, ref, up_s.at[0], sib_r.at[u], sib).wait_recv()
        term = jnp.dot(lhs_ref[u], gh[u], preferred_element_type=F32)
        if start:
            prod[...] = term
        else:
            prod[...] += term

    tap(0)
    for copy in pair:
        copy.wait()
    for h in halves:
        mine_rows = pl.ds(pl.multiple_of(core * 640 + h * 320, 16), 320)
        r = slice(320 * h, 320 * h + 320)
        half[r] = (half[r].astype(F32) + xs[mine_rows].astype(F32)).astype(BF16)
    up, down, far = [], [], []
    for h in halves:
        up.append(first_at[h](1))
        down.append(first_at[h](-1))
        far.append(lax.rem(first_index[h] + 2, 4))
        sent.append(send(half.at[low_of(0, h, far[h])], ra.at[h], y_s.at[h, 0], y_r.at[h, 0], up[h][1]))
        sent.append(send(half.at[high_of(0, h, far[h])], rb.at[h], y_s.at[h, 1], y_r.at[h, 1], down[h][1]))
    tap(1)
    arrive(-2, "up", "sib")
    arrive(2, "down", "sib")
    for h in halves:
        remote(half.at[low_of(0, h, 0)], ra.at[h], y_s.at[h, 0], y_r.at[h, 0], sib).wait_recv()
        remote(half.at[high_of(0, h, 0)], rb.at[h], y_s.at[h, 1], y_r.at[h, 1], sib).wait_recv()
        r = low_of(0, h, up[h][0])
        half[r] = (half[r].astype(F32) + ra[h].astype(F32)).astype(BF16)
        r = high_of(0, h, down[h][0])
        half[r] = (half[r].astype(F32) + rb[h].astype(F32)).astype(BF16)
        sent.append(send(half.at[part(0, h, up[h][0])], rc.at[h], y_s.at[h, 2], y_r.at[h, 2], up[h][1]))
        sent.append(send(half.at[part(0, h, down[h][0])], rd.at[h], y_s.at[h, 3], y_r.at[h, 3], down[h][1]))
    tap(2)
    gain(0, True)
    arrive(-3, "up", "sib")
    arrive(3, "down", "sib")
    gain(-1)
    def quarter(k):
        return pl.ds(pl.multiple_of(k * 128, 128), 128)

    def slot(k):
        return pl.ds(pl.multiple_of(k * 16, 16), 16)

    crossing = []
    for h in halves:
        remote(half.at[part(0, h, 0)], rc.at[h], y_s.at[h, 2], y_r.at[h, 2], sib).wait_recv()
        remote(half.at[part(0, h, 0)], rd.at[h], y_s.at[h, 3], y_r.at[h, 3], sib).wait_recv()
        whole = half[part(0, h, first_index[h])].astype(F32) + rc[h].astype(F32) + rd[h].astype(F32)
        for n in range(5):
            plane[h, 80 * n : 80 * n + 80] = whole[:, 128 * n : 128 * n + 128].astype(BF16)
        plane[h, 400:512] = jnp.zeros((112, 128), BF16)
        for s in range(1, 4):
            other, device = second_at[h](s)
            crossing.append(send(plane.at[h, quarter(other)], xin.at[h, s], x_s.at[h, s], x_r.at[h, s], device))
    gain(1)
    arrive(4, "sib")
    for copy in crossing:
        copy.wait()
    for h in halves:
        whole = plane[h, quarter(second_index[h])].astype(F32)
        for s in range(1, 4):
            whole = whole + xin[h, s].astype(F32)
        xsum[h] = whole.astype(BF16)
    along = []
    for s in range(1, 8):
        other, device = at_z(s)
        along.append(send(xsum.at[:, slot(other), :], zin.at[s], z_s.at[s], z_r.at[s], device))
    gain(-2)
    whole = xsum[:, slot(z), :].astype(F32)
    for s in range(1, 8):
        along[s - 1].wait()
        whole = whole + zin[s].astype(F32)
    zfull[:, slot(z), :] = whole.astype(BF16)
    zback = []
    for s in range(1, 8):
        ref = zfull.at[:, slot(z), :]
        zback.append(send(ref, ref, zb_s.at[s], zb_r.at[s], at_z(s)[1]))
    gain(2)
    for copy in zback:
        copy.wait()
    xback = []
    for h in halves:
        pfull[h, quarter(second_index[h])] = zfull[h]
        for s in range(1, 4):
            ref = pfull.at[h, quarter(second_index[h])]
            xback.append(send(ref, ref, xb_s.at[h, s], xb_r.at[h, s], second_at[h](s)[1]))
    gain(-3)
    gain(3)
    for copy in xback:
        copy.wait()
    fin = []
    for h in halves:
        for n in range(5):
            out_ref[part(core, h, first_index[h]), 128 * n : 128 * n + 128] = pfull[h, 80 * n : 80 * n + 80]

    def forward(rows, send_sem, recv_sem, device):
        return send(out_ref.at[rows], out_ref.at[rows], send_sem, recv_sem, device)

    def landed(rows, h, i):
        remote(out_ref.at[rows], out_ref.at[rows], yb_s.at[h, i], yb_r.at[h, i], sib).wait_recv()

    for h in halves:
        rows = part(core, h, first_index[h])
        sent.append(forward(rows, yb_s.at[h, 0], yb_r.at[h, 0], up[h][1]))
        sent.append(forward(rows, yb_s.at[h, 1], yb_r.at[h, 1], down[h][1]))
        fin.append(forward(rows, fin_s.at[h, 0], fin_r.at[h, 0], sib))
    gain(4)

    places = [(n, i, 192 * n + 16 * i) for n in range(5) for i in range(12)]
    small[180:192] = jnp.zeros((12, 640), F32)
    for c in range(2):
        for t in range(9):
            small[20 * t : 20 * t + 20] = prod[288 * c + 32 * t : 288 * c + 32 * t + 20]
        for n, i, f in places:
            piece = small[16 * i : 16 * i + 16, 128 * n : 128 * n + 128].astype(BF16)
            tb[c, f // 128, f % 128 : f % 128 + 16] = piece
        tb[c, 7, 64:128] = jnp.zeros((64, 128), BF16)
    there = []
    for s in range(1, 16):
        other, device = at_spot(s)
        there.append(send(tb.at[lax.rem(other, 2), other // 2], tin.at[s], t_s.at[s], t_r.at[s], device))
    tap(3)
    for h in halves:
        landed(part(core, h, down[h][0]), h, 0)
        landed(part(core, h, up[h][0]), h, 1)
        sent.append(forward(low_of(core, h, down[h][0]), yb_s.at[h, 2], yb_r.at[h, 2], up[h][1]))
        sent.append(forward(high_of(core, h, up[h][0]), yb_s.at[h, 3], yb_r.at[h, 3], down[h][1]))
        fin.append(forward(part(core, h, down[h][0]), fin_s.at[h, 1], fin_r.at[h, 1], sib))
        fin.append(forward(part(core, h, up[h][0]), fin_s.at[h, 2], fin_r.at[h, 2], sib))
    tap(4)
    tap(5)
    for h in halves:
        landed(low_of(core, h, far[h]), h, 2)
        landed(high_of(core, h, far[h]), h, 3)
        fin.append(forward(part(core, h, far[h]), fin_s.at[h, 3], fin_r.at[h, 3], sib))
    tap(6)
    whole = tb[xlo, dp].astype(F32)
    for s in range(1, 16):
        there[s - 1].wait()
        whole = whole + tin[s].astype(F32)
    tfull[dp] = whole.astype(BF16)
    tback = []
    for s in range(1, 8):
        ref = tfull.at[dp]
        tback.append(send(ref, ref, u_s.at[s], u_r.at[s], at_dp(s)[1]))
    tap(7)
    tap(8)
    lat_ref[...] = acc[...].astype(BF16)
    for copy in tback:
        copy.wait()
    for n, i, f in places:
        small[16 * i : 16 * i + 16, 128 * n : 128 * n + 128] = tfull[f // 128, f % 128 : f % 128 + 16].astype(F32)
    for t in range(9):
        taps_ref[t] = small[20 * t : 20 * t + 20]
    for copy in fin:
        copy.wait()
    for copy in sent:
        copy.wait_send()


ATTEND = 52


def whole_kernel(*refs):
    hbm, (rows_ref, taps_ref, lat_ref), scratch = refs[:7], refs[7:10], refs[10:]
    shared, scratch = scratch[:11], scratch[11:]
    latent, cot, wq, wk, wv, wo, w, hidden, packed, lhs, parts = shared
    one, two, three = scratch[:15], scratch[15:15 + ATTEND], scratch[15 + ATTEND :]
    windows = first_kernel(hbm, latent, cot, wq, wk, wv, wo, w, hidden, packed, *one)
    attend_kernel(windows, lhs, packed, parts, *two)
    finish_kernel(parts, hidden, cot, wq, wk, wv, lhs, w, rows_ref, taps_ref, lat_ref, *three)


def whole(*args):
    dma = pltpu.SemaphoreType.DMA
    vmem = pl.BlockSpec(memory_space=pltpu.VMEM)

    def b16(*shape):
        return pltpu.VMEM(shape, BF16)

    def f32(*shape):
        return pltpu.VMEM(shape, F32)

    shared = [
        b16(128, 640), b16(128, 640), b16(320, 640), b16(320, 640), b16(320, 640), b16(320, 640),
        b16(9, 640, 640), b16(128, 640), b16(10, 128, 128), b16(8, 576, 256), b16(4, 128, 384),
    ]
    one = [
        dma((6,)), dma((9,)), b16(2, 64, 640), f32(656, 128), b16(16, 2, 32, 128), b16(18, 2, 32, 128),
        b16(3, 256, 640), f32(128, 640), f32(2, 128, 128),
        dma((2,)), dma((2,)), dma((16,)), dma((16,)), dma((16,)), dma((1,)),
    ]
    two = [
        b16(8, 640, 128), b16(8, 128, 640), b16(2, 512, 128), b16(512, 128), b16(512, 128), b16(512, 128), b16(512, 128),
        f32(64, 512), f32(64, 512),
        f32(8, 640, 512), f32(640, 512), b16(640, 512), b16(640, 512),
        f32(1, 512), f32(1, 512), f32(64, 512), f32(1, 512), f32(64, 512),
        f32(1, 512), f32(1, 512), f32(64, 512), f32(1, 512), f32(64, 512),
        f32(640, 128), b16(4, 640, 128), b16(4, 640, 128), b16(4, 640, 128), b16(4, 640, 128),
        f32(4, 72, 128), f32(4, 72, 128), f32(4, 8, 128), f32(128, 128), b16(3, 512, 128), b16(4, 3, 128, 128),
        dma((4,)), dma((4,)), dma((2, 4)), dma((2, 4)),
        dma((4,)), dma((4,)), dma((4,)), dma((4,)), dma((4,)), dma((4,)), dma((4,)), dma((4,)),
        dma((4,)), dma((4,)), dma((4,)), dma((4,)), dma((2, 4)), dma((2, 4)),
    ]
    three = [
        b16(8, 256, 640), b16(2, 64, 640), b16(3, 256, 640), f32(128, 640),
        f32(576, 640), f32(192, 640), b16(384, 128),
        b16(1280, 640), b16(640, 640), b16(2, 48, 640), b16(2, 32, 640), b16(2, 80, 640), b16(2, 80, 640),
        b16(2, 512, 128), b16(2, 4, 128, 128), b16(2, 128, 128), b16(8, 2, 16, 128), b16(2, 128, 128), b16(2, 512, 128),
        b16(2, 8, 128, 128), b16(16, 128, 128), b16(8, 128, 128),
        dma((2,)), dma((2,)), dma((4,)), dma((4,)), dma((8,)), dma((10,)), dma((8,)),
        dma((2,)), dma((2,)), dma((2, 4)), dma((2, 4)), dma((2, 4)), dma((2, 4)), dma((8,)), dma((8,)),
        dma((8,)), dma((8,)), dma((2, 4)), dma((2, 4)), dma((2, 4)), dma((2, 4)), dma((2, 4)), dma((2, 4)),
        dma((16,)), dma((16,)), dma((8,)), dma((8,)),
    ]
    return pl.pallas_call(
        whole_kernel,
        out_shape=(
            jax.ShapeDtypeStruct((1280, 640), BF16),
            jax.ShapeDtypeStruct((9, 20, 640), F32),
            jax.ShapeDtypeStruct((128, 640), BF16),
        ),
        in_specs=[pl.BlockSpec(memory_space=pl.ANY)] * 7,
        out_specs=(vmem,) * 3,
        scratch_shapes=shared + one + two + three,
        compiler_params=pltpu.CompilerParams(
            collective_id=0, has_side_effects=True, vmem_limit_bytes=60 * 1024 * 1024
        ),
        name="whole",
    )(*args)


def hand_kernel(rows_ref, taps_ref, lat_ref, taps_out, lat_out, *rest):
    outs, (rows, wide, taps, lat, in_sem, out_sem) = rest[:4], rest[4:]
    loads = [
        pltpu.make_async_copy(rows_ref.at[AW * i : AW * i + AW], rows.at[i], in_sem.at[i]) for i in range(4)
    ]
    loads.append(pltpu.make_async_copy(taps_ref, taps, in_sem.at[4]))
    loads.append(pltpu.make_async_copy(lat_ref, lat, in_sem.at[5]))
    for copy in loads:
        copy.start()
    stores = []
    for i in range(6):
        loads[i].wait()
        if i < 4:
            wide[i] = rows[i].astype(F32)
            copy = pltpu.make_async_copy(wide.at[i], outs[i], out_sem.at[i])
        elif i == 4:
            copy = pltpu.make_async_copy(taps, taps_out, out_sem.at[i])
        else:
            copy = pltpu.make_async_copy(lat, lat_out, out_sem.at[i])
        copy.start()
        stores.append(copy)
    for copy in stores:
        copy.wait()


def hand_out(rows, taps, grad_latent):
    anywhere = pl.BlockSpec(memory_space=pl.ANY)
    return pl.pallas_call(
        hand_kernel,
        out_shape=(
            jax.ShapeDtypeStruct(taps.shape, F32),
            jax.ShapeDtypeStruct(grad_latent.shape, BF16),
        )
        + (jax.ShapeDtypeStruct((AW, 640), F32),) * 4,
        in_specs=[anywhere] * 3,
        out_specs=(anywhere,) * 6,
        scratch_shapes=[
            pltpu.VMEM((4, AW, 640), BF16),
            pltpu.VMEM((4, AW, 640), F32),
            pltpu.VMEM(taps.shape, F32),
            pltpu.VMEM(grad_latent.shape, BF16),
            pltpu.SemaphoreType.DMA((6,)),
            pltpu.SemaphoreType.DMA((6,)),
        ],
        compiler_params=pltpu.CompilerParams(vmem_limit_bytes=60 * 1024 * 1024),
        name="hand_out",
    )(rows, taps, grad_latent)


def body(latent, cotangent, conv_weight, query_weight, key_weight, value_weight, out_weight):
    sums = whole(
        latent.reshape(128, 640), cotangent.reshape(128, 640), out_weight, key_weight.T, value_weight.T,
        query_weight.T, conv_weight.reshape(9, 640, 640),
    )
    taps, grad_latent, query, key, value, out = hand_out(*sums)
    return (grad_latent.reshape(latent.shape), taps.reshape(3, 3, 20, 640), query.T, key.T, value.T, out)


def solution(mesh):
    placed = (P("dp", "patch", None, None), P("dp", "patch", None, None), P(), P(), P(), P(), P())
    return jax.shard_map(
        body,
        mesh=mesh,
        in_specs=placed,
        out_specs=(P("dp", "patch", None, None), P(None, None, "patch", None), P(), P(), P(), P()),
        check_vma=False,
    )
```

```python
import functools
import jax
import jax.numpy as jnp
from jax import lax
from jax.experimental import pallas as pl
from jax.experimental.pallas import tpu as pltpu
from jax.sharding import PartitionSpec as P

NH = 5
HD = 64
AW = 320
MESH = pl.DeviceIdType.MESH
F32 = jnp.float32
BF16 = jnp.bfloat16


def place():
    p = lax.axis_index("patch")
    return lax.axis_index("dp"), p // 16, lax.rem(p, 16) // 2, lax.rem(p, 2)


def send(src, dst, send_sem, recv_sem, device):
    copy = pltpu.make_async_remote_copy(
        src_ref=src, dst_ref=dst, send_sem=send_sem, recv_sem=recv_sem,
        device_id=device, device_id_type=MESH,
    )
    copy.start()
    return copy


NT = (((1,), (1,)), ((), ()))
LOG2E = 1.4426950408889634


def remote(src, dst, send_sem, recv_sem, device):
    return pltpu.make_async_remote_copy(
        src_ref=src, dst_ref=dst, send_sem=send_sem, recv_sem=recv_sem,
        device_id=device, device_id_type=MESH,
    )


def attend_kernel(windows, lhs_ref, x_ref, out_ref, kv, kvt, qd, qs, gs, q4, g4, gt, gt4, scores, slope, pb, sb,
                  top, low, att, delta, dq, top4, low4, att4, delta4, dq4, part, box_up, box_down, ahead, behind,
                  mix, mix_in, stat, own4, stage, res,
                  kv_s, kv_r, qd_s, qd_r, up_s, up_r, down_s, down_r, rup_s, rup_r, rdown_s, rdown_r,
                  mix_s, mix_r, stat_s, stat_r, g_s, g_r):
    dp, xlo, z, core = place()
    j = xlo * 2 + core

    def at_z(step):
        return (dp, xlo * 16 + lax.rem(z + step + 8, 8) * 2 + core)

    def in_quad(step):
        m = lax.rem(j + step, 4)
        return m, (dp, (m // 2) * 16 + z * 2 + lax.rem(m, 2))

    def rows(m):
        return pl.ds(pl.multiple_of(m * 128, 128), 128)

    first, second = [], []
    for s in range(1, 4):
        m, device = in_quad(s)
        first.append(send(x_ref.at[2 * m], kv.at[z, rows(j), :], kv_s.at[s], kv_r.at[s], device))
    for s in range(1, 4):
        m, device = in_quad(s)
        second.append(send(x_ref.at[2 * m + 1], qd.at[0, rows(j), :], qd_s.at[0, s], qd_r.at[0, s], device))
        second.append(send(x_ref.at[8], qd.at[1, rows(j), :], qd_s.at[1, s], qd_r.at[1, s], device))
    kv[z, rows(j), :] = x_ref[2 * j]
    kv[z, 512:640] = x_ref[9]
    qd[0, rows(j), :] = x_ref[2 * j + 1]
    qd[1, rows(j), :] = x_ref[8]
    lane = lax.broadcasted_iota(jnp.int32, (128, 128), 1)
    left = lane < 64
    for ref in (top, top4):
        ref[...] = jnp.full(ref.shape, -jnp.inf, F32)
    for ref in (low, low4, att, att4, dq, dq4):
        ref[...] = jnp.zeros(ref.shape, F32)

    cuts = (slice(0, 320), slice(320, 640))

    def ring_up(s, i):
        ref = kv.at[lax.rem(z + 8 - s, 8), cuts[i]]
        return remote(ref, ref, up_s.at[s, i], up_r.at[s, i], at_z(1))

    def ring_down(s, i):
        ref = kv.at[lax.rem(z + s, 8), cuts[i]]
        return remote(ref, ref, down_s.at[s, i], down_r.at[s, i], at_z(-1))

    for copy in first:
        copy.wait()
    for i in range(2):
        ring_up(0, i).start()
        ring_down(0, i).start()
    windows(lhs_ref)
    for copy in second:
        copy.wait()
    for m in range(4):
        r = slice(m * 128, m * 128 + 128)
        for i, (a, b, bt) in enumerate(((qs, gs, gt), (q4, g4, gt4))):
            pair = qd[i, r].astype(F32)
            a[r] = jnp.where(left, pair, 0.0).astype(BF16)
            b[r] = jnp.where(left, 0.0, pair).astype(BF16)
            bt[:, r] = pair.T[64:128]

    def soften(b, keys, q, top, low, att):
        s = scores[b, keys, q]
        old = top[:, q]
        new = jnp.maximum(old, jnp.max(s, axis=0, keepdims=True))
        p = jnp.exp2(s - new)
        fade = jnp.exp2(old - new)
        low[:, q] = low[:, q] * fade + jnp.sum(p, axis=0, keepdims=True)
        top[:, q] = new
        att[:, q] = att[:, q] * fade
        pb[keys, q] = p.astype(BF16)

    main, side = slice(0, 512), slice(512, 640)
    quarters = [slice(128 * i, 128 * i + 128) for i in range(4)]

    def pass_one(t, carry):
        for s in range(3):
            @pl.when(t == 2 * s + 1)
            def _():
                for i in range(2):
                    ring_up(s, i).wait_recv()
                    if s < 2 or i == 0:
                        ring_up(s + 1, i).start()
                    ring_down(s, i).wait_recv()
                    if s < 2 or i == 1:
                        ring_down(s + 1, i).start()

        @pl.when(t == 7)
        def _():
            ring_up(3, 0).wait_recv()
            ring_down(3, 1).wait_recv()

        offset = jnp.where(lax.rem(t, 2) == 1, 8 - (t + 1) // 2, t // 2)
        b = lax.rem(z + offset, 8)
        scores[b, main] = lax.dot_general(kv[b, main], qs[...], NT, preferred_element_type=F32) * LOG2E
        scores[b, side] = lax.dot_general(kv[b, side], q4[...], NT, preferred_element_type=F32) * LOG2E
        for i in range(5):
            c = slice(128 * i, 128 * i + 128)
            kvt[b, :, c] = kv[b, c].astype(F32).T.astype(BF16)
        for q in quarters:
            soften(b, main, q, top, low, att)
            soften(b, side, q, top4, low4, att4)
        att[...] += jnp.dot(kvt[b, 64:128, main], pb[main], preferred_element_type=F32)
        att4[...] += jnp.dot(kvt[b, 64:128, side], pb[side], preferred_element_type=F32)
        return carry

    lax.fori_loop(0, 8, pass_one, 0)
    for m in range(4):
        q = quarters[m]
        mix[m, 0:64] = att4[:, q]
        mix[m, 64:65] = top4[:, q]
        mix[m, 65:66] = low4[:, q]
        mix[m, 66:72] = jnp.zeros((6, 128), F32)
    mixing = []
    for s in range(1, 4):
        m, device = in_quad(s)
        mixing.append(send(mix.at[m], mix_in.at[s], mix_s.at[s], mix_r.at[s], device))
    mix_in[0] = mix[j]
    att[...] = att[...] / low[...]
    top[...] = top[...] + jnp.log2(low[...])
    delta[...] = jnp.sum(att[...] * gt[...], axis=0, keepdims=True)

    def stat_copy(s):
        return remote(stat.at[j], stat.at[j], stat_s.at[s], stat_r.at[s], in_quad(s)[1])

    late = []
    for q in quarters:
        stage[1, q] = jnp.concatenate([att[:, q], jnp.zeros((64, 128), F32)], axis=0).T.astype(BF16)
    for s in range(1, 4):
        m, device = in_quad(s)
        late.append(send(stage.at[1, rows(m), :], res.at[j, 1], g_s.at[2, s], g_r.at[2, s], device))
    for copy in mixing:
        copy.wait()
    tops = [mix_in[s, 64:65] for s in range(4)]
    best = jnp.maximum(jnp.maximum(tops[0], tops[1]), jnp.maximum(tops[2], tops[3]))
    total, blend = jnp.zeros((1, 128), F32), jnp.zeros((64, 128), F32)
    for s in range(4):
        weight = jnp.exp2(tops[s] - best)
        total = total + mix_in[s, 65:66] * weight
        blend = blend + mix_in[s, 0:64] * weight
    blend = blend / total
    own4[0:64] = blend
    own4[64:128] = jnp.zeros((64, 128), F32)
    stat[j, 0:1] = best + jnp.log2(total)
    stat[j, 1:2] = jnp.sum(blend * gt4[:, rows(j)], axis=0, keepdims=True)
    stat[j, 2:8] = jnp.zeros((6, 128), F32)
    for s in range(1, 4):
        stat_copy(s).start()

    def sum_up(s, i):
        return remote(box_up.at[s, cuts[i]], ahead.at[s, cuts[i]], rup_s.at[s, i], rup_r.at[s, i], at_z(1))

    def sum_down(s, i):
        return remote(
            box_down.at[s, cuts[i]], behind.at[s, cuts[i]], rdown_s.at[s, i], rdown_r.at[s, i], at_z(-1)
        )

    def pass_on(box, landed, step, s, i):
        c = cuts[i]
        step(s, i).wait_recv()
        box[s + 1, c] = (part[c] + landed[s, c].astype(F32)).astype(BF16)
        step(s + 1, i).start()

    def slopes(b, keys, q, top, delta):
        p = jnp.exp2(scores[b, keys, q] - top[:, q])
        pb[keys, q] = p.astype(BF16)
        sb[keys, q] = (p * (slope[keys, q] - delta[:, q])).astype(BF16)

    def pass_two(t, carry):
        offset = jnp.where(lax.rem(t, 2) == 0, 4 + t // 2, 4 - (t + 1) // 2)
        b = lax.rem(z + offset, 8)
        slope[main] = lax.dot_general(kv[b, main], gs[...], NT, preferred_element_type=F32)
        slope[side] = lax.dot_general(kv[b, side], g4[...], NT, preferred_element_type=F32)
        for q in quarters:
            slopes(b, main, q, top, delta)
        dq[...] += jnp.dot(kvt[b, 0:64, main], sb[main], preferred_element_type=F32)
        part[main] = jnp.dot(sb[main], qs[...], preferred_element_type=F32) + jnp.dot(
            pb[main], gs[...], preferred_element_type=F32
        )

        @pl.when(t == 0)
        def _():
            for s in range(1, 4):
                stat_copy(s).wait()
            for m in range(4):
                top4[:, quarters[m]] = stat[m, 0:1]
                delta4[:, quarters[m]] = stat[m, 1:2]

        for q in quarters:
            slopes(b, side, q, top4, delta4)
        dq4[...] += jnp.dot(kvt[b, 0:64, side], sb[side], preferred_element_type=F32)
        part[side] = jnp.dot(sb[side], q4[...], preferred_element_type=F32) + jnp.dot(
            pb[side], g4[...], preferred_element_type=F32
        )

        @pl.when(t == 0)
        def _():
            box_up[0, cuts[0]] = part[cuts[0]].astype(BF16)
            sum_up(0, 0).start()
            box_down[0, cuts[1]] = part[cuts[1]].astype(BF16)
            sum_down(0, 1).start()

        @pl.when(t == 1)
        def _():
            box_up[1, cuts[1]] = part[cuts[1]].astype(BF16)
            sum_up(1, 1).start()
            pass_on(box_up, ahead, sum_up, 0, 0)

        @pl.when(t == 2)
        def _():
            box_down[1, cuts[0]] = part[cuts[0]].astype(BF16)
            sum_down(1, 0).start()
            pass_on(box_down, behind, sum_down, 0, 1)

        for s in range(1, 3):
            @pl.when(t == 2 * s + 1)
            def _():
                pass_on(box_up, ahead, sum_up, s, 1)
                pass_on(box_up, ahead, sum_up, s, 0)

            @pl.when(t == 2 * s + 2)
            def _():
                pass_on(box_down, behind, sum_down, s, 0)
                pass_on(box_down, behind, sum_down, s, 1)

        return carry

    lax.fori_loop(0, 8, pass_two, 0)
    for q in quarters:
        both = jnp.concatenate([dq[:, q], dq4[:, q]], axis=0) * HD ** -0.5
        stage[0, q] = both.T.astype(BF16)
    for s in range(1, 4):
        m, device = in_quad(s)
        late.append(send(stage.at[0, rows(m), :], res.at[j, 0], g_s.at[0, s], g_r.at[0, s], device))
    for i in range(2):
        sum_up(3, i).wait_recv()
        sum_down(3, i).wait_recv()
    stage[2] = (part[main] + ahead[3, main].astype(F32) + behind[3, main].astype(F32)).astype(BF16)
    for s in range(1, 4):
        m, device = in_quad(s)
        late.append(send(stage.at[2, rows(m), :], res.at[j, 2], g_s.at[1, s], g_r.at[1, s], device))
    own = part[side] + ahead[3, side].astype(F32) + behind[3, side].astype(F32)
    for t in range(3):
        res[j, t] = stage[t, rows(j), :]
    for s in range(4):
        for i in range(2):
            if s < 3 or i == 0:
                ring_up(s, i).wait_send()
            if s < 3 or i == 1:
                ring_down(s, i).wait_send()
            if s > 0 or i == 0:
                sum_up(s, i).wait_send()
            if s > 0 or i == 1:
                sum_down(s, i).wait_send()
    for copy in late:
        copy.wait()

    def swap(a):
        return pltpu.roll(a, 64, axis=1)

    for t, source, high in ((0, 1, False), (1, 0, False), (2, 2, False), (3, 2, True)):
        for i in range(2):
            a, b = res[2 * i, source].astype(F32), res[2 * i + 1, source].astype(F32)
            pair = jnp.where(left, swap(a), b) if high else jnp.where(left, a, swap(b))
            out_ref[t, :, 128 * i : 128 * i + 128] = pair.astype(BF16)
    last4 = (
        own4[...].T,
        swap(sum(res[m, 0].astype(F32) for m in range(4))),
        own,
        swap(own),
    )
    for t in range(4):
        out_ref[t, :, 256:384] = jnp.where(left, last4[t], 0.0).astype(BF16)


def shifted(rows, j):
    before = jnp.where(j == 0, 0.0, pltpu.roll(rows, 1, axis=0))
    after = jnp.where(j == 63, 0.0, pltpu.roll(rows, 63, axis=0))
    return before, rows, after


def first_kernel(hbm, lat_ref, cot_ref, wq_ref, wk_ref, wv_ref, wo_ref, w, hid_ref, x_ref, load_sem, w_sem,
                 halo, turned, sbuf, share, sh, acc, tmp, halo_s, halo_r, share_s, share_r, rim_s, rim_r):
    dp, xlo, z, core = place()
    p = lax.axis_index("patch")
    spot = dp * 2 + xlo
    index = lax.rem(p, 16)

    def at(step):
        other = lax.rem(p + step + 32, 32)
        return (dp, other)

    local = (lat_ref, cot_ref, wo_ref, wk_ref, wv_ref, wq_ref)
    inputs = []
    for i, ref in enumerate(local):
        copy = pltpu.make_async_copy(hbm[i], ref, load_sem.at[i])
        copy.start()
        inputs.append(copy)
    loads = []
    for t in range(9):
        copy = pltpu.make_async_copy(hbm[6].at[t], w.at[t], w_sem.at[t])
        copy.start()
        loads.append(copy)
    barrier = pltpu.get_barrier_semaphore()

    def hello(s, carry):
        pl.semaphore_signal(barrier, inc=1, device_id=at(s), device_id_type=MESH)
        return carry

    def hello_plane(s, carry):
        other = lax.rem(spot + s, 16)
        device = (other // 2, lax.rem(other, 2) * 16 + index)
        pl.semaphore_signal(barrier, inc=1, device_id=device, device_id_type=MESH)
        return carry

    lax.fori_loop(1, 32, hello, 0)
    lax.fori_loop(1, 16, hello_plane, 0)
    inputs[0].wait()
    turned[0:640] = lat_ref[...].astype(F32).T
    turned[640:656] = jnp.zeros((16, 128), F32)
    for k in range(32):
        sbuf[k % 16, k // 16] = turned[20 * k : 20 * k + 32].astype(BF16)
    share[jnp.where(xlo == 0, 0, 17)] = jnp.zeros((2, 32, 128), BF16)
    share[index + 1] = sbuf[index]
    pl.semaphore_wait(barrier, 46)
    near = [
        send(lat_ref.at[64:128], halo.at[0], halo_s.at[0], halo_r.at[0], at(1)),
        send(lat_ref.at[0:64], halo.at[1], halo_s.at[1], halo_r.at[1], at(-1)),
    ]

    def share_copy(s):
        other = lax.rem(index + s, 16)
        return remote(sbuf.at[other], share.at[index + 1], share_s.at[s], share_r.at[s], (dp, xlo * 16 + other))

    rim = index == jnp.where(xlo == 0, 15, 0)
    rim_slot = jnp.where(xlo == 0, 0, 17)

    def rim_copy(s):
        return remote(sbuf.at[s], share.at[rim_slot], rim_s.at[s], rim_r.at[0], (dp, (1 - xlo) * 16 + s))

    def share_start(s, carry):
        share_copy(s).start()
        return carry

    def rim_start(s, carry):
        rim_copy(s).start()
        return carry

    lax.fori_loop(1, 16, share_start, 0)

    @pl.when(rim)
    def _():
        lax.fori_loop(0, 16, rim_start, 0)

    lane = lax.broadcasted_iota(jnp.int32, (128, 128), 1)
    left = lane < 64

    def pack(low_value, high_value, first_slot, last_slot):
        for n in range(3):
            c = slice(128 * n, min(128 * n + 128, AW))
            width = c.stop - c.start
            tmp[0, :, 0:width] = low_value[:, c]
            tmp[1, :, 0:width] = high_value[:, c]
            a, b = tmp[0], tmp[1]
            even = jnp.where(left, a, pltpu.roll(b, 64, axis=1)).astype(BF16)
            if n == 2:
                x_ref[last_slot] = even
            else:
                x_ref[4 * n + first_slot] = even
                x_ref[4 * n + 2 + first_slot] = jnp.where(left, pltpu.roll(a, 64, axis=1), b).astype(BF16)

    inputs[1].wait()
    inputs[2].wait()
    out_grad = lax.dot_general(cot_ref[...], wo_ref[...], NT, preferred_element_type=F32)
    tmp[...] = jnp.zeros(tmp.shape, F32)
    for copy in near:
        copy.wait()
    j = lax.broadcasted_iota(jnp.int32, (64, 640), 0)
    rows = (
        jnp.where(p > 0, halo[0].astype(F32), 0.0),
        lat_ref[0:64].astype(F32),
        lat_ref[64:128].astype(F32),
        jnp.where(p < 31, halo[1].astype(F32), 0.0),
    )
    for r in range(4):
        moved = shifted(rows[r], j)
        for b in range(3):
            sh[b, 64 * r : 64 * r + 64] = moved[b].astype(BF16)
    for t in range(9):
        a, b = t // 3, t % 3
        loads[t].wait()
        term = jnp.dot(sh[b, 64 * a : 64 * a + 128], w[t], preferred_element_type=F32)
        if t:
            acc[...] += term
        else:
            acc[...] = term
    hid_ref[...] = acc[...].astype(BF16)
    for copy in inputs[3:]:
        copy.wait()

    def project(ref):
        value = lax.dot_general(hid_ref[...], ref[...], NT, preferred_element_type=F32)
        return value.astype(BF16).astype(F32)

    pack(project(wk_ref), project(wv_ref), 0, 9)
    pack(project(wq_ref) * HD ** -0.5, out_grad, 1, 8)

    def windows(lhs_ref):
        def share_end(s, carry):
            share_copy(s).wait()
            return carry

        def rim_end(s, carry):
            rim_copy(s).wait_send()
            return carry

        lax.fori_loop(1, 16, share_end, 0)
        rim_copy(0).wait_recv()

        @pl.when(rim)
        def _():
            lax.fori_loop(0, 16, rim_end, 0)

        col = lax.broadcasted_iota(jnp.int32, (32, 128), 1)
        near_side = col < 64
        col = lax.rem(col, 64)

        def one(q, carry):
            lanes = pl.ds(pl.multiple_of(lax.rem(q, 2) * 128, 128), 128)
            for c in range(2):
                here = share[q + 1, c].astype(F32)
                turn = pltpu.roll(here, 64, axis=1)
                above = jnp.where(near_side, pltpu.roll(share[q, c].astype(F32), 64, axis=1), turn)
                below = jnp.where(near_side, turn, pltpu.roll(share[q + 2, c].astype(F32), 64, axis=1))
                for a, value in enumerate((above, here, below)):
                    three = (
                        jnp.where(col == 0, 0.0, pltpu.roll(value, 1, axis=1)),
                        value,
                        jnp.where(col == 63, 0.0, pltpu.roll(value, 127, axis=1)),
                    )
                    for b in range(3):
                        row = 288 * c + 32 * (3 * a + b)
                        lhs_ref[q // 2, row : row + 32, lanes] = three[b].astype(BF16)
            return carry

        lax.fori_loop(0, 16, one, 0)

    return windows


def finish_kernel(parts_ref, hid_ref, cot_ref, wq_ref, wk_ref, wv_ref, lhs_ref, w, out_ref, taps_ref, lat_ref,
                  gh, halo, sh, acc, prod, small, turned, xs, half, ra, rb, rc, rd,
                  plane, xin, xsum, zin, zfull, pfull, tb, tin, tfull, halo_s, halo_r, up_s, down_s, sib_s, own_r, sib_r,
                  pair_s, pair_r, y_s, y_r, x_s, x_r, z_s, z_r, zb_s, zb_r, xb_s, xb_r, yb_s, yb_r, fin_s, fin_r,
                  t_s, t_r, u_s, u_r):
    dp, xlo, z, core = place()
    p = lax.axis_index("patch")
    xhi, y = dp // 4, lax.rem(dp, 4)
    x = xhi * 2 + xlo
    sib = (dp, xlo * 16 + z * 2 + 1 - core)

    def at_z(s):
        other = lax.rem(z + s + 8, 8)
        return other, (dp, xlo * 16 + other * 2 + core)

    def at_y(s):
        other = lax.rem(y + s + 4, 4)
        return other, (xhi * 4 + other, p)

    def at_x(s):
        other = lax.rem(x + s + 4, 4)
        return other, (other // 2 * 4 + y, lax.rem(other, 2) * 16 + z * 2 + core)

    spot = dp * 2 + xlo

    def at_spot(s):
        other = lax.rem(spot + s, 16)
        return other, (other // 2, lax.rem(other, 2) * 16 + z * 2 + core)

    def at_dp(s):
        other = lax.rem(dp + s, 8)
        return other, (other, p)

    def at_p(s):
        return (dp, lax.rem(p + s + 32, 32))

    mine = pl.ds(pl.multiple_of(core * 128, 128), 128)
    sent = []

    value = cot_ref[...].astype(F32)
    for t, ref in ((1, wq_ref), (2, wk_ref), (3, wv_ref)):
        value = value + jnp.dot(parts_ref[t, :, 0:AW], ref[...], preferred_element_type=F32)
    gh[z, mine, :] = value.astype(BF16)

    ways = {"up": (up_s, at_z(1)[1]), "down": (down_s, at_z(-1)[1]), "sib": (sib_s, sib)}
    count = {way: 0 for way in ways}
    low = pl.ds(pl.multiple_of(core * 128, 64), 64)
    high = pl.ds(pl.multiple_of(core * 128 + 64, 64), 64)

    def block(dz):
        return lax.rem(z + dz + 8, 8)

    def ship(dz, way, i):
        u = block(dz)
        sem, device = ways[way]
        if way == "sib":
            ref, recv = gh.at[u, mine, :], sib_r.at[u]
        else:
            ref, recv = gh.at[u, (low, high)[i], :], own_r.at[2 * u + i]
        sent.append(send(ref, ref, sem.at[count[way]], recv, device))
        count[way] += 1

    def arrive(dz):
        u = block(dz)
        for i in range(2):
            ref = gh.at[u, (low, high)[i], :]
            remote(ref, ref, up_s.at[0], own_r.at[2 * u + i], sib).wait_recv()
        ship(dz, "sib", 0)

    def arrive_both(dz):
        for i in range(2):
            for d, way in ((-dz, "up"), (dz, "down")):
                u = block(d)
                ref = gh.at[u, (low, high)[i], :]
                remote(ref, ref, up_s.at[0], own_r.at[2 * u + i], sib).wait_recv()
                if dz < 3 or i == (0 if way == "up" else 1):
                    ship(d, way, i)
        ship(-dz, "sib", 0)
        ship(dz, "sib", 0)

    edge = gh.at[z]
    near = [
        send(edge.at[high, :], halo.at[0], halo_s.at[0], halo_r.at[0], at_p(1)),
        send(edge.at[low, :], halo.at[1], halo_s.at[1], halo_r.at[1], at_p(-1)),
    ]
    for i in range(2):
        ship(0, "up", i)
        ship(0, "down", i)
    ship(0, "sib", 0)

    for i, t in enumerate((1, 2, 3, 0)):
        turned[...] = parts_ref[t].astype(F32).T.astype(BF16)
        right = hid_ref if t else cot_ref
        xs[AW * i : AW * i + AW] = jnp.dot(turned[0:AW], right[...], preferred_element_type=F32).astype(BF16)

    first_at, second_at = (at_y, at_x), (at_x, at_y)
    first_index, second_index = (y, x), (x, y)
    halves = range(2)

    def part(c, h, k):
        return pl.ds(pl.multiple_of(c * 640 + h * 320 + k * 80, 16), 80)

    def low_of(c, h, k):
        return pl.ds(pl.multiple_of(c * 640 + h * 320 + k * 80, 16), 48)

    def high_of(c, h, k):
        return pl.ds(pl.multiple_of(c * 640 + h * 320 + k * 80 + 48, 16), 32)

    pair = []
    for h in halves:
        theirs = pl.ds(pl.multiple_of((1 - core) * 640 + h * 320, 16), 320)
        there = pl.ds(320 * h, 320)
        pair.append(send(xs.at[theirs], half.at[there], pair_s.at[h], pair_r.at[h], sib))
    arrive_both(1)

    for copy in near:
        copy.wait()
    j = lax.broadcasted_iota(jnp.int32, (64, 640), 0)
    rows = (
        jnp.where(p > 0, halo[0].astype(F32), 0.0),
        gh[z, low, :].astype(F32),
        gh[z, high, :].astype(F32),
        jnp.where(p < 31, halo[1].astype(F32), 0.0),
    )
    for r in range(4):
        moved = shifted(rows[r], j)
        for b in range(3):
            sh[2 - b, 64 * r : 64 * r + 64] = moved[b].astype(BF16)

    def tap(t):
        a, b = t // 3, t % 3
        start = 64 * (2 - a)
        term = lax.dot_general(sh[b, start : start + 128], w[t], NT, preferred_element_type=F32)
        if t:
            acc[...] += term
        else:
            acc[...] = term

    def gain(dz, start=False):
        u = block(dz)
        ref = gh.at[u, pl.ds(pl.multiple_of((1 - core) * 128, 128), 128), :]
        remote(ref, ref, up_s.at[0], sib_r.at[u], sib).wait_recv()
        term = jnp.dot(lhs_ref[u], gh[u], preferred_element_type=F32)
        if start:
            prod[...] = term
        else:
            prod[...] += term

    tap(0)
    for copy in pair:
        copy.wait()
    for h in halves:
        mine_rows = pl.ds(pl.multiple_of(core * 640 + h * 320, 16), 320)
        r = slice(320 * h, 320 * h + 320)
        half[r] = (half[r].astype(F32) + xs[mine_rows].astype(F32)).astype(BF16)
    up, down, far = [], [], []
    for h in halves:
        up.append(first_at[h](1))
        down.append(first_at[h](-1))
        far.append(lax.rem(first_index[h] + 2, 4))
        sent.append(send(half.at[low_of(0, h, far[h])], ra.at[h], y_s.at[h, 0], y_r.at[h, 0], up[h][1]))
        sent.append(send(half.at[high_of(0, h, far[h])], rb.at[h], y_s.at[h, 1], y_r.at[h, 1], down[h][1]))
    tap(1)
    arrive_both(2)
    for h in halves:
        remote(half.at[low_of(0, h, 0)], ra.at[h], y_s.at[h, 0], y_r.at[h, 0], sib).wait_recv()
        remote(half.at[high_of(0, h, 0)], rb.at[h], y_s.at[h, 1], y_r.at[h, 1], sib).wait_recv()
        r = low_of(0, h, up[h][0])
        half[r] = (half[r].astype(F32) + ra[h].astype(F32)).astype(BF16)
        r = high_of(0, h, down[h][0])
        half[r] = (half[r].astype(F32) + rb[h].astype(F32)).astype(BF16)
        sent.append(send(half.at[part(0, h, up[h][0])], rc.at[h], y_s.at[h, 2], y_r.at[h, 2], up[h][1]))
        sent.append(send(half.at[part(0, h, down[h][0])], rd.at[h], y_s.at[h, 3], y_r.at[h, 3], down[h][1]))
    tap(2)
    gain(0, True)
    arrive_both(3)
    gain(-1)
    def quarter(k):
        return pl.ds(pl.multiple_of(k * 128, 128), 128)

    def slot(k):
        return pl.ds(pl.multiple_of(k * 16, 16), 16)

    crossing = []
    for h in halves:
        remote(half.at[part(0, h, 0)], rc.at[h], y_s.at[h, 2], y_r.at[h, 2], sib).wait_recv()
        remote(half.at[part(0, h, 0)], rd.at[h], y_s.at[h, 3], y_r.at[h, 3], sib).wait_recv()
        whole = half[part(0, h, first_index[h])].astype(F32) + rc[h].astype(F32) + rd[h].astype(F32)
        for n in range(5):
            plane[h, 80 * n : 80 * n + 80] = whole[:, 128 * n : 128 * n + 128].astype(BF16)
        plane[h, 400:512] = jnp.zeros((112, 128), BF16)
        for s in range(1, 4):
            other, device = second_at[h](s)
            crossing.append(send(plane.at[h, quarter(other)], xin.at[h, s], x_s.at[h, s], x_r.at[h, s], device))
    gain(1)
    arrive(4)
    for copy in crossing:
        copy.wait()
    for h in halves:
        whole = plane[h, quarter(second_index[h])].astype(F32)
        for s in range(1, 4):
            whole = whole + xin[h, s].astype(F32)
        xsum[h] = whole.astype(BF16)
    along = []
    for s in range(1, 8):
        other, device = at_z(s)
        along.append(send(xsum.at[:, slot(other), :], zin.at[s], z_s.at[s], z_r.at[s], device))
    gain(-2)
    whole = xsum[:, slot(z), :].astype(F32)
    for s in range(1, 8):
        along[s - 1].wait()
        whole = whole + zin[s].astype(F32)
    zfull[:, slot(z), :] = whole.astype(BF16)
    zback = []
    for s in range(1, 8):
        ref = zfull.at[:, slot(z), :]
        zback.append(send(ref, ref, zb_s.at[s], zb_r.at[s], at_z(s)[1]))
    gain(2)
    for copy in zback:
        copy.wait()
    xback = []
    for h in halves:
        pfull[h, quarter(second_index[h])] = zfull[h]
        for s in range(1, 4):
            ref = pfull.at[h, quarter(second_index[h])]
            xback.append(send(ref, ref, xb_s.at[h, s], xb_r.at[h, s], second_at[h](s)[1]))
    gain(-3)
    gain(3)
    for copy in xback:
        copy.wait()
    fin = []
    for h in halves:
        for n in range(5):
            out_ref[part(core, h, first_index[h]), 128 * n : 128 * n + 128] = pfull[h, 80 * n : 80 * n + 80]

    def forward(rows, send_sem, recv_sem, device):
        return send(out_ref.at[rows], out_ref.at[rows], send_sem, recv_sem, device)

    def landed(rows, h, i):
        remote(out_ref.at[rows], out_ref.at[rows], yb_s.at[h, i], yb_r.at[h, i], sib).wait_recv()

    for h in halves:
        rows = part(core, h, first_index[h])
        sent.append(forward(rows, yb_s.at[h, 0], yb_r.at[h, 0], up[h][1]))
        sent.append(forward(rows, yb_s.at[h, 1], yb_r.at[h, 1], down[h][1]))
        fin.append(forward(rows, fin_s.at[h, 0], fin_r.at[h, 0], sib))
    gain(4)

    places = [(n, i, 192 * n + 16 * i) for n in range(5) for i in range(12)]
    small[180:192] = jnp.zeros((12, 640), F32)
    for c in range(2):
        for t in range(9):
            small[20 * t : 20 * t + 20] = prod[288 * c + 32 * t : 288 * c + 32 * t + 20]
        for n, i, f in places:
            piece = small[16 * i : 16 * i + 16, 128 * n : 128 * n + 128].astype(BF16)
            tb[c, f // 128, f % 128 : f % 128 + 16] = piece
        tb[c, 7, 64:128] = jnp.zeros((64, 128), BF16)
    there = []
    for s in range(1, 16):
        other, device = at_spot(s)
        there.append(send(tb.at[lax.rem(other, 2), other // 2], tin.at[s], t_s.at[s], t_r.at[s], device))
    tap(3)
    for h in halves:
        landed(part(core, h, down[h][0]), h, 0)
        landed(part(core, h, up[h][0]), h, 1)
        sent.append(forward(low_of(core, h, down[h][0]), yb_s.at[h, 2], yb_r.at[h, 2], up[h][1]))
        sent.append(forward(high_of(core, h, up[h][0]), yb_s.at[h, 3], yb_r.at[h, 3], down[h][1]))
        fin.append(forward(part(core, h, down[h][0]), fin_s.at[h, 1], fin_r.at[h, 1], sib))
        fin.append(forward(part(core, h, up[h][0]), fin_s.at[h, 2], fin_r.at[h, 2], sib))
    tap(4)
    tap(5)
    for h in halves:
        landed(low_of(core, h, far[h]), h, 2)
        landed(high_of(core, h, far[h]), h, 3)
        fin.append(forward(part(core, h, far[h]), fin_s.at[h, 3], fin_r.at[h, 3], sib))
    tap(6)
    whole = tb[xlo, dp].astype(F32)
    for s in range(1, 16):
        there[s - 1].wait()
        whole = whole + tin[s].astype(F32)
    tfull[dp] = whole.astype(BF16)
    tback = []
    for s in range(1, 8):
        ref = tfull.at[dp]
        tback.append(send(ref, ref, u_s.at[s], u_r.at[s], at_dp(s)[1]))
    tap(7)
    tap(8)
    lat_ref[...] = acc[...].astype(BF16)
    for copy in tback:
        copy.wait()
    for n, i, f in places:
        small[16 * i : 16 * i + 16, 128 * n : 128 * n + 128] = tfull[f // 128, f % 128 : f % 128 + 16].astype(F32)
    for t in range(9):
        taps_ref[t] = small[20 * t : 20 * t + 20]
    for copy in fin:
        copy.wait()
    for copy in sent:
        copy.wait_send()


ATTEND = 52


def whole_kernel(*refs):
    hbm, (rows_ref, taps_ref, lat_ref), scratch = refs[:7], refs[7:10], refs[10:]
    shared, scratch = scratch[:11], scratch[11:]
    latent, cot, wq, wk, wv, wo, w, hidden, packed, lhs, parts = shared
    one, two, three = scratch[:15], scratch[15:15 + ATTEND], scratch[15 + ATTEND :]
    windows = first_kernel(hbm, latent, cot, wq, wk, wv, wo, w, hidden, packed, *one)
    attend_kernel(windows, lhs, packed, parts, *two)
    finish_kernel(parts, hidden, cot, wq, wk, wv, lhs, w, rows_ref, taps_ref, lat_ref, *three)


def whole(*args):
    dma = pltpu.SemaphoreType.DMA
    vmem = pl.BlockSpec(memory_space=pltpu.VMEM)

    def b16(*shape):
        return pltpu.VMEM(shape, BF16)

    def f32(*shape):
        return pltpu.VMEM(shape, F32)

    shared = [
        b16(128, 640), b16(128, 640), b16(320, 640), b16(320, 640), b16(320, 640), b16(320, 640),
        b16(9, 640, 640), b16(128, 640), b16(10, 128, 128), b16(8, 576, 256), b16(4, 128, 384),
    ]
    one = [
        dma((6,)), dma((9,)), b16(2, 64, 640), f32(656, 128), b16(16, 2, 32, 128), b16(18, 2, 32, 128),
        b16(3, 256, 640), f32(128, 640), f32(2, 128, 128),
        dma((2,)), dma((2,)), dma((16,)), dma((16,)), dma((16,)), dma((1,)),
    ]
    two = [
        b16(8, 640, 128), b16(8, 128, 640), b16(2, 512, 128), b16(512, 128), b16(512, 128), b16(512, 128), b16(512, 128),
        f32(64, 512), f32(64, 512),
        f32(8, 640, 512), f32(640, 512), b16(640, 512), b16(640, 512),
        f32(1, 512), f32(1, 512), f32(64, 512), f32(1, 512), f32(64, 512),
        f32(1, 512), f32(1, 512), f32(64, 512), f32(1, 512), f32(64, 512),
        f32(640, 128), b16(4, 640, 128), b16(4, 640, 128), b16(4, 640, 128), b16(4, 640, 128),
        f32(4, 72, 128), f32(4, 72, 128), f32(4, 8, 128), f32(128, 128), b16(3, 512, 128), b16(4, 3, 128, 128),
        dma((4,)), dma((4,)), dma((2, 4)), dma((2, 4)),
        dma((4, 2)), dma((4, 2)), dma((4, 2)), dma((4, 2)), dma((4, 2)), dma((4, 2)), dma((4, 2)), dma((4, 2)),
        dma((4,)), dma((4,)), dma((4,)), dma((4,)), dma((3, 4)), dma((3, 4)),
    ]
    three = [
        b16(8, 256, 640), b16(2, 64, 640), b16(3, 256, 640), f32(128, 640),
        f32(576, 640), f32(192, 640), b16(384, 128),
        b16(1280, 640), b16(640, 640), b16(2, 48, 640), b16(2, 32, 640), b16(2, 80, 640), b16(2, 80, 640),
        b16(2, 512, 128), b16(2, 4, 128, 128), b16(2, 128, 128), b16(8, 2, 16, 128), b16(2, 128, 128), b16(2, 512, 128),
        b16(2, 8, 128, 128), b16(16, 128, 128), b16(8, 128, 128),
        dma((2,)), dma((2,)), dma((7,)), dma((7,)), dma((8,)), dma((16,)), dma((8,)),
        dma((2,)), dma((2,)), dma((2, 4)), dma((2, 4)), dma((2, 4)), dma((2, 4)), dma((8,)), dma((8,)),
        dma((8,)), dma((8,)), dma((2, 4)), dma((2, 4)), dma((2, 4)), dma((2, 4)), dma((2, 4)), dma((2, 4)),
        dma((16,)), dma((16,)), dma((8,)), dma((8,)),
    ]
    return pl.pallas_call(
        whole_kernel,
        out_shape=(
            jax.ShapeDtypeStruct((1280, 640), BF16),
            jax.ShapeDtypeStruct((9, 20, 640), F32),
            jax.ShapeDtypeStruct((128, 640), BF16),
        ),
        in_specs=[pl.BlockSpec(memory_space=pl.ANY)] * 7,
        out_specs=(vmem,) * 3,
        scratch_shapes=shared + one + two + three,
        compiler_params=pltpu.CompilerParams(
            collective_id=0, has_side_effects=True, vmem_limit_bytes=60 * 1024 * 1024
        ),
        name="whole",
    )(*args)


def hand_kernel(rows_ref, taps_ref, lat_ref, taps_out, lat_out, *rest):
    outs, (rows, wide, taps, lat, in_sem, out_sem) = rest[:4], rest[4:]
    loads = [
        pltpu.make_async_copy(rows_ref.at[AW * i : AW * i + AW], rows.at[i], in_sem.at[i]) for i in range(4)
    ]
    loads.append(pltpu.make_async_copy(taps_ref, taps, in_sem.at[4]))
    loads.append(pltpu.make_async_copy(lat_ref, lat, in_sem.at[5]))
    for copy in loads:
        copy.start()
    stores = []
    for i in range(6):
        loads[i].wait()
        if i < 4:
            wide[i] = rows[i].astype(F32)
            copy = pltpu.make_async_copy(wide.at[i], outs[i], out_sem.at[i])
        elif i == 4:
            copy = pltpu.make_async_copy(taps, taps_out, out_sem.at[i])
        else:
            copy = pltpu.make_async_copy(lat, lat_out, out_sem.at[i])
        copy.start()
        stores.append(copy)
    for copy in stores:
        copy.wait()


def hand_out(rows, taps, grad_latent):
    anywhere = pl.BlockSpec(memory_space=pl.ANY)
    return pl.pallas_call(
        hand_kernel,
        out_shape=(
            jax.ShapeDtypeStruct(taps.shape, F32),
            jax.ShapeDtypeStruct(grad_latent.shape, BF16),
        )
        + (jax.ShapeDtypeStruct((AW, 640), F32),) * 4,
        in_specs=[anywhere] * 3,
        out_specs=(anywhere,) * 6,
        scratch_shapes=[
            pltpu.VMEM((4, AW, 640), BF16),
            pltpu.VMEM((4, AW, 640), F32),
            pltpu.VMEM(taps.shape, F32),
            pltpu.VMEM(grad_latent.shape, BF16),
            pltpu.SemaphoreType.DMA((6,)),
            pltpu.SemaphoreType.DMA((6,)),
        ],
        compiler_params=pltpu.CompilerParams(vmem_limit_bytes=60 * 1024 * 1024),
        name="hand_out",
    )(rows, taps, grad_latent)


def body(latent, cotangent, conv_weight, query_weight, key_weight, value_weight, out_weight):
    sums = whole(
        latent.reshape(128, 640), cotangent.reshape(128, 640), out_weight, key_weight.T, value_weight.T,
        query_weight.T, conv_weight.reshape(9, 640, 640),
    )
    taps, grad_latent, query, key, value, out = hand_out(*sums)
    return (grad_latent.reshape(latent.shape), taps.reshape(3, 3, 20, 640), query.T, key.T, value.T, out)


def solution(mesh):
    placed = (P("dp", "patch", None, None), P("dp", "patch", None, None), P(), P(), P(), P(), P())
    return jax.shard_map(
        body,
        mesh=mesh,
        in_specs=placed,
        out_specs=(P("dp", "patch", None, None), P(None, None, "patch", None), P(), P(), P(), P()),
        check_vma=False,
    )
```

```python
import functools
import jax
import jax.numpy as jnp
from jax import lax
from jax.experimental import pallas as pl
from jax.experimental.pallas import tpu as pltpu
from jax.sharding import PartitionSpec as P

NH = 5
HD = 64
AW = 320
MESH = pl.DeviceIdType.MESH
F32 = jnp.float32
BF16 = jnp.bfloat16


def place():
    p = lax.axis_index("patch")
    return lax.axis_index("dp"), p // 16, lax.rem(p, 16) // 2, lax.rem(p, 2)


def send(src, dst, send_sem, recv_sem, device):
    copy = pltpu.make_async_remote_copy(
        src_ref=src, dst_ref=dst, send_sem=send_sem, recv_sem=recv_sem,
        device_id=device, device_id_type=MESH,
    )
    copy.start()
    return copy


NT = (((1,), (1,)), ((), ()))
LOG2E = 1.4426950408889634


def remote(src, dst, send_sem, recv_sem, device):
    return pltpu.make_async_remote_copy(
        src_ref=src, dst_ref=dst, send_sem=send_sem, recv_sem=recv_sem,
        device_id=device, device_id_type=MESH,
    )


def attend_kernel(windows, queries, lhs_ref, x_ref, out_ref, kv, kvt, qd, qs, gs, q4, g4, gt, gt4, scores, slope, pb, sb,
                  top, low, att, delta, dq, top4, low4, att4, delta4, dq4, part, box_up, box_down, ahead, behind,
                  mix, mix_in, stat, own4, stage, res,
                  kv_s, kv_r, qd_s, qd_r, up_s, up_r, down_s, down_r, rup_s, rup_r, rdown_s, rdown_r,
                  mix_s, mix_r, stat_s, stat_r, g_s, g_r):
    dp, xlo, z, core = place()
    j = xlo * 2 + core

    def at_z(step):
        return (dp, xlo * 16 + lax.rem(z + step + 8, 8) * 2 + core)

    def in_quad(step):
        m = lax.rem(j + step, 4)
        return m, (dp, (m // 2) * 16 + z * 2 + lax.rem(m, 2))

    def rows(m):
        return pl.ds(pl.multiple_of(m * 128, 128), 128)

    first, second = [], []
    for s in range(1, 4):
        m, device = in_quad(s)
        first.append(send(x_ref.at[2 * m], kv.at[z, rows(j), :], kv_s.at[s], kv_r.at[s], device))
    queries()
    for s in range(1, 4):
        m, device = in_quad(s)
        second.append(send(x_ref.at[2 * m + 1], qd.at[0, rows(j), :], qd_s.at[0, s], qd_r.at[0, s], device))
        second.append(send(x_ref.at[8], qd.at[1, rows(j), :], qd_s.at[1, s], qd_r.at[1, s], device))
    kv[z, rows(j), :] = x_ref[2 * j]
    kv[z, 512:640] = x_ref[9]
    qd[0, rows(j), :] = x_ref[2 * j + 1]
    qd[1, rows(j), :] = x_ref[8]
    lane = lax.broadcasted_iota(jnp.int32, (128, 128), 1)
    left = lane < 64
    for ref in (top, top4):
        ref[...] = jnp.full(ref.shape, -jnp.inf, F32)
    for ref in (low, low4, att, att4, dq, dq4):
        ref[...] = jnp.zeros(ref.shape, F32)

    cuts = (slice(0, 320), slice(320, 640))

    def ring_up(s, i):
        ref = kv.at[lax.rem(z + 8 - s, 8), cuts[i]]
        return remote(ref, ref, up_s.at[s, i], up_r.at[s, i], at_z(1))

    def ring_down(s, i):
        ref = kv.at[lax.rem(z + s, 8), cuts[i]]
        return remote(ref, ref, down_s.at[s, i], down_r.at[s, i], at_z(-1))

    for copy in first:
        copy.wait()
    for i in range(2):
        ring_up(0, i).start()
        ring_down(0, i).start()
    windows(lhs_ref)
    for copy in second:
        copy.wait()
    for m in range(4):
        r = slice(m * 128, m * 128 + 128)
        for i, (a, b, bt) in enumerate(((qs, gs, gt), (q4, g4, gt4))):
            pair = qd[i, r].astype(F32)
            a[r] = jnp.where(left, pair, 0.0).astype(BF16)
            b[r] = jnp.where(left, 0.0, pair).astype(BF16)
            bt[:, r] = pair.T[64:128]

    def soften(b, keys, q, top, low, att):
        s = scores[b, keys, q]
        old = top[:, q]
        new = jnp.maximum(old, jnp.max(s, axis=0, keepdims=True))
        p = jnp.exp2(s - new)
        fade = jnp.exp2(old - new)
        low[:, q] = low[:, q] * fade + jnp.sum(p, axis=0, keepdims=True)
        top[:, q] = new
        att[:, q] = att[:, q] * fade
        pb[keys, q] = p.astype(BF16)

    main, side = slice(0, 512), slice(512, 640)
    quarters = [slice(128 * i, 128 * i + 128) for i in range(4)]

    def pass_one(t, carry):
        for s in range(3):
            @pl.when(t == 2 * s + 1)
            def _():
                for i in range(2):
                    ring_up(s, i).wait_recv()
                    if s < 2 or i == 0:
                        ring_up(s + 1, i).start()
                    ring_down(s, i).wait_recv()
                    if s < 2 or i == 1:
                        ring_down(s + 1, i).start()

        @pl.when(t == 7)
        def _():
            ring_up(3, 0).wait_recv()
            ring_down(3, 1).wait_recv()

        offset = jnp.where(lax.rem(t, 2) == 1, 8 - (t + 1) // 2, t // 2)
        b = lax.rem(z + offset, 8)
        scores[b, main] = lax.dot_general(kv[b, main], qs[...], NT, preferred_element_type=F32) * LOG2E
        scores[b, side] = lax.dot_general(kv[b, side], q4[...], NT, preferred_element_type=F32) * LOG2E
        for i in range(5):
            c = slice(128 * i, 128 * i + 128)
            kvt[b, :, c] = kv[b, c].astype(F32).T.astype(BF16)
        for q in quarters:
            soften(b, main, q, top, low, att)
            soften(b, side, q, top4, low4, att4)
        att[...] += jnp.dot(kvt[b, 64:128, main], pb[main], preferred_element_type=F32)
        att4[...] += jnp.dot(kvt[b, 64:128, side], pb[side], preferred_element_type=F32)
        return carry

    lax.fori_loop(0, 8, pass_one, 0)
    for m in range(4):
        q = quarters[m]
        mix[m, 0:64] = att4[:, q]
        mix[m, 64:65] = top4[:, q]
        mix[m, 65:66] = low4[:, q]
        mix[m, 66:72] = jnp.zeros((6, 128), F32)
    mixing = []
    for s in range(1, 4):
        m, device = in_quad(s)
        mixing.append(send(mix.at[m], mix_in.at[s], mix_s.at[s], mix_r.at[s], device))
    mix_in[0] = mix[j]
    att[...] = att[...] / low[...]
    top[...] = top[...] + jnp.log2(low[...])
    delta[...] = jnp.sum(att[...] * gt[...], axis=0, keepdims=True)

    def stat_copy(s):
        return remote(stat.at[j], stat.at[j], stat_s.at[s], stat_r.at[s], in_quad(s)[1])

    late = []
    for q in quarters:
        stage[1, q] = jnp.concatenate([att[:, q], jnp.zeros((64, 128), F32)], axis=0).T.astype(BF16)
    for s in range(1, 4):
        m, device = in_quad(s)
        late.append(send(stage.at[1, rows(m), :], res.at[j, 1], g_s.at[2, s], g_r.at[2, s], device))
    def sum_up(s, i):
        return remote(box_up.at[s, cuts[i]], ahead.at[s, cuts[i]], rup_s.at[s, i], rup_r.at[s, i], at_z(1))

    def sum_down(s, i):
        return remote(
            box_down.at[s, cuts[i]], behind.at[s, cuts[i]], rdown_s.at[s, i], rdown_r.at[s, i], at_z(-1)
        )

    def pass_on(box, landed, step, s, i):
        c = cuts[i]
        step(s, i).wait_recv()
        box[s + 1, c] = (part[c] + landed[s, c].astype(F32)).astype(BF16)
        step(s + 1, i).start()

    def slopes(b, keys, q, top, delta):
        p = jnp.exp2(scores[b, keys, q] - top[:, q])
        pb[keys, q] = p.astype(BF16)
        sb[keys, q] = (p * (slope[keys, q] - delta[:, q])).astype(BF16)

    def merge():
        for copy in mixing:
            copy.wait()
        tops = [mix_in[s, 64:65] for s in range(4)]
        best = jnp.maximum(jnp.maximum(tops[0], tops[1]), jnp.maximum(tops[2], tops[3]))
        total, blend = jnp.zeros((1, 128), F32), jnp.zeros((64, 128), F32)
        for s in range(4):
            weight = jnp.exp2(tops[s] - best)
            total = total + mix_in[s, 65:66] * weight
            blend = blend + mix_in[s, 0:64] * weight
        blend = blend / total
        own4[0:64] = blend
        own4[64:128] = jnp.zeros((64, 128), F32)
        stat[j, 0:1] = best + jnp.log2(total)
        stat[j, 1:2] = jnp.sum(blend * gt4[:, rows(j)], axis=0, keepdims=True)
        stat[j, 2:8] = jnp.zeros((6, 128), F32)
        for s in range(1, 4):
            stat_copy(s).start()

    def main_part(b):
        slope[main] = lax.dot_general(kv[b, main], gs[...], NT, preferred_element_type=F32)
        for q in quarters:
            slopes(b, main, q, top, delta)
        part[main] = jnp.dot(sb[main], qs[...], preferred_element_type=F32) + jnp.dot(
            pb[main], gs[...], preferred_element_type=F32
        )

    def main_dq(b):
        dq[...] += jnp.dot(kvt[b, 0:64, main], sb[main], preferred_element_type=F32)

    def side_part(b):
        slope[side] = lax.dot_general(kv[b, side], g4[...], NT, preferred_element_type=F32)
        for q in quarters:
            slopes(b, side, q, top4, delta4)
        part[side] = jnp.dot(sb[side], q4[...], preferred_element_type=F32) + jnp.dot(
            pb[side], g4[...], preferred_element_type=F32
        )

    def side_dq(b):
        dq4[...] += jnp.dot(kvt[b, 0:64, side], sb[side], preferred_element_type=F32)

    edge = lax.rem(z + 4, 8)
    main_part(edge)
    box_up[0, cuts[0]] = part[cuts[0]].astype(BF16)
    sum_up(0, 0).start()
    box_down[0, 320:512] = part[320:512].astype(BF16)
    main_dq(edge)
    merge()

    def pass_two(t, carry):
        offset = jnp.where(lax.rem(t, 2) == 0, 4 + t // 2, 4 - (t + 1) // 2)
        b = lax.rem(z + offset, 8)
        main_part(b)

        @pl.when(t == 1)
        def _():
            for s in range(1, 4):
                stat_copy(s).wait()
            for m in range(4):
                top4[:, quarters[m]] = stat[m, 0:1]
                delta4[:, quarters[m]] = stat[m, 1:2]
            side_part(edge)
            box_down[0, side] = part[side].astype(BF16)
            sum_down(0, 1).start()
            side_dq(edge)

        side_part(b)

        @pl.when(t == 1)
        def _():
            box_up[1, cuts[1]] = part[cuts[1]].astype(BF16)
            sum_up(1, 1).start()
            pass_on(box_up, ahead, sum_up, 0, 0)

        @pl.when(t == 2)
        def _():
            box_down[1, cuts[0]] = part[cuts[0]].astype(BF16)
            sum_down(1, 0).start()
            pass_on(box_down, behind, sum_down, 0, 1)

        for s in range(1, 3):
            @pl.when(t == 2 * s + 1)
            def _():
                pass_on(box_up, ahead, sum_up, s, 1)
                pass_on(box_up, ahead, sum_up, s, 0)

            @pl.when(t == 2 * s + 2)
            def _():
                pass_on(box_down, behind, sum_down, s, 0)
                pass_on(box_down, behind, sum_down, s, 1)

        main_dq(b)
        side_dq(b)
        return carry

    lax.fori_loop(1, 8, pass_two, 0)
    for q in quarters:
        both = jnp.concatenate([dq[:, q], dq4[:, q]], axis=0) * HD ** -0.5
        stage[0, q] = both.T.astype(BF16)
    for s in range(1, 4):
        m, device = in_quad(s)
        late.append(send(stage.at[0, rows(m), :], res.at[j, 0], g_s.at[0, s], g_r.at[0, s], device))
    for i in range(2):
        sum_up(3, i).wait_recv()
        sum_down(3, i).wait_recv()
    stage[2] = (part[main] + ahead[3, main].astype(F32) + behind[3, main].astype(F32)).astype(BF16)
    for s in range(1, 4):
        m, device = in_quad(s)
        late.append(send(stage.at[2, rows(m), :], res.at[j, 2], g_s.at[1, s], g_r.at[1, s], device))
    own = part[side] + ahead[3, side].astype(F32) + behind[3, side].astype(F32)
    for t in range(3):
        res[j, t] = stage[t, rows(j), :]
    for s in range(4):
        for i in range(2):
            if s < 3 or i == 0:
                ring_up(s, i).wait_send()
            if s < 3 or i == 1:
                ring_down(s, i).wait_send()
            if s > 0 or i == 0:
                sum_up(s, i).wait_send()
            if s > 0 or i == 1:
                sum_down(s, i).wait_send()
    for copy in late:
        copy.wait()

    def swap(a):
        return pltpu.roll(a, 64, axis=1)

    for t, source, high in ((0, 1, False), (1, 0, False), (2, 2, False), (3, 2, True)):
        for i in range(2):
            a, b = res[2 * i, source].astype(F32), res[2 * i + 1, source].astype(F32)
            pair = jnp.where(left, swap(a), b) if high else jnp.where(left, a, swap(b))
            out_ref[t, :, 128 * i : 128 * i + 128] = pair.astype(BF16)
    last4 = (
        own4[...].T,
        swap(sum(res[m, 0].astype(F32) for m in range(4))),
        own,
        swap(own),
    )
    for t in range(4):
        out_ref[t, :, 256:384] = jnp.where(left, last4[t], 0.0).astype(BF16)


def shifted(rows, j):
    before = jnp.where(j == 0, 0.0, pltpu.roll(rows, 1, axis=0))
    after = jnp.where(j == 63, 0.0, pltpu.roll(rows, 63, axis=0))
    return before, rows, after


def first_kernel(hbm, lat_ref, cot_ref, wq_ref, wk_ref, wv_ref, wo_ref, w, hid_ref, x_ref, load_sem, w_sem,
                 halo, turned, sbuf, share, sh, acc, tmp, kept, halo_s, halo_r, share_s, share_r, rim_s, rim_r):
    dp, xlo, z, core = place()
    p = lax.axis_index("patch")
    spot = dp * 2 + xlo
    index = lax.rem(p, 16)

    def at(step):
        other = lax.rem(p + step + 32, 32)
        return (dp, other)

    local = (lat_ref, cot_ref, wo_ref, wk_ref, wv_ref, wq_ref)
    inputs = []
    for i, ref in enumerate(local):
        copy = pltpu.make_async_copy(hbm[i], ref, load_sem.at[i])
        copy.start()
        inputs.append(copy)
    loads = [pltpu.make_async_copy(hbm[6].at[t], w.at[t], w_sem.at[t]) for t in range(9)]
    for t in (3, 4, 5, 0, 1, 2, 6, 7, 8):
        loads[t].start()
    barrier = pltpu.get_barrier_semaphore()

    def hello(s, carry):
        pl.semaphore_signal(barrier, inc=1, device_id=at(s), device_id_type=MESH)
        return carry

    def hello_plane(s, carry):
        other = lax.rem(spot + s, 16)
        device = (other // 2, lax.rem(other, 2) * 16 + index)
        pl.semaphore_signal(barrier, inc=1, device_id=device, device_id_type=MESH)
        return carry

    lax.fori_loop(1, 32, hello, 0)
    lax.fori_loop(1, 16, hello_plane, 0)
    inputs[0].wait()
    turned[0:640] = lat_ref[...].astype(F32).T
    turned[640:656] = jnp.zeros((16, 128), F32)
    for k in range(32):
        sbuf[k % 16, k // 16] = turned[20 * k : 20 * k + 32].astype(BF16)
    share[jnp.where(xlo == 0, 0, 17)] = jnp.zeros((2, 32, 128), BF16)
    share[index + 1] = sbuf[index]
    pl.semaphore_wait(barrier, 46)
    near = [
        send(lat_ref.at[64:128], halo.at[0], halo_s.at[0], halo_r.at[0], at(1)),
        send(lat_ref.at[0:64], halo.at[1], halo_s.at[1], halo_r.at[1], at(-1)),
    ]

    def share_copy(s):
        other = lax.rem(index + s, 16)
        return remote(sbuf.at[other], share.at[index + 1], share_s.at[s], share_r.at[s], (dp, xlo * 16 + other))

    rim = index == jnp.where(xlo == 0, 15, 0)
    rim_slot = jnp.where(xlo == 0, 0, 17)

    def rim_copy(s):
        return remote(sbuf.at[s], share.at[rim_slot], rim_s.at[s], rim_r.at[0], (dp, (1 - xlo) * 16 + s))

    def share_start(s, carry):
        share_copy(s).start()
        return carry

    def rim_start(s, carry):
        rim_copy(s).start()
        return carry

    lax.fori_loop(1, 16, share_start, 0)

    @pl.when(rim)
    def _():
        lax.fori_loop(0, 16, rim_start, 0)

    lane = lax.broadcasted_iota(jnp.int32, (128, 128), 1)
    left = lane < 64

    def pack(low_value, high_value, first_slot, last_slot):
        for n in range(3):
            c = slice(128 * n, min(128 * n + 128, AW))
            width = c.stop - c.start
            tmp[0, :, 0:width] = low_value[:, c]
            tmp[1, :, 0:width] = high_value[:, c]
            a, b = tmp[0], tmp[1]
            even = jnp.where(left, a, pltpu.roll(b, 64, axis=1)).astype(BF16)
            if n == 2:
                x_ref[last_slot] = even
            else:
                x_ref[4 * n + first_slot] = even
                x_ref[4 * n + 2 + first_slot] = jnp.where(left, pltpu.roll(a, 64, axis=1), b).astype(BF16)

    inputs[1].wait()
    inputs[2].wait()
    out_grad = lax.dot_general(cot_ref[...], wo_ref[...], NT, preferred_element_type=F32)
    tmp[...] = jnp.zeros(tmp.shape, F32)
    j = lax.broadcasted_iota(jnp.int32, (64, 640), 0)

    def lay(r, value):
        for b, moved in enumerate(shifted(value, j)):
            sh[b, 64 * r : 64 * r + 64] = moved.astype(BF16)

    lay(1, lat_ref[0:64].astype(F32))
    lay(2, lat_ref[64:128].astype(F32))
    for t in (3, 4, 5, 0, 1, 2, 6, 7, 8):
        a, b = t // 3, t % 3
        if t == 0:
            for copy in near:
                copy.wait()
            lay(0, jnp.where(p > 0, halo[0].astype(F32), 0.0))
            lay(3, jnp.where(p < 31, halo[1].astype(F32), 0.0))
        loads[t].wait()
        term = jnp.dot(sh[b, 64 * a : 64 * a + 128], w[t], preferred_element_type=F32)
        if t == 3:
            acc[...] = term
        else:
            acc[...] += term
    hid_ref[...] = acc[...].astype(BF16)
    for copy in inputs[3:]:
        copy.wait()

    def project(ref):
        value = lax.dot_general(hid_ref[...], ref[...], NT, preferred_element_type=F32)
        return value.astype(BF16).astype(F32)

    pack(project(wk_ref), project(wv_ref), 0, 9)
    kept[...] = out_grad

    def queries():
        pack(project(wq_ref) * HD ** -0.5, kept[...], 1, 8)

    def windows(lhs_ref):
        def share_end(s, carry):
            share_copy(s).wait()
            return carry

        def rim_end(s, carry):
            rim_copy(s).wait_send()
            return carry

        lax.fori_loop(1, 16, share_end, 0)
        rim_copy(0).wait_recv()

        @pl.when(rim)
        def _():
            lax.fori_loop(0, 16, rim_end, 0)

        col = lax.broadcasted_iota(jnp.int32, (32, 128), 1)
        near_side = col < 64
        col = lax.rem(col, 64)

        def one(q, carry):
            lanes = pl.ds(pl.multiple_of(lax.rem(q, 2) * 128, 128), 128)
            for c in range(2):
                here = share[q + 1, c].astype(F32)
                turn = pltpu.roll(here, 64, axis=1)
                above = jnp.where(near_side, pltpu.roll(share[q, c].astype(F32), 64, axis=1), turn)
                below = jnp.where(near_side, turn, pltpu.roll(share[q + 2, c].astype(F32), 64, axis=1))
                for a, value in enumerate((above, here, below)):
                    three = (
                        jnp.where(col == 0, 0.0, pltpu.roll(value, 1, axis=1)),
                        value,
                        jnp.where(col == 63, 0.0, pltpu.roll(value, 127, axis=1)),
                    )
                    for b in range(3):
                        row = 288 * c + 32 * (3 * a + b)
                        lhs_ref[q // 2, row : row + 32, lanes] = three[b].astype(BF16)
            return carry

        lax.fori_loop(0, 16, one, 0)

    return windows, queries


def finish_kernel(parts_ref, both_ref, wq_ref, wk_ref, wv_ref, lhs_ref, w, out_ref, taps_ref, lat_ref,
                  gh, halo, sh, acc, prod, small, turned, xs, half, ra, rb, rc, rd,
                  plane, xin, xsum, zin, zfull, pfull, tb, tin, tfull, halo_s, halo_r, up_s, down_s, sib_s, own_r, sib_r,
                  pair_s, pair_r, y_s, y_r, x_s, x_r, z_s, z_r, zb_s, zb_r, xb_s, xb_r, yb_s, yb_r, fin_s, fin_r,
                  t_s, t_r, u_s, u_r):
    dp, xlo, z, core = place()
    p = lax.axis_index("patch")
    xhi, y = dp // 4, lax.rem(dp, 4)
    x = xhi * 2 + xlo
    sib = (dp, xlo * 16 + z * 2 + 1 - core)

    def at_z(s):
        other = lax.rem(z + s + 8, 8)
        return other, (dp, xlo * 16 + other * 2 + core)

    def at_y(s):
        other = lax.rem(y + s + 4, 4)
        return other, (xhi * 4 + other, p)

    def at_x(s):
        other = lax.rem(x + s + 4, 4)
        return other, (other // 2 * 4 + y, lax.rem(other, 2) * 16 + z * 2 + core)

    spot = dp * 2 + xlo

    def at_spot(s):
        other = lax.rem(spot + s, 16)
        return other, (other // 2, lax.rem(other, 2) * 16 + z * 2 + core)

    def at_dp(s):
        other = lax.rem(dp + s, 8)
        return other, (other, p)

    def at_p(s):
        return (dp, lax.rem(p + s + 32, 32))

    mine = pl.ds(pl.multiple_of(core * 128, 128), 128)
    sent = []

    value = both_ref[1].astype(F32)
    for t, ref in ((1, wq_ref), (2, wk_ref), (3, wv_ref)):
        value = value + jnp.dot(parts_ref[t, :, 0:AW], ref[...], preferred_element_type=F32)
    gh[z, mine, :] = value.astype(BF16)

    ways = {"up": (up_s, at_z(1)[1]), "down": (down_s, at_z(-1)[1]), "sib": (sib_s, sib)}
    count = {way: 0 for way in ways}
    low = pl.ds(pl.multiple_of(core * 128, 64), 64)
    high = pl.ds(pl.multiple_of(core * 128 + 64, 64), 64)

    def block(dz):
        return lax.rem(z + dz + 8, 8)

    def ship(dz, way, i):
        u = block(dz)
        sem, device = ways[way]
        if way == "sib":
            ref, recv = gh.at[u, mine, :], sib_r.at[u]
        else:
            ref, recv = gh.at[u, (low, high)[i], :], own_r.at[2 * u + i]
        sent.append(send(ref, ref, sem.at[count[way]], recv, device))
        count[way] += 1

    def arrive(dz):
        u = block(dz)
        for i in range(2):
            ref = gh.at[u, (low, high)[i], :]
            remote(ref, ref, up_s.at[0], own_r.at[2 * u + i], sib).wait_recv()
        ship(dz, "sib", 0)

    def arrive_both(dz):
        for i in range(2):
            for d, way in ((-dz, "up"), (dz, "down")):
                u = block(d)
                ref = gh.at[u, (low, high)[i], :]
                remote(ref, ref, up_s.at[0], own_r.at[2 * u + i], sib).wait_recv()
                if dz < 3 or i == (0 if way == "up" else 1):
                    ship(d, way, i)
        ship(-dz, "sib", 0)
        ship(dz, "sib", 0)

    edge = gh.at[z]
    near = [
        send(edge.at[high, :], halo.at[0], halo_s.at[0], halo_r.at[0], at_p(1)),
        send(edge.at[low, :], halo.at[1], halo_s.at[1], halo_r.at[1], at_p(-1)),
    ]
    for i in range(2):
        ship(0, "up", i)
        ship(0, "down", i)
    ship(0, "sib", 0)

    first_at, second_at = (at_y, at_x), (at_x, at_y)
    first_index, second_index = (y, x), (x, y)
    halves = range(2)

    def part(c, h, k):
        return pl.ds(pl.multiple_of(c * 640 + h * 320 + k * 80, 16), 80)

    def low_of(c, h, k):
        return pl.ds(pl.multiple_of(c * 640 + h * 320 + k * 80, 16), 48)

    def high_of(c, h, k):
        return pl.ds(pl.multiple_of(c * 640 + h * 320 + k * 80 + 48, 16), 32)

    pair = []
    for i in range(4):
        k = lax.rem(2 * (1 - core) + i, 4)
        t = lax.rem(k + 1, 4)
        turned[...] = parts_ref[t].astype(F32).T.astype(BF16)
        r = pl.ds(pl.multiple_of(k * AW, 16), AW)
        right = both_ref[jnp.where(t == 0, 1, 0)]
        xs[r] = jnp.dot(turned[0:AW], right, preferred_element_type=F32).astype(BF16)
        if i < 2:
            pair.append(send(xs.at[r], half.at[pl.ds(320 * i, 320)], pair_s.at[i], pair_r.at[i], sib))
    arrive_both(1)

    for copy in near:
        copy.wait()
    j = lax.broadcasted_iota(jnp.int32, (64, 640), 0)
    rows = (
        jnp.where(p > 0, halo[0].astype(F32), 0.0),
        gh[z, low, :].astype(F32),
        gh[z, high, :].astype(F32),
        jnp.where(p < 31, halo[1].astype(F32), 0.0),
    )
    for r in range(4):
        moved = shifted(rows[r], j)
        for b in range(3):
            sh[2 - b, 64 * r : 64 * r + 64] = moved[b].astype(BF16)

    def tap(t):
        a, b = t // 3, t % 3
        start = 64 * (2 - a)
        term = lax.dot_general(sh[b, start : start + 128], w[t], NT, preferred_element_type=F32)
        if t:
            acc[...] += term
        else:
            acc[...] = term

    def gain(dz, start=False):
        u = block(dz)
        ref = gh.at[u, pl.ds(pl.multiple_of((1 - core) * 128, 128), 128), :]
        remote(ref, ref, up_s.at[0], sib_r.at[u], sib).wait_recv()
        term = jnp.dot(lhs_ref[u], gh[u], preferred_element_type=F32)
        if start:
            prod[...] = term
        else:
            prod[...] += term

    tap(0)
    for copy in pair:
        copy.wait()
    for h in halves:
        mine_rows = pl.ds(pl.multiple_of(core * 640 + h * 320, 16), 320)
        r = slice(320 * h, 320 * h + 320)
        half[r] = (half[r].astype(F32) + xs[mine_rows].astype(F32)).astype(BF16)
    up, down, far = [], [], []
    for h in halves:
        up.append(first_at[h](1))
        down.append(first_at[h](-1))
        far.append(lax.rem(first_index[h] + 2, 4))
        sent.append(send(half.at[low_of(0, h, far[h])], ra.at[h], y_s.at[h, 0], y_r.at[h, 0], up[h][1]))
        sent.append(send(half.at[high_of(0, h, far[h])], rb.at[h], y_s.at[h, 1], y_r.at[h, 1], down[h][1]))
    tap(1)
    arrive_both(2)
    for h in halves:
        remote(half.at[low_of(0, h, 0)], ra.at[h], y_s.at[h, 0], y_r.at[h, 0], sib).wait_recv()
        remote(half.at[high_of(0, h, 0)], rb.at[h], y_s.at[h, 1], y_r.at[h, 1], sib).wait_recv()
        r = low_of(0, h, up[h][0])
        half[r] = (half[r].astype(F32) + ra[h].astype(F32)).astype(BF16)
        r = high_of(0, h, down[h][0])
        half[r] = (half[r].astype(F32) + rb[h].astype(F32)).astype(BF16)
        sent.append(send(half.at[part(0, h, up[h][0])], rc.at[h], y_s.at[h, 2], y_r.at[h, 2], up[h][1]))
        sent.append(send(half.at[part(0, h, down[h][0])], rd.at[h], y_s.at[h, 3], y_r.at[h, 3], down[h][1]))
    tap(2)
    gain(0, True)
    arrive_both(3)
    gain(-1)
    def quarter(k):
        return pl.ds(pl.multiple_of(k * 128, 128), 128)

    def slot(k):
        return pl.ds(pl.multiple_of(k * 16, 16), 16)

    crossing = []
    for h in halves:
        remote(half.at[part(0, h, 0)], rc.at[h], y_s.at[h, 2], y_r.at[h, 2], sib).wait_recv()
        remote(half.at[part(0, h, 0)], rd.at[h], y_s.at[h, 3], y_r.at[h, 3], sib).wait_recv()
        whole = half[part(0, h, first_index[h])].astype(F32) + rc[h].astype(F32) + rd[h].astype(F32)
        for n in range(5):
            plane[h, 80 * n : 80 * n + 80] = whole[:, 128 * n : 128 * n + 128].astype(BF16)
        plane[h, 400:512] = jnp.zeros((112, 128), BF16)
        for s in range(1, 4):
            other, device = second_at[h](s)
            crossing.append(send(plane.at[h, quarter(other)], xin.at[h, s], x_s.at[h, s], x_r.at[h, s], device))
    gain(1)
    arrive(4)
    for copy in crossing:
        copy.wait()
    for h in halves:
        whole = plane[h, quarter(second_index[h])].astype(F32)
        for s in range(1, 4):
            whole = whole + xin[h, s].astype(F32)
        xsum[h] = whole.astype(BF16)
    along = []
    for s in range(1, 8):
        other, device = at_z(s)
        along.append(send(xsum.at[:, slot(other), :], zin.at[s], z_s.at[s], z_r.at[s], device))
    gain(-2)
    whole = xsum[:, slot(z), :].astype(F32)
    for s in range(1, 8):
        along[s - 1].wait()
        whole = whole + zin[s].astype(F32)
    zfull[:, slot(z), :] = whole.astype(BF16)
    zback = []
    for s in range(1, 8):
        ref = zfull.at[:, slot(z), :]
        zback.append(send(ref, ref, zb_s.at[s], zb_r.at[s], at_z(s)[1]))
    gain(2)
    for copy in zback:
        copy.wait()
    xback = []
    for h in halves:
        pfull[h, quarter(second_index[h])] = zfull[h]
        for s in range(1, 4):
            ref = pfull.at[h, quarter(second_index[h])]
            xback.append(send(ref, ref, xb_s.at[h, s], xb_r.at[h, s], second_at[h](s)[1]))
    gain(-3)
    gain(3)
    for copy in xback:
        copy.wait()
    fin = []
    for h in halves:
        for n in range(5):
            out_ref[part(core, h, first_index[h]), 128 * n : 128 * n + 128] = pfull[h, 80 * n : 80 * n + 80]

    def forward(rows, send_sem, recv_sem, device):
        return send(out_ref.at[rows], out_ref.at[rows], send_sem, recv_sem, device)

    def landed(rows, h, i):
        remote(out_ref.at[rows], out_ref.at[rows], yb_s.at[h, i], yb_r.at[h, i], sib).wait_recv()

    for h in halves:
        rows = part(core, h, first_index[h])
        sent.append(forward(rows, yb_s.at[h, 0], yb_r.at[h, 0], up[h][1]))
        sent.append(forward(rows, yb_s.at[h, 1], yb_r.at[h, 1], down[h][1]))
        fin.append(forward(rows, fin_s.at[h, 0], fin_r.at[h, 0], sib))
    gain(4)

    places = [(n, i, 192 * n + 16 * i) for n in range(5) for i in range(12)]
    small[180:192] = jnp.zeros((12, 640), F32)
    for c in range(2):
        for t in range(9):
            small[20 * t : 20 * t + 20] = prod[288 * c + 32 * t : 288 * c + 32 * t + 20]
        for n, i, f in places:
            piece = small[16 * i : 16 * i + 16, 128 * n : 128 * n + 128].astype(BF16)
            tb[c, f // 128, f % 128 : f % 128 + 16] = piece
        tb[c, 7, 64:128] = jnp.zeros((64, 128), BF16)
    there = []
    for s in range(1, 16):
        other, device = at_spot(s)
        there.append(send(tb.at[lax.rem(other, 2), other // 2], tin.at[s], t_s.at[s], t_r.at[s], device))
    tap(3)
    for h in halves:
        landed(part(core, h, down[h][0]), h, 0)
        landed(part(core, h, up[h][0]), h, 1)
        sent.append(forward(low_of(core, h, down[h][0]), yb_s.at[h, 2], yb_r.at[h, 2], up[h][1]))
        sent.append(forward(high_of(core, h, up[h][0]), yb_s.at[h, 3], yb_r.at[h, 3], down[h][1]))
        fin.append(forward(part(core, h, down[h][0]), fin_s.at[h, 1], fin_r.at[h, 1], sib))
        fin.append(forward(part(core, h, up[h][0]), fin_s.at[h, 2], fin_r.at[h, 2], sib))
    tap(4)
    tap(5)
    for h in halves:
        landed(low_of(core, h, far[h]), h, 2)
        landed(high_of(core, h, far[h]), h, 3)
        fin.append(forward(part(core, h, far[h]), fin_s.at[h, 3], fin_r.at[h, 3], sib))
    tap(6)
    whole = tb[xlo, dp].astype(F32)
    for s in range(1, 16):
        there[s - 1].wait()
        whole = whole + tin[s].astype(F32)
    tfull[dp] = whole.astype(BF16)
    tback = []
    for s in range(1, 8):
        ref = tfull.at[dp]
        tback.append(send(ref, ref, u_s.at[s], u_r.at[s], at_dp(s)[1]))
    tap(7)
    tap(8)
    lat_ref[...] = acc[...].astype(BF16)
    for copy in tback:
        copy.wait()
    for n, i, f in places:
        small[16 * i : 16 * i + 16, 128 * n : 128 * n + 128] = tfull[f // 128, f % 128 : f % 128 + 16].astype(F32)
    for t in range(9):
        taps_ref[t] = small[20 * t : 20 * t + 20]
    for copy in fin:
        copy.wait()
    for copy in sent:
        copy.wait_send()


ATTEND = 52


def whole_kernel(*refs):
    hbm, (rows_ref, taps_ref, lat_ref), scratch = refs[:7], refs[7:10], refs[10:]
    shared, scratch = scratch[:10], scratch[10:]
    latent, wq, wk, wv, wo, w, both, packed, lhs, parts = shared
    hidden, cot = both.at[0], both.at[1]
    one, two, three = scratch[:16], scratch[16 : 16 + ATTEND], scratch[16 + ATTEND :]
    windows, queries = first_kernel(hbm, latent, cot, wq, wk, wv, wo, w, hidden, packed, *one)
    attend_kernel(windows, queries, lhs, packed, parts, *two)
    finish_kernel(parts, both, wq, wk, wv, lhs, w, rows_ref, taps_ref, lat_ref, *three)


def whole(*args):
    dma = pltpu.SemaphoreType.DMA
    vmem = pl.BlockSpec(memory_space=pltpu.VMEM)

    def b16(*shape):
        return pltpu.VMEM(shape, BF16)

    def f32(*shape):
        return pltpu.VMEM(shape, F32)

    shared = [
        b16(128, 640), b16(320, 640), b16(320, 640), b16(320, 640), b16(320, 640),
        b16(9, 640, 640), b16(2, 128, 640), b16(10, 128, 128), b16(8, 576, 256), b16(4, 128, 384),
    ]
    one = [
        dma((6,)), dma((9,)), b16(2, 64, 640), f32(656, 128), b16(16, 2, 32, 128), b16(18, 2, 32, 128),
        b16(3, 256, 640), f32(128, 640), f32(2, 128, 128), f32(128, 320),
        dma((2,)), dma((2,)), dma((16,)), dma((16,)), dma((16,)), dma((1,)),
    ]
    two = [
        b16(8, 640, 128), b16(8, 128, 640), b16(2, 512, 128), b16(512, 128), b16(512, 128), b16(512, 128), b16(512, 128),
        f32(64, 512), f32(64, 512),
        f32(8, 640, 512), f32(640, 512), b16(640, 512), b16(640, 512),
        f32(1, 512), f32(1, 512), f32(64, 512), f32(1, 512), f32(64, 512),
        f32(1, 512), f32(1, 512), f32(64, 512), f32(1, 512), f32(64, 512),
        f32(640, 128), b16(4, 640, 128), b16(4, 640, 128), b16(4, 640, 128), b16(4, 640, 128),
        f32(4, 72, 128), f32(4, 72, 128), f32(4, 8, 128), f32(128, 128), b16(3, 512, 128), b16(4, 3, 128, 128),
        dma((4,)), dma((4,)), dma((2, 4)), dma((2, 4)),
        dma((4, 2)), dma((4, 2)), dma((4, 2)), dma((4, 2)), dma((4, 2)), dma((4, 2)), dma((4, 2)), dma((4, 2)),
        dma((4,)), dma((4,)), dma((4,)), dma((4,)), dma((3, 4)), dma((3, 4)),
    ]
    three = [
        b16(8, 256, 640), b16(2, 64, 640), b16(3, 256, 640), f32(128, 640),
        f32(576, 640), f32(192, 640), b16(384, 128),
        b16(1280, 640), b16(640, 640), b16(2, 48, 640), b16(2, 32, 640), b16(2, 80, 640), b16(2, 80, 640),
        b16(2, 512, 128), b16(2, 4, 128, 128), b16(2, 128, 128), b16(8, 2, 16, 128), b16(2, 128, 128), b16(2, 512, 128),
        b16(2, 8, 128, 128), b16(16, 128, 128), b16(8, 128, 128),
        dma((2,)), dma((2,)), dma((7,)), dma((7,)), dma((8,)), dma((16,)), dma((8,)),
        dma((2,)), dma((2,)), dma((2, 4)), dma((2, 4)), dma((2, 4)), dma((2, 4)), dma((8,)), dma((8,)),
        dma((8,)), dma((8,)), dma((2, 4)), dma((2, 4)), dma((2, 4)), dma((2, 4)), dma((2, 4)), dma((2, 4)),
        dma((16,)), dma((16,)), dma((8,)), dma((8,)),
    ]
    return pl.pallas_call(
        whole_kernel,
        out_shape=(
            jax.ShapeDtypeStruct((1280, 640), BF16),
            jax.ShapeDtypeStruct((9, 20, 640), F32),
            jax.ShapeDtypeStruct((128, 640), BF16),
        ),
        in_specs=[pl.BlockSpec(memory_space=pl.ANY)] * 7,
        out_specs=(vmem,) * 3,
        scratch_shapes=shared + one + two + three,
        compiler_params=pltpu.CompilerParams(
            collective_id=0, has_side_effects=True, vmem_limit_bytes=60 * 1024 * 1024
        ),
        name="whole",
    )(*args)


def hand_kernel(rows_ref, taps_ref, lat_ref, taps_out, lat_out, *rest):
    outs, (rows, wide, taps, lat, in_sem, out_sem) = rest[:4], rest[4:]
    loads = [
        pltpu.make_async_copy(rows_ref.at[AW * i : AW * i + AW], rows.at[i], in_sem.at[i]) for i in range(4)
    ]
    loads.append(pltpu.make_async_copy(taps_ref, taps, in_sem.at[4]))
    loads.append(pltpu.make_async_copy(lat_ref, lat, in_sem.at[5]))
    for copy in loads:
        copy.start()
    stores = []
    for i in range(6):
        loads[i].wait()
        if i < 4:
            wide[i] = rows[i].astype(F32)
            copy = pltpu.make_async_copy(wide.at[i], outs[i], out_sem.at[i])
        elif i == 4:
            copy = pltpu.make_async_copy(taps, taps_out, out_sem.at[i])
        else:
            copy = pltpu.make_async_copy(lat, lat_out, out_sem.at[i])
        copy.start()
        stores.append(copy)
    for copy in stores:
        copy.wait()


def hand_out(rows, taps, grad_latent):
    anywhere = pl.BlockSpec(memory_space=pl.ANY)
    return pl.pallas_call(
        hand_kernel,
        out_shape=(
            jax.ShapeDtypeStruct(taps.shape, F32),
            jax.ShapeDtypeStruct(grad_latent.shape, BF16),
        )
        + (jax.ShapeDtypeStruct((AW, 640), F32),) * 4,
        in_specs=[anywhere] * 3,
        out_specs=(anywhere,) * 6,
        scratch_shapes=[
            pltpu.VMEM((4, AW, 640), BF16),
            pltpu.VMEM((4, AW, 640), F32),
            pltpu.VMEM(taps.shape, F32),
            pltpu.VMEM(grad_latent.shape, BF16),
            pltpu.SemaphoreType.DMA((6,)),
            pltpu.SemaphoreType.DMA((6,)),
        ],
        compiler_params=pltpu.CompilerParams(vmem_limit_bytes=60 * 1024 * 1024),
        name="hand_out",
    )(rows, taps, grad_latent)


def body(latent, cotangent, conv_weight, query_weight, key_weight, value_weight, out_weight):
    sums = whole(
        latent.reshape(128, 640), cotangent.reshape(128, 640), out_weight, key_weight.T, value_weight.T,
        query_weight.T, conv_weight.reshape(9, 640, 640),
    )
    taps, grad_latent, query, key, value, out = hand_out(*sums)
    return (grad_latent.reshape(latent.shape), taps.reshape(3, 3, 20, 640), query.T, key.T, value.T, out)


def solution(mesh):
    placed = (P("dp", "patch", None, None), P("dp", "patch", None, None), P(), P(), P(), P(), P())
    return jax.shard_map(
        body,
        mesh=mesh,
        in_specs=placed,
        out_specs=(P("dp", "patch", None, None), P(None, None, "patch", None), P(), P(), P(), P()),
        check_vma=False,
    )
```

```python
import functools
import jax
import jax.numpy as jnp
from jax import lax
from jax.experimental import pallas as pl
from jax.experimental.pallas import tpu as pltpu
from jax.sharding import PartitionSpec as P

NH = 5
HD = 64
AW = 320
MESH = pl.DeviceIdType.MESH
F32 = jnp.float32
BF16 = jnp.bfloat16


def place():
    p = lax.axis_index("patch")
    return lax.axis_index("dp"), p // 16, lax.rem(p, 16) // 2, lax.rem(p, 2)


def send(src, dst, send_sem, recv_sem, device):
    copy = pltpu.make_async_remote_copy(
        src_ref=src, dst_ref=dst, send_sem=send_sem, recv_sem=recv_sem,
        device_id=device, device_id_type=MESH,
    )
    copy.start()
    return copy


NT = (((1,), (1,)), ((), ()))
LOG2E = 1.4426950408889634


def remote(src, dst, send_sem, recv_sem, device):
    return pltpu.make_async_remote_copy(
        src_ref=src, dst_ref=dst, send_sem=send_sem, recv_sem=recv_sem,
        device_id=device, device_id_type=MESH,
    )


def attend_kernel(windows, queries, lhs_ref, x_ref, out_ref, kv, kvt, qd, qs, gs, q4, g4, gt, gt4, scores, slope, pb, sb,
                  top, low, att, delta, dq, top4, low4, att4, delta4, dq4, part, box_up, box_down, ahead, behind,
                  mix, mix_in, stat, own4, stage, res,
                  kv_s, kv_r, qd_s, qd_r, up_s, up_r, down_s, down_r, rup_s, rup_r, rdown_s, rdown_r,
                  mix_s, mix_r, stat_s, stat_r, g_s, g_r):
    dp, xlo, z, core = place()
    j = xlo * 2 + core

    def at_z(step):
        return (dp, xlo * 16 + lax.rem(z + step + 8, 8) * 2 + core)

    def in_quad(step):
        m = lax.rem(j + step, 4)
        return m, (dp, (m // 2) * 16 + z * 2 + lax.rem(m, 2))

    def rows(m):
        return pl.ds(pl.multiple_of(m * 128, 128), 128)

    first, second = [], []
    for s in range(1, 4):
        m, device = in_quad(s)
        first.append(send(x_ref.at[2 * m], kv.at[z, rows(j), :], kv_s.at[s], kv_r.at[s], device))
    queries()
    for s in range(1, 4):
        m, device = in_quad(s)
        second.append(send(x_ref.at[2 * m + 1], qd.at[0, rows(j), :], qd_s.at[0, s], qd_r.at[0, s], device))
        second.append(send(x_ref.at[8], qd.at[1, rows(j), :], qd_s.at[1, s], qd_r.at[1, s], device))
    kv[z, rows(j), :] = x_ref[2 * j]
    kv[z, 512:640] = x_ref[9]
    qd[0, rows(j), :] = x_ref[2 * j + 1]
    qd[1, rows(j), :] = x_ref[8]
    lane = lax.broadcasted_iota(jnp.int32, (128, 128), 1)
    left = lane < 64
    for ref in (top, top4):
        ref[...] = jnp.full(ref.shape, -jnp.inf, F32)
    for ref in (low, low4, att, att4, dq, dq4):
        ref[...] = jnp.zeros(ref.shape, F32)

    cuts = (slice(0, 320), slice(320, 640))

    def ring_up(s, i):
        ref = kv.at[lax.rem(z + 8 - s, 8), cuts[i]]
        return remote(ref, ref, up_s.at[s, i], up_r.at[s, i], at_z(1))

    def ring_down(s, i):
        ref = kv.at[lax.rem(z + s, 8), cuts[i]]
        return remote(ref, ref, down_s.at[s, i], down_r.at[s, i], at_z(-1))

    for copy in first:
        copy.wait()
    for i in range(2):
        ring_up(0, i).start()
        ring_down(0, i).start()
    windows(lhs_ref)
    for copy in second:
        copy.wait()
    for m in range(4):
        r = slice(m * 128, m * 128 + 128)
        for i, (a, b, bt) in enumerate(((qs, gs, gt), (q4, g4, gt4))):
            pair = qd[i, r].astype(F32)
            a[r] = jnp.where(left, pair, 0.0).astype(BF16)
            b[r] = jnp.where(left, 0.0, pair).astype(BF16)
            bt[:, r] = pair.T[64:128]

    def soften(b, keys, q, top, low, att):
        s = scores[b, keys, q]
        old = top[:, q]
        new = jnp.maximum(old, jnp.max(s, axis=0, keepdims=True))
        p = jnp.exp2(s - new)
        fade = jnp.exp2(old - new)
        low[:, q] = low[:, q] * fade + jnp.sum(p, axis=0, keepdims=True)
        top[:, q] = new
        att[:, q] = att[:, q] * fade
        pb[keys, q] = p.astype(BF16)

    main, side = slice(0, 512), slice(512, 640)
    quarters = [slice(128 * i, 128 * i + 128) for i in range(4)]

    def pass_one(t, carry):
        for s in range(3):
            @pl.when(t == 2 * s + 1)
            def _():
                for i in range(2):
                    ring_up(s, i).wait_recv()
                    if s < 2 or i == 0:
                        ring_up(s + 1, i).start()
                    ring_down(s, i).wait_recv()
                    if s < 2 or i == 1:
                        ring_down(s + 1, i).start()

        @pl.when(t == 7)
        def _():
            ring_up(3, 0).wait_recv()
            ring_down(3, 1).wait_recv()

        offset = jnp.where(lax.rem(t, 2) == 1, 8 - (t + 1) // 2, t // 2)
        b = lax.rem(z + offset, 8)
        scores[b, main] = lax.dot_general(kv[b, main], qs[...], NT, preferred_element_type=F32) * LOG2E
        scores[b, side] = lax.dot_general(kv[b, side], q4[...], NT, preferred_element_type=F32) * LOG2E
        for i in range(5):
            c = slice(128 * i, 128 * i + 128)
            kvt[b, :, c] = kv[b, c].astype(F32).T.astype(BF16)
        for q in quarters:
            soften(b, main, q, top, low, att)
            soften(b, side, q, top4, low4, att4)
        att[...] += jnp.dot(kvt[b, 64:128, main], pb[main], preferred_element_type=F32)
        att4[...] += jnp.dot(kvt[b, 64:128, side], pb[side], preferred_element_type=F32)
        return carry

    lax.fori_loop(0, 8, pass_one, 0)
    for m in range(4):
        q = quarters[m]
        mix[m, 0:64] = att4[:, q]
        mix[m, 64:65] = top4[:, q]
        mix[m, 65:66] = low4[:, q]
        mix[m, 66:72] = jnp.zeros((6, 128), F32)
    mixing = []
    for s in range(1, 4):
        m, device = in_quad(s)
        mixing.append(send(mix.at[m], mix_in.at[s], mix_s.at[s], mix_r.at[s], device))
    mix_in[0] = mix[j]
    att[...] = att[...] / low[...]
    top[...] = top[...] + jnp.log2(low[...])
    delta[...] = jnp.sum(att[...] * gt[...], axis=0, keepdims=True)

    def stat_copy(s):
        return remote(stat.at[j], stat.at[j], stat_s.at[s], stat_r.at[s], in_quad(s)[1])

    late = []
    for q in quarters:
        stage[1, q] = jnp.concatenate([att[:, q], jnp.zeros((64, 128), F32)], axis=0).T.astype(BF16)
    for s in range(1, 4):
        m, device = in_quad(s)
        late.append(send(stage.at[1, rows(m), :], res.at[j, 1], g_s.at[2, s], g_r.at[2, s], device))
    def sum_up(s, i):
        return remote(box_up.at[s, cuts[i]], ahead.at[s, cuts[i]], rup_s.at[s, i], rup_r.at[s, i], at_z(1))

    def sum_down(s, i):
        return remote(
            box_down.at[s, cuts[i]], behind.at[s, cuts[i]], rdown_s.at[s, i], rdown_r.at[s, i], at_z(-1)
        )

    def pass_on(box, landed, step, s, i):
        c = cuts[i]
        step(s, i).wait_recv()
        box[s + 1, c] = (part[c] + landed[s, c].astype(F32)).astype(BF16)
        step(s + 1, i).start()

    def slopes(b, keys, q, top, delta):
        p = jnp.exp2(scores[b, keys, q] - top[:, q])
        pb[keys, q] = p.astype(BF16)
        sb[keys, q] = (p * (slope[keys, q] - delta[:, q])).astype(BF16)

    def merge():
        for copy in mixing:
            copy.wait()
        tops = [mix_in[s, 64:65] for s in range(4)]
        best = jnp.maximum(jnp.maximum(tops[0], tops[1]), jnp.maximum(tops[2], tops[3]))
        total, blend = jnp.zeros((1, 128), F32), jnp.zeros((64, 128), F32)
        for s in range(4):
            weight = jnp.exp2(tops[s] - best)
            total = total + mix_in[s, 65:66] * weight
            blend = blend + mix_in[s, 0:64] * weight
        blend = blend / total
        own4[0:64] = blend
        own4[64:128] = jnp.zeros((64, 128), F32)
        stat[j, 0:1] = best + jnp.log2(total)
        stat[j, 1:2] = jnp.sum(blend * gt4[:, rows(j)], axis=0, keepdims=True)
        stat[j, 2:8] = jnp.zeros((6, 128), F32)
        for s in range(1, 4):
            stat_copy(s).start()

    def main_part(b):
        slope[main] = lax.dot_general(kv[b, main], gs[...], NT, preferred_element_type=F32)
        for q in quarters:
            slopes(b, main, q, top, delta)
        part[main] = jnp.dot(sb[main], qs[...], preferred_element_type=F32) + jnp.dot(
            pb[main], gs[...], preferred_element_type=F32
        )

    def main_dq(b):
        dq[...] += jnp.dot(kvt[b, 0:64, main], sb[main], preferred_element_type=F32)

    def side_part(b):
        slope[side] = lax.dot_general(kv[b, side], g4[...], NT, preferred_element_type=F32)
        for q in quarters:
            slopes(b, side, q, top4, delta4)
        part[side] = jnp.dot(sb[side], q4[...], preferred_element_type=F32) + jnp.dot(
            pb[side], g4[...], preferred_element_type=F32
        )

    def side_dq(b):
        dq4[...] += jnp.dot(kvt[b, 0:64, side], sb[side], preferred_element_type=F32)

    edge = lax.rem(z + 4, 8)
    main_part(edge)
    box_up[0, cuts[0]] = part[cuts[0]].astype(BF16)
    sum_up(0, 0).start()
    box_down[0, 320:512] = part[320:512].astype(BF16)
    main_dq(edge)
    merge()

    def pass_two(t, carry):
        offset = jnp.where(lax.rem(t, 2) == 0, 4 + t // 2, 4 - (t + 1) // 2)
        b = lax.rem(z + offset, 8)
        main_part(b)

        @pl.when(t == 1)
        def _():
            for s in range(1, 4):
                stat_copy(s).wait()
            for m in range(4):
                top4[:, quarters[m]] = stat[m, 0:1]
                delta4[:, quarters[m]] = stat[m, 1:2]
            side_part(edge)
            box_down[0, side] = part[side].astype(BF16)
            sum_down(0, 1).start()
            side_dq(edge)

        side_part(b)

        @pl.when(t == 1)
        def _():
            box_up[1, cuts[1]] = part[cuts[1]].astype(BF16)
            sum_up(1, 1).start()
            pass_on(box_up, ahead, sum_up, 0, 0)

        @pl.when(t == 2)
        def _():
            box_down[1, cuts[0]] = part[cuts[0]].astype(BF16)
            sum_down(1, 0).start()
            pass_on(box_down, behind, sum_down, 0, 1)

        for s in range(1, 3):
            @pl.when(t == 2 * s + 1)
            def _():
                pass_on(box_up, ahead, sum_up, s, 1)
                pass_on(box_up, ahead, sum_up, s, 0)

            @pl.when(t == 2 * s + 2)
            def _():
                pass_on(box_down, behind, sum_down, s, 0)
                pass_on(box_down, behind, sum_down, s, 1)

        main_dq(b)
        side_dq(b)
        return carry

    lax.fori_loop(1, 8, pass_two, 0)
    for q in quarters:
        both = jnp.concatenate([dq[:, q], dq4[:, q]], axis=0) * HD ** -0.5
        stage[0, q] = both.T.astype(BF16)
    for s in range(1, 4):
        m, device = in_quad(s)
        late.append(send(stage.at[0, rows(m), :], res.at[j, 0], g_s.at[0, s], g_r.at[0, s], device))
    for i in range(2):
        sum_up(3, i).wait_recv()
        sum_down(3, i).wait_recv()
    stage[2] = (part[main] + ahead[3, main].astype(F32) + behind[3, main].astype(F32)).astype(BF16)
    for s in range(1, 4):
        m, device = in_quad(s)
        late.append(send(stage.at[2, rows(m), :], res.at[j, 2], g_s.at[1, s], g_r.at[1, s], device))
    own = part[side] + ahead[3, side].astype(F32) + behind[3, side].astype(F32)
    for t in range(3):
        res[j, t] = stage[t, rows(j), :]
    for s in range(4):
        for i in range(2):
            if s < 3 or i == 0:
                ring_up(s, i).wait_send()
            if s < 3 or i == 1:
                ring_down(s, i).wait_send()
            if s > 0 or i == 0:
                sum_up(s, i).wait_send()
            if s > 0 or i == 1:
                sum_down(s, i).wait_send()
    for copy in late:
        copy.wait()

    def swap(a):
        return pltpu.roll(a, 64, axis=1)

    for t, source, high in ((0, 1, False), (1, 0, False), (2, 2, False), (3, 2, True)):
        for i in range(2):
            a, b = res[2 * i, source].astype(F32), res[2 * i + 1, source].astype(F32)
            pair = jnp.where(left, swap(a), b) if high else jnp.where(left, a, swap(b))
            out_ref[t, :, 128 * i : 128 * i + 128] = pair.astype(BF16)
    last4 = (
        own4[...].T,
        swap(sum(res[m, 0].astype(F32) for m in range(4))),
        own,
        swap(own),
    )
    for t in range(4):
        out_ref[t, :, 256:384] = jnp.where(left, last4[t], 0.0).astype(BF16)


def shifted(rows, j):
    before = jnp.where(j == 0, 0.0, pltpu.roll(rows, 1, axis=0))
    after = jnp.where(j == 63, 0.0, pltpu.roll(rows, 63, axis=0))
    return before, rows, after


def first_kernel(hbm, lat_ref, cot_ref, wq_ref, wk_ref, wv_ref, wo_ref, w, hid_ref, x_ref, load_sem, w_sem,
                 halo, turned, sbuf, share, sh, acc, tmp, kept, halo_s, halo_r, share_s, share_r, rim_s, rim_r):
    dp, xlo, z, core = place()
    p = lax.axis_index("patch")
    spot = dp * 2 + xlo
    index = lax.rem(p, 16)

    def at(step):
        other = lax.rem(p + step + 32, 32)
        return (dp, other)

    local = (lat_ref, cot_ref, wo_ref, wk_ref, wv_ref, wq_ref)
    inputs = []
    for i, ref in enumerate(local):
        copy = pltpu.make_async_copy(hbm[i], ref, load_sem.at[i])
        copy.start()
        inputs.append(copy)
    loads = [pltpu.make_async_copy(hbm[6].at[t], w.at[t], w_sem.at[t]) for t in range(9)]
    for t in (3, 4, 5, 0, 1, 2, 6, 7, 8):
        loads[t].start()
    barrier = pltpu.get_barrier_semaphore()

    def hello(s, carry):
        pl.semaphore_signal(barrier, inc=1, device_id=at(s), device_id_type=MESH)
        return carry

    def hello_plane(s, carry):
        other = lax.rem(spot + s, 16)
        device = (other // 2, lax.rem(other, 2) * 16 + index)
        pl.semaphore_signal(barrier, inc=1, device_id=device, device_id_type=MESH)
        return carry

    lax.fori_loop(1, 32, hello, 0)
    lax.fori_loop(1, 16, hello_plane, 0)
    inputs[0].wait()
    turned[0:640] = lat_ref[...].astype(F32).T
    turned[640:656] = jnp.zeros((16, 128), F32)
    for k in range(32):
        sbuf[k % 16, k // 16] = turned[20 * k : 20 * k + 32].astype(BF16)
    share[jnp.where(xlo == 0, 0, 17)] = jnp.zeros((2, 32, 128), BF16)
    share[index + 1] = sbuf[index]
    pl.semaphore_wait(barrier, 46)
    near = [
        send(lat_ref.at[64:128], halo.at[0], halo_s.at[0], halo_r.at[0], at(1)),
        send(lat_ref.at[0:64], halo.at[1], halo_s.at[1], halo_r.at[1], at(-1)),
    ]

    def share_copy(s):
        other = lax.rem(index + s, 16)
        return remote(sbuf.at[other], share.at[index + 1], share_s.at[s], share_r.at[s], (dp, xlo * 16 + other))

    rim = index == jnp.where(xlo == 0, 15, 0)
    rim_slot = jnp.where(xlo == 0, 0, 17)

    def rim_copy(s):
        return remote(sbuf.at[s], share.at[rim_slot], rim_s.at[s], rim_r.at[0], (dp, (1 - xlo) * 16 + s))

    def share_start(s, carry):
        share_copy(s).start()
        return carry

    def rim_start(s, carry):
        rim_copy(s).start()
        return carry

    lax.fori_loop(1, 16, share_start, 0)

    @pl.when(rim)
    def _():
        lax.fori_loop(0, 16, rim_start, 0)

    lane = lax.broadcasted_iota(jnp.int32, (128, 128), 1)
    left = lane < 64

    def pack(low_value, high_value, first_slot, last_slot):
        for n in range(3):
            c = slice(128 * n, min(128 * n + 128, AW))
            width = c.stop - c.start
            tmp[0, :, 0:width] = low_value[:, c]
            tmp[1, :, 0:width] = high_value[:, c]
            a, b = tmp[0], tmp[1]
            even = jnp.where(left, a, pltpu.roll(b, 64, axis=1)).astype(BF16)
            if n == 2:
                x_ref[last_slot] = even
            else:
                x_ref[4 * n + first_slot] = even
                x_ref[4 * n + 2 + first_slot] = jnp.where(left, pltpu.roll(a, 64, axis=1), b).astype(BF16)

    inputs[1].wait()
    inputs[2].wait()
    out_grad = lax.dot_general(cot_ref[...], wo_ref[...], NT, preferred_element_type=F32)
    tmp[...] = jnp.zeros(tmp.shape, F32)
    j = lax.broadcasted_iota(jnp.int32, (64, 640), 0)

    def lay(r, value):
        for b, moved in enumerate(shifted(value, j)):
            sh[b, 64 * r : 64 * r + 64] = moved.astype(BF16)

    lay(1, lat_ref[0:64].astype(F32))
    lay(2, lat_ref[64:128].astype(F32))
    for t in (3, 4, 5, 0, 1, 2, 6, 7, 8):
        a, b = t // 3, t % 3
        if t == 0:
            for copy in near:
                copy.wait()
            lay(0, jnp.where(p > 0, halo[0].astype(F32), 0.0))
            lay(3, jnp.where(p < 31, halo[1].astype(F32), 0.0))
        loads[t].wait()
        term = jnp.dot(sh[b, 64 * a : 64 * a + 128], w[t], preferred_element_type=F32)
        if t == 3:
            acc[...] = term
        else:
            acc[...] += term
    hid_ref[...] = acc[...].astype(BF16)
    for copy in inputs[3:]:
        copy.wait()

    def project(ref):
        value = lax.dot_general(hid_ref[...], ref[...], NT, preferred_element_type=F32)
        return value.astype(BF16).astype(F32)

    pack(project(wk_ref), project(wv_ref), 0, 9)
    kept[...] = out_grad

    def queries():
        pack(project(wq_ref) * HD ** -0.5, kept[...], 1, 8)

    def windows(lhs_ref):
        def share_end(s, carry):
            share_copy(s).wait()
            return carry

        def rim_end(s, carry):
            rim_copy(s).wait_send()
            return carry

        lax.fori_loop(1, 16, share_end, 0)
        rim_copy(0).wait_recv()

        @pl.when(rim)
        def _():
            lax.fori_loop(0, 16, rim_end, 0)

        col = lax.broadcasted_iota(jnp.int32, (32, 128), 1)
        near_side = col < 64
        col = lax.rem(col, 64)

        def one(q, carry):
            lanes = pl.ds(pl.multiple_of(lax.rem(q, 2) * 128, 128), 128)
            for c in range(2):
                here = share[q + 1, c].astype(F32)
                turn = pltpu.roll(here, 64, axis=1)
                above = jnp.where(near_side, pltpu.roll(share[q, c].astype(F32), 64, axis=1), turn)
                below = jnp.where(near_side, turn, pltpu.roll(share[q + 2, c].astype(F32), 64, axis=1))
                for a, value in enumerate((above, here, below)):
                    three = (
                        jnp.where(col == 0, 0.0, pltpu.roll(value, 1, axis=1)),
                        value,
                        jnp.where(col == 63, 0.0, pltpu.roll(value, 127, axis=1)),
                    )
                    for b in range(3):
                        row = 288 * c + 32 * (3 * a + b)
                        lhs_ref[q // 2, row : row + 32, lanes] = three[b].astype(BF16)
            return carry

        lax.fori_loop(0, 16, one, 0)

    return windows, queries


def finish_kernel(parts_ref, both_ref, wq_ref, wk_ref, wv_ref, lhs_ref, w, out_ref, taps_ref, lat_ref,
                  gh, halo, sh, acc, prod, small, turned, xs, half, ra, rb, rc, rd,
                  plane, xin, xsum, zin, zfull, pfull, tb, tin, tfull, halo_s, halo_r, up_s, down_s, sib_s, own_r, sib_r,
                  pair_s, pair_r, y_s, y_r, x_s, x_r, z_s, z_r, zb_s, zb_r, xb_s, xb_r, yb_s, yb_r, fin_s, fin_r,
                  t_s, t_r, u_s, u_r):
    dp, xlo, z, core = place()
    p = lax.axis_index("patch")
    xhi, y = dp // 4, lax.rem(dp, 4)
    x = xhi * 2 + xlo
    sib = (dp, xlo * 16 + z * 2 + 1 - core)

    def at_z(s):
        other = lax.rem(z + s + 8, 8)
        return other, (dp, xlo * 16 + other * 2 + core)

    def at_y(s):
        other = lax.rem(y + s + 4, 4)
        return other, (xhi * 4 + other, p)

    def at_x(s):
        other = lax.rem(x + s + 4, 4)
        return other, (other // 2 * 4 + y, lax.rem(other, 2) * 16 + z * 2 + core)

    spot = dp * 2 + xlo

    def at_spot(s):
        other = lax.rem(spot + s, 16)
        return other, (other // 2, lax.rem(other, 2) * 16 + z * 2 + core)

    def at_dp(s):
        other = lax.rem(dp + s, 8)
        return other, (other, p)

    def at_p(s):
        return (dp, lax.rem(p + s + 32, 32))

    mine = pl.ds(pl.multiple_of(core * 128, 128), 128)
    sent = []

    value = both_ref[1].astype(F32)
    for t, ref in ((1, wq_ref), (2, wk_ref), (3, wv_ref)):
        value = value + jnp.dot(parts_ref[t, :, 0:AW], ref[...], preferred_element_type=F32)
    gh[z, mine, :] = value.astype(BF16)

    ways = {"up": (up_s, at_z(1)[1]), "down": (down_s, at_z(-1)[1]), "sib": (sib_s, sib)}
    count = {way: 0 for way in ways}
    low = pl.ds(pl.multiple_of(core * 128, 64), 64)
    high = pl.ds(pl.multiple_of(core * 128 + 64, 64), 64)

    def block(dz):
        return lax.rem(z + dz + 8, 8)

    def ship(dz, way, i):
        u = block(dz)
        sem, device = ways[way]
        if way == "sib":
            ref, recv = gh.at[u, mine, :], sib_r.at[u]
        else:
            ref, recv = gh.at[u, (low, high)[i], :], own_r.at[2 * u + i]
        sent.append(send(ref, ref, sem.at[count[way]], recv, device))
        count[way] += 1

    def arrive(dz):
        u = block(dz)
        for i in range(2):
            ref = gh.at[u, (low, high)[i], :]
            remote(ref, ref, up_s.at[0], own_r.at[2 * u + i], sib).wait_recv()
        ship(dz, "sib", 0)

    def arrive_both(dz):
        for i in range(2):
            for d, way in ((-dz, "up"), (dz, "down")):
                u = block(d)
                ref = gh.at[u, (low, high)[i], :]
                remote(ref, ref, up_s.at[0], own_r.at[2 * u + i], sib).wait_recv()
                if dz < 3 or i == (0 if way == "up" else 1):
                    ship(d, way, i)
        ship(-dz, "sib", 0)
        ship(dz, "sib", 0)

    edge = gh.at[z]
    near = [
        send(edge.at[high, :], halo.at[0], halo_s.at[0], halo_r.at[0], at_p(1)),
        send(edge.at[low, :], halo.at[1], halo_s.at[1], halo_r.at[1], at_p(-1)),
    ]
    for i in range(2):
        ship(0, "up", i)
        ship(0, "down", i)
    ship(0, "sib", 0)

    first_at, second_at = (at_y, at_x), (at_x, at_y)
    first_index, second_index = (y, x), (x, y)
    halves = range(2)

    def part(c, h, k):
        return pl.ds(pl.multiple_of(c * 640 + h * 320 + k * 80, 16), 80)

    def low_of(c, h, k):
        return pl.ds(pl.multiple_of(c * 640 + h * 320 + k * 80, 16), 48)

    def high_of(c, h, k):
        return pl.ds(pl.multiple_of(c * 640 + h * 320 + k * 80 + 48, 16), 32)

    pair = []
    for i in range(4):
        k = lax.rem(2 * (1 - core) + i, 4)
        t = lax.rem(k + 1, 4)
        turned[...] = parts_ref[t].astype(F32).T.astype(BF16)
        r = pl.ds(pl.multiple_of(k * AW, 16), AW)
        right = both_ref[jnp.where(t == 0, 1, 0)]
        xs[r] = jnp.dot(turned[0:AW], right, preferred_element_type=F32).astype(BF16)
        if i < 2:
            pair.append(send(xs.at[r], half.at[pl.ds(320 * i, 320)], pair_s.at[i], pair_r.at[i], sib))
    arrive_both(1)

    for copy in near:
        copy.wait()
    j = lax.broadcasted_iota(jnp.int32, (64, 640), 0)
    rows = (
        jnp.where(p > 0, halo[0].astype(F32), 0.0),
        gh[z, low, :].astype(F32),
        gh[z, high, :].astype(F32),
        jnp.where(p < 31, halo[1].astype(F32), 0.0),
    )
    for r in range(4):
        moved = shifted(rows[r], j)
        for b in range(3):
            sh[2 - b, 64 * r : 64 * r + 64] = moved[b].astype(BF16)

    def tap(t):
        a, b = t // 3, t % 3
        start = 64 * (2 - a)
        term = lax.dot_general(sh[b, start : start + 128], w[t], NT, preferred_element_type=F32)
        if t:
            acc[...] += term
        else:
            acc[...] = term

    def gain(dz, start=False):
        u = block(dz)
        ref = gh.at[u, pl.ds(pl.multiple_of((1 - core) * 128, 128), 128), :]
        remote(ref, ref, up_s.at[0], sib_r.at[u], sib).wait_recv()
        term = jnp.dot(lhs_ref[u], gh[u], preferred_element_type=F32)
        if start:
            prod[...] = term
        else:
            prod[...] += term

    tap(0)
    for copy in pair:
        copy.wait()
    for h in halves:
        mine_rows = pl.ds(pl.multiple_of(core * 640 + h * 320, 16), 320)
        r = slice(320 * h, 320 * h + 320)
        half[r] = (half[r].astype(F32) + xs[mine_rows].astype(F32)).astype(BF16)
    up, down, far = [], [], []
    for h in halves:
        up.append(first_at[h](1))
        down.append(first_at[h](-1))
        far.append(lax.rem(first_index[h] + 2, 4))
        sent.append(send(half.at[low_of(0, h, far[h])], ra.at[h], y_s.at[h, 0], y_r.at[h, 0], up[h][1]))
        sent.append(send(half.at[high_of(0, h, far[h])], rb.at[h], y_s.at[h, 1], y_r.at[h, 1], down[h][1]))
    tap(1)
    arrive_both(2)
    for h in halves:
        remote(half.at[low_of(0, h, 0)], ra.at[h], y_s.at[h, 0], y_r.at[h, 0], sib).wait_recv()
        remote(half.at[high_of(0, h, 0)], rb.at[h], y_s.at[h, 1], y_r.at[h, 1], sib).wait_recv()
        r = low_of(0, h, up[h][0])
        half[r] = (half[r].astype(F32) + ra[h].astype(F32)).astype(BF16)
        r = high_of(0, h, down[h][0])
        half[r] = (half[r].astype(F32) + rb[h].astype(F32)).astype(BF16)
        sent.append(send(half.at[part(0, h, up[h][0])], rc.at[h], y_s.at[h, 2], y_r.at[h, 2], up[h][1]))
        sent.append(send(half.at[part(0, h, down[h][0])], rd.at[h], y_s.at[h, 3], y_r.at[h, 3], down[h][1]))
    tap(2)
    gain(0, True)
    arrive_both(3)
    gain(-1)
    def quarter(k):
        return pl.ds(pl.multiple_of(k * 128, 128), 128)

    def slot(k):
        return pl.ds(pl.multiple_of(k * 16, 16), 16)

    crossing = []
    for h in halves:
        remote(half.at[part(0, h, 0)], rc.at[h], y_s.at[h, 2], y_r.at[h, 2], sib).wait_recv()
        remote(half.at[part(0, h, 0)], rd.at[h], y_s.at[h, 3], y_r.at[h, 3], sib).wait_recv()
        whole = half[part(0, h, first_index[h])].astype(F32) + rc[h].astype(F32) + rd[h].astype(F32)
        for n in range(5):
            plane[h, 80 * n : 80 * n + 80] = whole[:, 128 * n : 128 * n + 128].astype(BF16)
        plane[h, 400:512] = jnp.zeros((112, 128), BF16)
        for s in range(1, 4):
            other, device = second_at[h](s)
            crossing.append(send(plane.at[h, quarter(other)], xin.at[h, s], x_s.at[h, s], x_r.at[h, s], device))
    gain(1)
    arrive(4)
    gain(-2)
    gain(2)
    for copy in crossing:
        copy.wait()
    for h in halves:
        whole = plane[h, quarter(second_index[h])].astype(F32)
        for s in range(1, 4):
            whole = whole + xin[h, s].astype(F32)
        xsum[h] = whole.astype(BF16)
    along = []
    for s in range(1, 8):
        other, device = at_z(s)
        along.append(send(xsum.at[:, slot(other), :], zin.at[s], z_s.at[s], z_r.at[s], device))
    gain(-3)
    gain(3)
    gain(4)
    whole = xsum[:, slot(z), :].astype(F32)
    for s in range(1, 8):
        along[s - 1].wait()
        whole = whole + zin[s].astype(F32)
    zfull[:, slot(z), :] = whole.astype(BF16)
    zback = []
    for s in range(1, 8):
        ref = zfull.at[:, slot(z), :]
        zback.append(send(ref, ref, zb_s.at[s], zb_r.at[s], at_z(s)[1]))
    places = [(n, i, 192 * n + 16 * i) for n in range(5) for i in range(12)]
    small[180:192] = jnp.zeros((12, 640), F32)
    for c in range(2):
        for t in range(9):
            small[20 * t : 20 * t + 20] = prod[288 * c + 32 * t : 288 * c + 32 * t + 20]
        for n, i, f in places:
            piece = small[16 * i : 16 * i + 16, 128 * n : 128 * n + 128].astype(BF16)
            tb[c, f // 128, f % 128 : f % 128 + 16] = piece
        tb[c, 7, 64:128] = jnp.zeros((64, 128), BF16)
    there = []
    for s in range(1, 16):
        other, device = at_spot(s)
        there.append(send(tb.at[lax.rem(other, 2), other // 2], tin.at[s], t_s.at[s], t_r.at[s], device))
    for copy in zback:
        copy.wait()
    xback = []
    for h in halves:
        pfull[h, quarter(second_index[h])] = zfull[h]
        for s in range(1, 4):
            ref = pfull.at[h, quarter(second_index[h])]
            xback.append(send(ref, ref, xb_s.at[h, s], xb_r.at[h, s], second_at[h](s)[1]))
    tap(3)
    tap(4)
    for copy in xback:
        copy.wait()
    fin = []
    for h in halves:
        for n in range(5):
            out_ref[part(core, h, first_index[h]), 128 * n : 128 * n + 128] = pfull[h, 80 * n : 80 * n + 80]

    def forward(rows, send_sem, recv_sem, device):
        return send(out_ref.at[rows], out_ref.at[rows], send_sem, recv_sem, device)

    def landed(rows, h, i):
        remote(out_ref.at[rows], out_ref.at[rows], yb_s.at[h, i], yb_r.at[h, i], sib).wait_recv()

    for h in halves:
        rows = part(core, h, first_index[h])
        sent.append(forward(rows, yb_s.at[h, 0], yb_r.at[h, 0], up[h][1]))
        sent.append(forward(rows, yb_s.at[h, 1], yb_r.at[h, 1], down[h][1]))
        fin.append(forward(rows, fin_s.at[h, 0], fin_r.at[h, 0], sib))
    tap(5)
    tap(6)
    for h in halves:
        landed(part(core, h, down[h][0]), h, 0)
        landed(part(core, h, up[h][0]), h, 1)
        sent.append(forward(low_of(core, h, down[h][0]), yb_s.at[h, 2], yb_r.at[h, 2], up[h][1]))
        sent.append(forward(high_of(core, h, up[h][0]), yb_s.at[h, 3], yb_r.at[h, 3], down[h][1]))
        fin.append(forward(part(core, h, down[h][0]), fin_s.at[h, 1], fin_r.at[h, 1], sib))
        fin.append(forward(part(core, h, up[h][0]), fin_s.at[h, 2], fin_r.at[h, 2], sib))
    tap(7)
    whole = tb[xlo, dp].astype(F32)
    for s in range(1, 16):
        there[s - 1].wait()
        whole = whole + tin[s].astype(F32)
    tfull[dp] = whole.astype(BF16)
    tback = []
    for s in range(1, 8):
        ref = tfull.at[dp]
        tback.append(send(ref, ref, u_s.at[s], u_r.at[s], at_dp(s)[1]))
    for h in halves:
        landed(low_of(core, h, far[h]), h, 2)
        landed(high_of(core, h, far[h]), h, 3)
        fin.append(forward(part(core, h, far[h]), fin_s.at[h, 3], fin_r.at[h, 3], sib))
    tap(8)
    lat_ref[...] = acc[...].astype(BF16)
    for copy in tback:
        copy.wait()
    for n, i, f in places:
        small[16 * i : 16 * i + 16, 128 * n : 128 * n + 128] = tfull[f // 128, f % 128 : f % 128 + 16].astype(F32)
    for t in range(9):
        taps_ref[t] = small[20 * t : 20 * t + 20]
    for copy in fin:
        copy.wait()
    for copy in sent:
        copy.wait_send()


ATTEND = 52


def whole_kernel(*refs):
    hbm, (rows_ref, taps_ref, lat_ref), scratch = refs[:7], refs[7:10], refs[10:]
    shared, scratch = scratch[:10], scratch[10:]
    latent, wq, wk, wv, wo, w, both, packed, lhs, parts = shared
    hidden, cot = both.at[0], both.at[1]
    one, two, three = scratch[:16], scratch[16 : 16 + ATTEND], scratch[16 + ATTEND :]
    windows, queries = first_kernel(hbm, latent, cot, wq, wk, wv, wo, w, hidden, packed, *one)
    attend_kernel(windows, queries, lhs, packed, parts, *two)
    finish_kernel(parts, both, wq, wk, wv, lhs, w, rows_ref, taps_ref, lat_ref, *three)


def whole(*args):
    dma = pltpu.SemaphoreType.DMA
    vmem = pl.BlockSpec(memory_space=pltpu.VMEM)

    def b16(*shape):
        return pltpu.VMEM(shape, BF16)

    def f32(*shape):
        return pltpu.VMEM(shape, F32)

    shared = [
        b16(128, 640), b16(320, 640), b16(320, 640), b16(320, 640), b16(320, 640),
        b16(9, 640, 640), b16(2, 128, 640), b16(10, 128, 128), b16(8, 576, 256), b16(4, 128, 384),
    ]
    one = [
        dma((6,)), dma((9,)), b16(2, 64, 640), f32(656, 128), b16(16, 2, 32, 128), b16(18, 2, 32, 128),
        b16(3, 256, 640), f32(128, 640), f32(2, 128, 128), f32(128, 320),
        dma((2,)), dma((2,)), dma((16,)), dma((16,)), dma((16,)), dma((1,)),
    ]
    two = [
        b16(8, 640, 128), b16(8, 128, 640), b16(2, 512, 128), b16(512, 128), b16(512, 128), b16(512, 128), b16(512, 128),
        f32(64, 512), f32(64, 512),
        f32(8, 640, 512), f32(640, 512), b16(640, 512), b16(640, 512),
        f32(1, 512), f32(1, 512), f32(64, 512), f32(1, 512), f32(64, 512),
        f32(1, 512), f32(1, 512), f32(64, 512), f32(1, 512), f32(64, 512),
        f32(640, 128), b16(4, 640, 128), b16(4, 640, 128), b16(4, 640, 128), b16(4, 640, 128),
        f32(4, 72, 128), f32(4, 72, 128), f32(4, 8, 128), f32(128, 128), b16(3, 512, 128), b16(4, 3, 128, 128),
        dma((4,)), dma((4,)), dma((2, 4)), dma((2, 4)),
        dma((4, 2)), dma((4, 2)), dma((4, 2)), dma((4, 2)), dma((4, 2)), dma((4, 2)), dma((4, 2)), dma((4, 2)),
        dma((4,)), dma((4,)), dma((4,)), dma((4,)), dma((3, 4)), dma((3, 4)),
    ]
    three = [
        b16(8, 256, 640), b16(2, 64, 640), b16(3, 256, 640), f32(128, 640),
        f32(576, 640), f32(192, 640), b16(384, 128),
        b16(1280, 640), b16(640, 640), b16(2, 48, 640), b16(2, 32, 640), b16(2, 80, 640), b16(2, 80, 640),
        b16(2, 512, 128), b16(2, 4, 128, 128), b16(2, 128, 128), b16(8, 2, 16, 128), b16(2, 128, 128), b16(2, 512, 128),
        b16(2, 8, 128, 128), b16(16, 128, 128), b16(8, 128, 128),
        dma((2,)), dma((2,)), dma((7,)), dma((7,)), dma((8,)), dma((16,)), dma((8,)),
        dma((2,)), dma((2,)), dma((2, 4)), dma((2, 4)), dma((2, 4)), dma((2, 4)), dma((8,)), dma((8,)),
        dma((8,)), dma((8,)), dma((2, 4)), dma((2, 4)), dma((2, 4)), dma((2, 4)), dma((2, 4)), dma((2, 4)),
        dma((16,)), dma((16,)), dma((8,)), dma((8,)),
    ]
    return pl.pallas_call(
        whole_kernel,
        out_shape=(
            jax.ShapeDtypeStruct((1280, 640), BF16),
            jax.ShapeDtypeStruct((9, 20, 640), F32),
            jax.ShapeDtypeStruct((128, 640), BF16),
        ),
        in_specs=[pl.BlockSpec(memory_space=pl.ANY)] * 7,
        out_specs=(vmem,) * 3,
        scratch_shapes=shared + one + two + three,
        compiler_params=pltpu.CompilerParams(
            collective_id=0, has_side_effects=True, vmem_limit_bytes=60 * 1024 * 1024
        ),
        name="whole",
    )(*args)


def hand_kernel(rows_ref, taps_ref, lat_ref, taps_out, lat_out, *rest):
    outs, (rows, wide, taps, lat, in_sem, out_sem) = rest[:4], rest[4:]
    loads = [
        pltpu.make_async_copy(rows_ref.at[AW * i : AW * i + AW], rows.at[i], in_sem.at[i]) for i in range(4)
    ]
    loads.append(pltpu.make_async_copy(taps_ref, taps, in_sem.at[4]))
    loads.append(pltpu.make_async_copy(lat_ref, lat, in_sem.at[5]))
    for copy in loads:
        copy.start()
    stores = []
    for i in range(6):
        loads[i].wait()
        if i < 4:
            wide[i] = rows[i].astype(F32)
            copy = pltpu.make_async_copy(wide.at[i], outs[i], out_sem.at[i])
        elif i == 4:
            copy = pltpu.make_async_copy(taps, taps_out, out_sem.at[i])
        else:
            copy = pltpu.make_async_copy(lat, lat_out, out_sem.at[i])
        copy.start()
        stores.append(copy)
    for copy in stores:
        copy.wait()


def hand_out(rows, taps, grad_latent):
    anywhere = pl.BlockSpec(memory_space=pl.ANY)
    return pl.pallas_call(
        hand_kernel,
        out_shape=(
            jax.ShapeDtypeStruct(taps.shape, F32),
            jax.ShapeDtypeStruct(grad_latent.shape, BF16),
        )
        + (jax.ShapeDtypeStruct((AW, 640), F32),) * 4,
        in_specs=[anywhere] * 3,
        out_specs=(anywhere,) * 6,
        scratch_shapes=[
            pltpu.VMEM((4, AW, 640), BF16),
            pltpu.VMEM((4, AW, 640), F32),
            pltpu.VMEM(taps.shape, F32),
            pltpu.VMEM(grad_latent.shape, BF16),
            pltpu.SemaphoreType.DMA((6,)),
            pltpu.SemaphoreType.DMA((6,)),
        ],
        compiler_params=pltpu.CompilerParams(vmem_limit_bytes=60 * 1024 * 1024),
        name="hand_out",
    )(rows, taps, grad_latent)


def body(latent, cotangent, conv_weight, query_weight, key_weight, value_weight, out_weight):
    sums = whole(
        latent.reshape(128, 640), cotangent.reshape(128, 640), out_weight, key_weight.T, value_weight.T,
        query_weight.T, conv_weight.reshape(9, 640, 640),
    )
    taps, grad_latent, query, key, value, out = hand_out(*sums)
    return (grad_latent.reshape(latent.shape), taps.reshape(3, 3, 20, 640), query.T, key.T, value.T, out)


def solution(mesh):
    placed = (P("dp", "patch", None, None), P("dp", "patch", None, None), P(), P(), P(), P(), P())
    return jax.shard_map(
        body,
        mesh=mesh,
        in_specs=placed,
        out_specs=(P("dp", "patch", None, None), P(None, None, "patch", None), P(), P(), P(), P()),
        check_vma=False,
    )
```

```python
import functools
import jax
import jax.numpy as jnp
from jax import lax
from jax.experimental import pallas as pl
from jax.experimental.pallas import tpu as pltpu
from jax.sharding import PartitionSpec as P

NH = 5
HD = 64
AW = 320
MESH = pl.DeviceIdType.MESH
F32 = jnp.float32
BF16 = jnp.bfloat16


def place():
    p = lax.axis_index("patch")
    return lax.axis_index("dp"), p // 16, lax.rem(p, 16) // 2, lax.rem(p, 2)


def send(src, dst, send_sem, recv_sem, device):
    copy = pltpu.make_async_remote_copy(
        src_ref=src, dst_ref=dst, send_sem=send_sem, recv_sem=recv_sem,
        device_id=device, device_id_type=MESH,
    )
    copy.start()
    return copy


NT = (((1,), (1,)), ((), ()))
LOG2E = 1.4426950408889634


def remote(src, dst, send_sem, recv_sem, device):
    return pltpu.make_async_remote_copy(
        src_ref=src, dst_ref=dst, send_sem=send_sem, recv_sem=recv_sem,
        device_id=device, device_id_type=MESH,
    )


def attend_kernel(windows, queries, lhs_ref, x_ref, out_ref, kv, kvt, qd, qs, gs, q4, g4, gt, gt4, scores, slope, pb, sb,
                  top, low, att, delta, dq, top4, low4, att4, delta4, dq4, part, box_up, box_down, ahead, behind,
                  mix, mix_in, stat, own4, stage, res,
                  kv_s, kv_r, qd_s, qd_r, up_s, up_r, down_s, down_r, rup_s, rup_r, rdown_s, rdown_r,
                  mix_s, mix_r, stat_s, stat_r, g_s, g_r):
    dp, xlo, z, core = place()
    j = xlo * 2 + core

    def at_z(step):
        return (dp, xlo * 16 + lax.rem(z + step + 8, 8) * 2 + core)

    def in_quad(step):
        m = lax.rem(j + step, 4)
        return m, (dp, (m // 2) * 16 + z * 2 + lax.rem(m, 2))

    def rows(m):
        return pl.ds(pl.multiple_of(m * 128, 128), 128)

    first, second = [], []
    for s in range(1, 4):
        m, device = in_quad(s)
        first.append(send(x_ref.at[2 * m], kv.at[z, rows(j), :], kv_s.at[s], kv_r.at[s], device))
    queries()
    for s in range(1, 4):
        m, device = in_quad(s)
        second.append(send(x_ref.at[2 * m + 1], qd.at[0, rows(j), :], qd_s.at[0, s], qd_r.at[0, s], device))
        second.append(send(x_ref.at[8], qd.at[1, rows(j), :], qd_s.at[1, s], qd_r.at[1, s], device))
    kv[z, rows(j), :] = x_ref[2 * j]
    kv[z, 512:640] = x_ref[9]
    qd[0, rows(j), :] = x_ref[2 * j + 1]
    qd[1, rows(j), :] = x_ref[8]
    lane = lax.broadcasted_iota(jnp.int32, (128, 128), 1)
    left = lane < 64
    for ref in (top, top4):
        ref[...] = jnp.full(ref.shape, -jnp.inf, F32)
    for ref in (low, low4, att, att4, dq, dq4):
        ref[...] = jnp.zeros(ref.shape, F32)

    cuts = (slice(0, 320), slice(320, 640))

    def ring_up(s, i):
        ref = kv.at[lax.rem(z + 8 - s, 8), cuts[i]]
        return remote(ref, ref, up_s.at[s, i], up_r.at[s, i], at_z(1))

    def ring_down(s, i):
        ref = kv.at[lax.rem(z + s, 8), cuts[i]]
        return remote(ref, ref, down_s.at[s, i], down_r.at[s, i], at_z(-1))

    for copy in first:
        copy.wait()
    for i in range(2):
        ring_up(0, i).start()
        ring_down(0, i).start()
    windows(lhs_ref)
    for copy in second:
        copy.wait()
    for m in range(4):
        r = slice(m * 128, m * 128 + 128)
        for i, (a, b, bt) in enumerate(((qs, gs, gt), (q4, g4, gt4))):
            pair = qd[i, r].astype(F32)
            a[r] = jnp.where(left, pair, 0.0).astype(BF16)
            b[r] = jnp.where(left, 0.0, pair).astype(BF16)
            bt[:, r] = pair.T[64:128]

    def soften(b, keys, q, top, low, att):
        s = scores[b, keys, q]
        old = top[:, q]
        new = jnp.maximum(old, jnp.max(s, axis=0, keepdims=True))
        p = jnp.exp2(s - new)
        fade = jnp.exp2(old - new)
        low[:, q] = low[:, q] * fade + jnp.sum(p, axis=0, keepdims=True)
        top[:, q] = new
        att[:, q] = att[:, q] * fade
        pb[keys, q] = p.astype(BF16)

    main, side = slice(0, 512), slice(512, 640)
    quarters = [slice(128 * i, 128 * i + 128) for i in range(4)]

    def pass_one(t, carry):
        for s in range(3):
            @pl.when(t == 2 * s + 1)
            def _():
                for i in range(2):
                    ring_up(s, i).wait_recv()
                    if s < 2 or i == 0:
                        ring_up(s + 1, i).start()
                    ring_down(s, i).wait_recv()
                    if s < 2 or i == 1:
                        ring_down(s + 1, i).start()

        @pl.when(t == 7)
        def _():
            ring_up(3, 0).wait_recv()
            ring_down(3, 1).wait_recv()

        offset = jnp.where(lax.rem(t, 2) == 1, 8 - (t + 1) // 2, t // 2)
        b = lax.rem(z + offset, 8)
        scores[b, main] = lax.dot_general(kv[b, main], qs[...], NT, preferred_element_type=F32) * LOG2E
        scores[b, side] = lax.dot_general(kv[b, side], q4[...], NT, preferred_element_type=F32) * LOG2E
        for i in range(5):
            c = slice(128 * i, 128 * i + 128)
            kvt[b, :, c] = kv[b, c].astype(F32).T.astype(BF16)
        for q in quarters:
            soften(b, main, q, top, low, att)
            soften(b, side, q, top4, low4, att4)
        att[...] += jnp.dot(kvt[b, 64:128, main], pb[main], preferred_element_type=F32)
        att4[...] += jnp.dot(kvt[b, 64:128, side], pb[side], preferred_element_type=F32)
        return carry

    lax.fori_loop(0, 8, pass_one, 0)
    for m in range(4):
        q = quarters[m]
        mix[m, 0:64] = att4[:, q]
        mix[m, 64:65] = top4[:, q]
        mix[m, 65:66] = low4[:, q]
        mix[m, 66:72] = jnp.zeros((6, 128), F32)
    mixing = []
    for s in range(1, 4):
        m, device = in_quad(s)
        mixing.append(send(mix.at[m], mix_in.at[s], mix_s.at[s], mix_r.at[s], device))
    mix_in[0] = mix[j]
    att[...] = att[...] / low[...]
    top[...] = top[...] + jnp.log2(low[...])
    delta[...] = jnp.sum(att[...] * gt[...], axis=0, keepdims=True)

    def stat_copy(s):
        return remote(stat.at[j], stat.at[j], stat_s.at[s], stat_r.at[s], in_quad(s)[1])

    late = []
    for q in quarters:
        stage[1, q] = jnp.concatenate([att[:, q], jnp.zeros((64, 128), F32)], axis=0).T.astype(BF16)
    for s in range(1, 4):
        m, device = in_quad(s)
        late.append(send(stage.at[1, rows(m), :], res.at[j, 1], g_s.at[2, s], g_r.at[2, s], device))
    def sum_up(s, i):
        return remote(box_up.at[s, cuts[i]], ahead.at[s, cuts[i]], rup_s.at[s, i], rup_r.at[s, i], at_z(1))

    def sum_down(s, i):
        return remote(
            box_down.at[s, cuts[i]], behind.at[s, cuts[i]], rdown_s.at[s, i], rdown_r.at[s, i], at_z(-1)
        )

    def pass_on(box, landed, step, s, i):
        c = cuts[i]
        step(s, i).wait_recv()
        box[s + 1, c] = (part[c] + landed[s, c].astype(F32)).astype(BF16)
        step(s + 1, i).start()

    def slopes(b, keys, q, top, delta):
        p = jnp.exp2(scores[b, keys, q] - top[:, q])
        pb[keys, q] = p.astype(BF16)
        sb[keys, q] = (p * (slope[keys, q] - delta[:, q])).astype(BF16)

    def merge():
        for copy in mixing:
            copy.wait()
        tops = [mix_in[s, 64:65] for s in range(4)]
        best = jnp.maximum(jnp.maximum(tops[0], tops[1]), jnp.maximum(tops[2], tops[3]))
        total, blend = jnp.zeros((1, 128), F32), jnp.zeros((64, 128), F32)
        for s in range(4):
            weight = jnp.exp2(tops[s] - best)
            total = total + mix_in[s, 65:66] * weight
            blend = blend + mix_in[s, 0:64] * weight
        blend = blend / total
        own4[0:64] = blend
        own4[64:128] = jnp.zeros((64, 128), F32)
        stat[j, 0:1] = best + jnp.log2(total)
        stat[j, 1:2] = jnp.sum(blend * gt4[:, rows(j)], axis=0, keepdims=True)
        stat[j, 2:8] = jnp.zeros((6, 128), F32)
        for s in range(1, 4):
            stat_copy(s).start()

    def main_part(b):
        slope[main] = lax.dot_general(kv[b, main], gs[...], NT, preferred_element_type=F32)
        for q in quarters:
            slopes(b, main, q, top, delta)
        part[main] = jnp.dot(sb[main], qs[...], preferred_element_type=F32) + jnp.dot(
            pb[main], gs[...], preferred_element_type=F32
        )

    def main_dq(b):
        dq[...] += jnp.dot(kvt[b, 0:64, main], sb[main], preferred_element_type=F32)

    def side_part(b):
        slope[side] = lax.dot_general(kv[b, side], g4[...], NT, preferred_element_type=F32)
        for q in quarters:
            slopes(b, side, q, top4, delta4)
        part[side] = jnp.dot(sb[side], q4[...], preferred_element_type=F32) + jnp.dot(
            pb[side], g4[...], preferred_element_type=F32
        )

    def side_dq(b):
        dq4[...] += jnp.dot(kvt[b, 0:64, side], sb[side], preferred_element_type=F32)

    edge = lax.rem(z + 4, 8)
    main_part(edge)
    box_up[0, cuts[0]] = part[cuts[0]].astype(BF16)
    sum_up(0, 0).start()
    box_down[0, 320:512] = part[320:512].astype(BF16)
    main_dq(edge)
    merge()

    def pass_two(t, carry):
        offset = jnp.where(lax.rem(t, 2) == 0, 4 + t // 2, 4 - (t + 1) // 2)
        b = lax.rem(z + offset, 8)
        main_part(b)

        @pl.when(t == 1)
        def _():
            for s in range(1, 4):
                stat_copy(s).wait()
            for m in range(4):
                top4[:, quarters[m]] = stat[m, 0:1]
                delta4[:, quarters[m]] = stat[m, 1:2]
            side_part(edge)
            box_down[0, side] = part[side].astype(BF16)
            sum_down(0, 1).start()
            side_dq(edge)

        side_part(b)

        @pl.when(t == 1)
        def _():
            box_up[1, cuts[1]] = part[cuts[1]].astype(BF16)
            sum_up(1, 1).start()
            pass_on(box_up, ahead, sum_up, 0, 0)

        @pl.when(t == 2)
        def _():
            box_down[1, cuts[0]] = part[cuts[0]].astype(BF16)
            sum_down(1, 0).start()
            pass_on(box_down, behind, sum_down, 0, 1)

        for s in range(1, 3):
            @pl.when(t == 2 * s + 1)
            def _():
                pass_on(box_up, ahead, sum_up, s, 1)
                pass_on(box_up, ahead, sum_up, s, 0)

            @pl.when(t == 2 * s + 2)
            def _():
                pass_on(box_down, behind, sum_down, s, 0)
                pass_on(box_down, behind, sum_down, s, 1)

        main_dq(b)
        side_dq(b)
        return carry

    lax.fori_loop(1, 8, pass_two, 0)
    for q in quarters:
        both = jnp.concatenate([dq[:, q], dq4[:, q]], axis=0) * HD ** -0.5
        stage[0, q] = both.T.astype(BF16)
    for s in range(1, 4):
        m, device = in_quad(s)
        late.append(send(stage.at[0, rows(m), :], res.at[j, 0], g_s.at[0, s], g_r.at[0, s], device))
    for i in range(2):
        sum_up(3, i).wait_recv()
        sum_down(3, i).wait_recv()
    stage[2] = (part[main] + ahead[3, main].astype(F32) + behind[3, main].astype(F32)).astype(BF16)
    for s in range(1, 4):
        m, device = in_quad(s)
        late.append(send(stage.at[2, rows(m), :], res.at[j, 2], g_s.at[1, s], g_r.at[1, s], device))
    own = part[side] + ahead[3, side].astype(F32) + behind[3, side].astype(F32)
    for t in range(3):
        res[j, t] = stage[t, rows(j), :]
    for s in range(4):
        for i in range(2):
            if s < 3 or i == 0:
                ring_up(s, i).wait_send()
            if s < 3 or i == 1:
                ring_down(s, i).wait_send()
            if s > 0 or i == 0:
                sum_up(s, i).wait_send()
            if s > 0 or i == 1:
                sum_down(s, i).wait_send()
    for copy in late:
        copy.wait()

    def swap(a):
        return pltpu.roll(a, 64, axis=1)

    for t, source, high in ((0, 1, False), (1, 0, False), (2, 2, False), (3, 2, True)):
        for i in range(2):
            a, b = res[2 * i, source].astype(F32), res[2 * i + 1, source].astype(F32)
            pair = jnp.where(left, swap(a), b) if high else jnp.where(left, a, swap(b))
            out_ref[t, :, 128 * i : 128 * i + 128] = pair.astype(BF16)
    last4 = (
        own4[...].T,
        swap(sum(res[m, 0].astype(F32) for m in range(4))),
        own,
        swap(own),
    )
    for t in range(4):
        out_ref[t, :, 256:384] = jnp.where(left, last4[t], 0.0).astype(BF16)


def shifted(rows, j):
    before = jnp.where(j == 0, 0.0, pltpu.roll(rows, 1, axis=0))
    after = jnp.where(j == 63, 0.0, pltpu.roll(rows, 63, axis=0))
    return before, rows, after


def first_kernel(hbm, lat_ref, cot_ref, wq_ref, wk_ref, wv_ref, wo_ref, w, hid_ref, x_ref, load_sem, w_sem,
                 halo, turned, sbuf, share, sh, acc, tmp, kept, halo_s, halo_r, share_s, share_r, rim_s, rim_r):
    dp, xlo, z, core = place()
    p = lax.axis_index("patch")
    spot = dp * 2 + xlo
    index = lax.rem(p, 16)

    def at(step):
        other = lax.rem(p + step + 32, 32)
        return (dp, other)

    local = (lat_ref, cot_ref, wo_ref, wk_ref, wv_ref, wq_ref)
    inputs = []
    for i, ref in enumerate(local):
        copy = pltpu.make_async_copy(hbm[i], ref, load_sem.at[i])
        copy.start()
        inputs.append(copy)
    loads = [pltpu.make_async_copy(hbm[6].at[t], w.at[t], w_sem.at[t]) for t in range(9)]
    for t in (3, 4, 5, 0, 1, 2, 6, 7, 8):
        loads[t].start()
    barrier = pltpu.get_barrier_semaphore()

    def hello(s, carry):
        pl.semaphore_signal(barrier, inc=1, device_id=at(s), device_id_type=MESH)
        return carry

    def hello_plane(s, carry):
        other = lax.rem(spot + s, 16)
        device = (other // 2, lax.rem(other, 2) * 16 + index)
        pl.semaphore_signal(barrier, inc=1, device_id=device, device_id_type=MESH)
        return carry

    lax.fori_loop(1, 32, hello, 0)
    lax.fori_loop(1, 16, hello_plane, 0)
    inputs[0].wait()
    turned[0:640] = lat_ref[...].astype(F32).T
    turned[640:656] = jnp.zeros((16, 128), F32)
    for k in range(32):
        sbuf[k % 16, k // 16] = turned[20 * k : 20 * k + 32].astype(BF16)
    share[jnp.where(xlo == 0, 0, 17)] = jnp.zeros((2, 32, 128), BF16)
    share[index + 1] = sbuf[index]
    pl.semaphore_wait(barrier, 46)
    near = [
        send(lat_ref.at[64:128], halo.at[0], halo_s.at[0], halo_r.at[0], at(1)),
        send(lat_ref.at[0:64], halo.at[1], halo_s.at[1], halo_r.at[1], at(-1)),
    ]

    def share_copy(s):
        other = lax.rem(index + s, 16)
        return remote(sbuf.at[other], share.at[index + 1], share_s.at[s], share_r.at[s], (dp, xlo * 16 + other))

    rim = index == jnp.where(xlo == 0, 15, 0)
    rim_slot = jnp.where(xlo == 0, 0, 17)

    def rim_copy(s):
        return remote(sbuf.at[s], share.at[rim_slot], rim_s.at[s], rim_r.at[0], (dp, (1 - xlo) * 16 + s))

    def share_start(s, carry):
        share_copy(s).start()
        return carry

    def rim_start(s, carry):
        rim_copy(s).start()
        return carry

    lax.fori_loop(1, 16, share_start, 0)

    @pl.when(rim)
    def _():
        lax.fori_loop(0, 16, rim_start, 0)

    lane = lax.broadcasted_iota(jnp.int32, (128, 128), 1)
    left = lane < 64

    def pack(low_value, high_value, first_slot, last_slot):
        for n in range(3):
            c = slice(128 * n, min(128 * n + 128, AW))
            width = c.stop - c.start
            tmp[0, :, 0:width] = low_value[:, c]
            tmp[1, :, 0:width] = high_value[:, c]
            a, b = tmp[0], tmp[1]
            even = jnp.where(left, a, pltpu.roll(b, 64, axis=1)).astype(BF16)
            if n == 2:
                x_ref[last_slot] = even
            else:
                x_ref[4 * n + first_slot] = even
                x_ref[4 * n + 2 + first_slot] = jnp.where(left, pltpu.roll(a, 64, axis=1), b).astype(BF16)

    inputs[1].wait()
    inputs[2].wait()
    out_grad = lax.dot_general(cot_ref[...], wo_ref[...], NT, preferred_element_type=F32)
    tmp[...] = jnp.zeros(tmp.shape, F32)
    j = lax.broadcasted_iota(jnp.int32, (64, 640), 0)

    def lay(r, value):
        for b, moved in enumerate(shifted(value, j)):
            sh[b, 64 * r : 64 * r + 64] = moved.astype(BF16)

    lay(1, lat_ref[0:64].astype(F32))
    lay(2, lat_ref[64:128].astype(F32))
    for t in (3, 4, 5, 0, 1, 2, 6, 7, 8):
        a, b = t // 3, t % 3
        if t == 0:
            for copy in near:
                copy.wait()
            lay(0, jnp.where(p > 0, halo[0].astype(F32), 0.0))
            lay(3, jnp.where(p < 31, halo[1].astype(F32), 0.0))
        loads[t].wait()
        term = jnp.dot(sh[b, 64 * a : 64 * a + 128], w[t], preferred_element_type=F32)
        if t == 3:
            acc[...] = term
        else:
            acc[...] += term
    hid_ref[...] = acc[...].astype(BF16)
    for copy in inputs[3:]:
        copy.wait()

    def project(ref):
        value = lax.dot_general(hid_ref[...], ref[...], NT, preferred_element_type=F32)
        return value.astype(BF16).astype(F32)

    pack(project(wk_ref), project(wv_ref), 0, 9)
    kept[...] = out_grad

    def queries():
        pack(project(wq_ref) * HD ** -0.5, kept[...], 1, 8)

    def windows(lhs_ref):
        def share_end(s, carry):
            share_copy(s).wait()
            return carry

        def rim_end(s, carry):
            rim_copy(s).wait_send()
            return carry

        lax.fori_loop(1, 16, share_end, 0)
        rim_copy(0).wait_recv()

        @pl.when(rim)
        def _():
            lax.fori_loop(0, 16, rim_end, 0)

        col = lax.broadcasted_iota(jnp.int32, (32, 128), 1)
        near_side = col < 64
        col = lax.rem(col, 64)

        def one(q, carry):
            lanes = pl.ds(pl.multiple_of(lax.rem(q, 2) * 128, 128), 128)
            for c in range(2):
                here = share[q + 1, c].astype(F32)
                turn = pltpu.roll(here, 64, axis=1)
                above = jnp.where(near_side, pltpu.roll(share[q, c].astype(F32), 64, axis=1), turn)
                below = jnp.where(near_side, turn, pltpu.roll(share[q + 2, c].astype(F32), 64, axis=1))
                for a, value in enumerate((above, here, below)):
                    three = (
                        jnp.where(col == 0, 0.0, pltpu.roll(value, 1, axis=1)),
                        value,
                        jnp.where(col == 63, 0.0, pltpu.roll(value, 127, axis=1)),
                    )
                    for b in range(3):
                        row = 288 * c + 32 * (3 * a + b)
                        lhs_ref[q // 2, row : row + 32, lanes] = three[b].astype(BF16)
            return carry

        lax.fori_loop(0, 16, one, 0)

    return windows, queries


def finish_kernel(parts_ref, both_ref, wq_ref, wk_ref, wv_ref, lhs_ref, w, out_ref, taps_ref, lat_ref,
                  gh, halo, sh, acc, prod, small, turned, xs, half, ra, rb, rc, rd,
                  plane, xin, xsum, zin, zfull, pfull, tb, tin, tfull, halo_s, halo_r, up_s, down_s, sib_s, own_r, sib_r,
                  pair_s, pair_r, y_s, y_r, x_s, x_r, z_s, z_r, zb_s, zb_r, xb_s, xb_r, yb_s, yb_r, fin_s, fin_r,
                  t_s, t_r, u_s, u_r):
    dp, xlo, z, core = place()
    p = lax.axis_index("patch")
    xhi, y = dp // 4, lax.rem(dp, 4)
    x = xhi * 2 + xlo
    sib = (dp, xlo * 16 + z * 2 + 1 - core)

    def at_z(s):
        other = lax.rem(z + s + 8, 8)
        return other, (dp, xlo * 16 + other * 2 + core)

    def at_y(s):
        other = lax.rem(y + s + 4, 4)
        return other, (xhi * 4 + other, p)

    def at_x(s):
        other = lax.rem(x + s + 4, 4)
        return other, (other // 2 * 4 + y, lax.rem(other, 2) * 16 + z * 2 + core)

    spot = dp * 2 + xlo

    def at_spot(s):
        other = lax.rem(spot + s, 16)
        return other, (other // 2, lax.rem(other, 2) * 16 + z * 2 + core)

    def at_dp(s):
        other = lax.rem(dp + s, 8)
        return other, (other, p)

    def at_p(s):
        return (dp, lax.rem(p + s + 32, 32))

    mine = pl.ds(pl.multiple_of(core * 128, 128), 128)
    sent = []

    value = both_ref[1].astype(F32)
    for t, ref in ((1, wq_ref), (2, wk_ref), (3, wv_ref)):
        value = value + jnp.dot(parts_ref[t, :, 0:AW], ref[...], preferred_element_type=F32)
    gh[z, mine, :] = value.astype(BF16)

    ways = {"up": (up_s, at_z(1)[1]), "down": (down_s, at_z(-1)[1]), "sib": (sib_s, sib)}
    count = {way: 0 for way in ways}
    low = pl.ds(pl.multiple_of(core * 128, 64), 64)
    high = pl.ds(pl.multiple_of(core * 128 + 64, 64), 64)

    def block(dz):
        return lax.rem(z + dz + 8, 8)

    def ship(dz, way, i):
        u = block(dz)
        sem, device = ways[way]
        if way == "sib":
            ref, recv = gh.at[u, mine, :], sib_r.at[u]
        else:
            ref, recv = gh.at[u, (low, high)[i], :], own_r.at[2 * u + i]
        sent.append(send(ref, ref, sem.at[count[way]], recv, device))
        count[way] += 1

    def arrive(dz):
        u = block(dz)
        for i in range(2):
            ref = gh.at[u, (low, high)[i], :]
            remote(ref, ref, up_s.at[0], own_r.at[2 * u + i], sib).wait_recv()
        ship(dz, "sib", 0)

    def arrive_both(dz):
        for i in range(2):
            for d, way in ((-dz, "up"), (dz, "down")):
                u = block(d)
                ref = gh.at[u, (low, high)[i], :]
                remote(ref, ref, up_s.at[0], own_r.at[2 * u + i], sib).wait_recv()
                if dz < 3 or i == (0 if way == "up" else 1):
                    ship(d, way, i)
        ship(-dz, "sib", 0)
        ship(dz, "sib", 0)

    edge = gh.at[z]
    near = [
        send(edge.at[high, :], halo.at[0], halo_s.at[0], halo_r.at[0], at_p(1)),
        send(edge.at[low, :], halo.at[1], halo_s.at[1], halo_r.at[1], at_p(-1)),
    ]
    for i in range(2):
        ship(0, "up", i)
        ship(0, "down", i)
    ship(0, "sib", 0)

    first_at, second_at = (at_y, at_x), (at_x, at_y)
    first_index, second_index = (y, x), (x, y)
    halves = range(2)

    def part(c, h, k):
        return pl.ds(pl.multiple_of(c * 640 + h * 320 + k * 80, 16), 80)

    def low_of(c, h, k):
        return pl.ds(pl.multiple_of(c * 640 + h * 320 + k * 80, 16), 48)

    def high_of(c, h, k):
        return pl.ds(pl.multiple_of(c * 640 + h * 320 + k * 80 + 48, 16), 32)

    pair = []
    for i in range(4):
        k = lax.rem(2 * (1 - core) + i, 4)
        t = lax.rem(k + 1, 4)
        turned[...] = parts_ref[t].astype(F32).T.astype(BF16)
        r = pl.ds(pl.multiple_of(k * AW, 16), AW)
        right = both_ref[jnp.where(t == 0, 1, 0)]
        xs[r] = jnp.dot(turned[0:AW], right, preferred_element_type=F32).astype(BF16)
        if i < 2:
            pair.append(send(xs.at[r], half.at[pl.ds(320 * i, 320)], pair_s.at[i], pair_r.at[i], sib))
    arrive_both(1)
    up, down, far = [], [], []
    for h in halves:
        up.append(first_at[h](1))
        down.append(first_at[h](-1))
        far.append(lax.rem(first_index[h] + 2, 4))
        pair[h].wait()
        mine_rows = pl.ds(pl.multiple_of(core * 640 + h * 320, 16), 320)
        r = slice(320 * h, 320 * h + 320)
        half[r] = (half[r].astype(F32) + xs[mine_rows].astype(F32)).astype(BF16)
        sent.append(send(half.at[low_of(0, h, far[h])], ra.at[h], y_s.at[h, 0], y_r.at[h, 0], up[h][1]))
        sent.append(send(half.at[high_of(0, h, far[h])], rb.at[h], y_s.at[h, 1], y_r.at[h, 1], down[h][1]))

    for copy in near:
        copy.wait()
    j = lax.broadcasted_iota(jnp.int32, (64, 640), 0)
    rows = (
        jnp.where(p > 0, halo[0].astype(F32), 0.0),
        gh[z, low, :].astype(F32),
        gh[z, high, :].astype(F32),
        jnp.where(p < 31, halo[1].astype(F32), 0.0),
    )
    for r in range(4):
        moved = shifted(rows[r], j)
        for b in range(3):
            sh[2 - b, 64 * r : 64 * r + 64] = moved[b].astype(BF16)

    def tap(t):
        a, b = t // 3, t % 3
        start = 64 * (2 - a)
        term = lax.dot_general(sh[b, start : start + 128], w[t], NT, preferred_element_type=F32)
        if t:
            acc[...] += term
        else:
            acc[...] = term

    def gain(dz, start=False):
        u = block(dz)
        ref = gh.at[u, pl.ds(pl.multiple_of((1 - core) * 128, 128), 128), :]
        remote(ref, ref, up_s.at[0], sib_r.at[u], sib).wait_recv()
        term = jnp.dot(lhs_ref[u], gh[u], preferred_element_type=F32)
        if start:
            prod[...] = term
        else:
            prod[...] += term

    tap(0)
    arrive_both(2)
    for h in halves:
        remote(half.at[low_of(0, h, 0)], ra.at[h], y_s.at[h, 0], y_r.at[h, 0], sib).wait_recv()
        remote(half.at[high_of(0, h, 0)], rb.at[h], y_s.at[h, 1], y_r.at[h, 1], sib).wait_recv()
        r = low_of(0, h, up[h][0])
        half[r] = (half[r].astype(F32) + ra[h].astype(F32)).astype(BF16)
        r = high_of(0, h, down[h][0])
        half[r] = (half[r].astype(F32) + rb[h].astype(F32)).astype(BF16)
        sent.append(send(half.at[part(0, h, up[h][0])], rc.at[h], y_s.at[h, 2], y_r.at[h, 2], up[h][1]))
        sent.append(send(half.at[part(0, h, down[h][0])], rd.at[h], y_s.at[h, 3], y_r.at[h, 3], down[h][1]))
    tap(1)
    gain(0, True)
    arrive_both(3)
    tap(2)
    def quarter(k):
        return pl.ds(pl.multiple_of(k * 128, 128), 128)

    def slot(k):
        return pl.ds(pl.multiple_of(k * 16, 16), 16)

    crossing = []
    for h in halves:
        remote(half.at[part(0, h, 0)], rc.at[h], y_s.at[h, 2], y_r.at[h, 2], sib).wait_recv()
        remote(half.at[part(0, h, 0)], rd.at[h], y_s.at[h, 3], y_r.at[h, 3], sib).wait_recv()
        whole = half[part(0, h, first_index[h])].astype(F32) + rc[h].astype(F32) + rd[h].astype(F32)
        for n in range(5):
            plane[h, 80 * n : 80 * n + 80] = whole[:, 128 * n : 128 * n + 128].astype(BF16)
        plane[h, 400:512] = jnp.zeros((112, 128), BF16)
        for s in range(1, 4):
            other, device = second_at[h](s)
            crossing.append(send(plane.at[h, quarter(other)], xin.at[h, s], x_s.at[h, s], x_r.at[h, s], device))
    gain(-1)
    gain(1)
    arrive(4)
    gain(-2)
    gain(2)
    for copy in crossing:
        copy.wait()
    for h in halves:
        whole = plane[h, quarter(second_index[h])].astype(F32)
        for s in range(1, 4):
            whole = whole + xin[h, s].astype(F32)
        xsum[h] = whole.astype(BF16)
    along = []
    for s in range(1, 8):
        other, device = at_z(s)
        along.append(send(xsum.at[:, slot(other), :], zin.at[s], z_s.at[s], z_r.at[s], device))
    gain(-3)
    gain(3)
    gain(4)
    whole = xsum[:, slot(z), :].astype(F32)
    for s in range(1, 8):
        along[s - 1].wait()
        whole = whole + zin[s].astype(F32)
    zfull[:, slot(z), :] = whole.astype(BF16)
    zback = []
    for s in range(1, 8):
        ref = zfull.at[:, slot(z), :]
        zback.append(send(ref, ref, zb_s.at[s], zb_r.at[s], at_z(s)[1]))
    places = [(n, i, 192 * n + 16 * i) for n in range(5) for i in range(12)]
    small[180:192] = jnp.zeros((12, 640), F32)
    for c in range(2):
        for t in range(9):
            small[20 * t : 20 * t + 20] = prod[288 * c + 32 * t : 288 * c + 32 * t + 20]
        for n, i, f in places:
            piece = small[16 * i : 16 * i + 16, 128 * n : 128 * n + 128].astype(BF16)
            tb[c, f // 128, f % 128 : f % 128 + 16] = piece
        tb[c, 7, 64:128] = jnp.zeros((64, 128), BF16)
    there = []
    for s in range(1, 16):
        other, device = at_spot(s)
        there.append(send(tb.at[lax.rem(other, 2), other // 2], tin.at[s], t_s.at[s], t_r.at[s], device))
    for copy in zback:
        copy.wait()
    xback = []
    for h in halves:
        pfull[h, quarter(second_index[h])] = zfull[h]
        for s in range(1, 4):
            ref = pfull.at[h, quarter(second_index[h])]
            xback.append(send(ref, ref, xb_s.at[h, s], xb_r.at[h, s], second_at[h](s)[1]))
    tap(3)
    tap(4)
    for copy in xback:
        copy.wait()
    fin = []
    for h in halves:
        for n in range(5):
            out_ref[part(core, h, first_index[h]), 128 * n : 128 * n + 128] = pfull[h, 80 * n : 80 * n + 80]

    def forward(rows, send_sem, recv_sem, device):
        return send(out_ref.at[rows], out_ref.at[rows], send_sem, recv_sem, device)

    def landed(rows, h, i):
        remote(out_ref.at[rows], out_ref.at[rows], yb_s.at[h, i], yb_r.at[h, i], sib).wait_recv()

    for h in halves:
        rows = part(core, h, first_index[h])
        sent.append(forward(rows, yb_s.at[h, 0], yb_r.at[h, 0], up[h][1]))
        sent.append(forward(rows, yb_s.at[h, 1], yb_r.at[h, 1], down[h][1]))
        fin.append(forward(rows, fin_s.at[h, 0], fin_r.at[h, 0], sib))
    tap(5)
    tap(6)
    for h in halves:
        landed(part(core, h, down[h][0]), h, 0)
        landed(part(core, h, up[h][0]), h, 1)
        sent.append(forward(low_of(core, h, down[h][0]), yb_s.at[h, 2], yb_r.at[h, 2], up[h][1]))
        sent.append(forward(high_of(core, h, up[h][0]), yb_s.at[h, 3], yb_r.at[h, 3], down[h][1]))
        fin.append(forward(part(core, h, down[h][0]), fin_s.at[h, 1], fin_r.at[h, 1], sib))
        fin.append(forward(part(core, h, up[h][0]), fin_s.at[h, 2], fin_r.at[h, 2], sib))
    tap(7)
    whole = tb[xlo, dp].astype(F32)
    for s in range(1, 16):
        there[s - 1].wait()
        whole = whole + tin[s].astype(F32)
    tfull[dp] = whole.astype(BF16)
    tback = []
    for s in range(1, 8):
        ref = tfull.at[dp]
        tback.append(send(ref, ref, u_s.at[s], u_r.at[s], at_dp(s)[1]))
    for h in halves:
        landed(low_of(core, h, far[h]), h, 2)
        landed(high_of(core, h, far[h]), h, 3)
        fin.append(forward(part(core, h, far[h]), fin_s.at[h, 3], fin_r.at[h, 3], sib))
    tap(8)
    lat_ref[...] = acc[...].astype(BF16)
    for copy in tback:
        copy.wait()
    for n, i, f in places:
        small[16 * i : 16 * i + 16, 128 * n : 128 * n + 128] = tfull[f // 128, f % 128 : f % 128 + 16].astype(F32)
    for t in range(9):
        taps_ref[t] = small[20 * t : 20 * t + 20]
    for copy in fin:
        copy.wait()
    for copy in sent:
        copy.wait_send()


ATTEND = 52


def whole_kernel(*refs):
    hbm, (rows_ref, taps_ref, lat_ref), scratch = refs[:7], refs[7:10], refs[10:]
    shared, scratch = scratch[:10], scratch[10:]
    latent, wq, wk, wv, wo, w, both, packed, lhs, parts = shared
    hidden, cot = both.at[0], both.at[1]
    one, two, three = scratch[:16], scratch[16 : 16 + ATTEND], scratch[16 + ATTEND :]
    windows, queries = first_kernel(hbm, latent, cot, wq, wk, wv, wo, w, hidden, packed, *one)
    attend_kernel(windows, queries, lhs, packed, parts, *two)
    finish_kernel(parts, both, wq, wk, wv, lhs, w, rows_ref, taps_ref, lat_ref, *three)


def whole(*args):
    dma = pltpu.SemaphoreType.DMA
    vmem = pl.BlockSpec(memory_space=pltpu.VMEM)

    def b16(*shape):
        return pltpu.VMEM(shape, BF16)

    def f32(*shape):
        return pltpu.VMEM(shape, F32)

    shared = [
        b16(128, 640), b16(320, 640), b16(320, 640), b16(320, 640), b16(320, 640),
        b16(9, 640, 640), b16(2, 128, 640), b16(10, 128, 128), b16(8, 576, 256), b16(4, 128, 384),
    ]
    one = [
        dma((6,)), dma((9,)), b16(2, 64, 640), f32(656, 128), b16(16, 2, 32, 128), b16(18, 2, 32, 128),
        b16(3, 256, 640), f32(128, 640), f32(2, 128, 128), f32(128, 320),
        dma((2,)), dma((2,)), dma((16,)), dma((16,)), dma((16,)), dma((1,)),
    ]
    two = [
        b16(8, 640, 128), b16(8, 128, 640), b16(2, 512, 128), b16(512, 128), b16(512, 128), b16(512, 128), b16(512, 128),
        f32(64, 512), f32(64, 512),
        f32(8, 640, 512), f32(640, 512), b16(640, 512), b16(640, 512),
        f32(1, 512), f32(1, 512), f32(64, 512), f32(1, 512), f32(64, 512),
        f32(1, 512), f32(1, 512), f32(64, 512), f32(1, 512), f32(64, 512),
        f32(640, 128), b16(4, 640, 128), b16(4, 640, 128), b16(4, 640, 128), b16(4, 640, 128),
        f32(4, 72, 128), f32(4, 72, 128), f32(4, 8, 128), f32(128, 128), b16(3, 512, 128), b16(4, 3, 128, 128),
        dma((4,)), dma((4,)), dma((2, 4)), dma((2, 4)),
        dma((4, 2)), dma((4, 2)), dma((4, 2)), dma((4, 2)), dma((4, 2)), dma((4, 2)), dma((4, 2)), dma((4, 2)),
        dma((4,)), dma((4,)), dma((4,)), dma((4,)), dma((3, 4)), dma((3, 4)),
    ]
    three = [
        b16(8, 256, 640), b16(2, 64, 640), b16(3, 256, 640), f32(128, 640),
        f32(576, 640), f32(192, 640), b16(384, 128),
        b16(1280, 640), b16(640, 640), b16(2, 48, 640), b16(2, 32, 640), b16(2, 80, 640), b16(2, 80, 640),
        b16(2, 512, 128), b16(2, 4, 128, 128), b16(2, 128, 128), b16(8, 2, 16, 128), b16(2, 128, 128), b16(2, 512, 128),
        b16(2, 8, 128, 128), b16(16, 128, 128), b16(8, 128, 128),
        dma((2,)), dma((2,)), dma((7,)), dma((7,)), dma((8,)), dma((16,)), dma((8,)),
        dma((2,)), dma((2,)), dma((2, 4)), dma((2, 4)), dma((2, 4)), dma((2, 4)), dma((8,)), dma((8,)),
        dma((8,)), dma((8,)), dma((2, 4)), dma((2, 4)), dma((2, 4)), dma((2, 4)), dma((2, 4)), dma((2, 4)),
        dma((16,)), dma((16,)), dma((8,)), dma((8,)),
    ]
    return pl.pallas_call(
        whole_kernel,
        out_shape=(
            jax.ShapeDtypeStruct((1280, 640), BF16),
            jax.ShapeDtypeStruct((9, 20, 640), F32),
            jax.ShapeDtypeStruct((128, 640), BF16),
        ),
        in_specs=[pl.BlockSpec(memory_space=pl.ANY)] * 7,
        out_specs=(vmem,) * 3,
        scratch_shapes=shared + one + two + three,
        compiler_params=pltpu.CompilerParams(
            collective_id=0, has_side_effects=True, vmem_limit_bytes=60 * 1024 * 1024
        ),
        name="whole",
    )(*args)


def hand_kernel(rows_ref, taps_ref, lat_ref, taps_out, lat_out, *rest):
    outs, (rows, wide, taps, lat, in_sem, out_sem) = rest[:4], rest[4:]
    step = AW // 2
    loads = [
        pltpu.make_async_copy(rows_ref.at[step * i : step * i + step], rows.at[i], in_sem.at[i]) for i in range(8)
    ]
    loads.append(pltpu.make_async_copy(taps_ref, taps, in_sem.at[8]))
    loads.append(pltpu.make_async_copy(lat_ref, lat, in_sem.at[9]))
    for copy in loads:
        copy.start()
    stores = []
    for i in range(10):
        loads[i].wait()
        if i < 8:
            wide[i] = rows[i].astype(F32)
            place = outs[i // 2].at[step * (i % 2) : step * (i % 2) + step]
            copy = pltpu.make_async_copy(wide.at[i], place, out_sem.at[i])
        elif i == 8:
            copy = pltpu.make_async_copy(taps, taps_out, out_sem.at[i])
        else:
            copy = pltpu.make_async_copy(lat, lat_out, out_sem.at[i])
        copy.start()
        stores.append(copy)
    for copy in stores:
        copy.wait()


def hand_out(rows, taps, grad_latent):
    anywhere = pl.BlockSpec(memory_space=pl.ANY)
    return pl.pallas_call(
        hand_kernel,
        out_shape=(
            jax.ShapeDtypeStruct(taps.shape, F32),
            jax.ShapeDtypeStruct(grad_latent.shape, BF16),
        )
        + (jax.ShapeDtypeStruct((AW, 640), F32),) * 4,
        in_specs=[anywhere] * 3,
        out_specs=(anywhere,) * 6,
        scratch_shapes=[
            pltpu.VMEM((8, AW // 2, 640), BF16),
            pltpu.VMEM((8, AW // 2, 640), F32),
            pltpu.VMEM(taps.shape, F32),
            pltpu.VMEM(grad_latent.shape, BF16),
            pltpu.SemaphoreType.DMA((10,)),
            pltpu.SemaphoreType.DMA((10,)),
        ],
        compiler_params=pltpu.CompilerParams(vmem_limit_bytes=60 * 1024 * 1024),
        name="hand_out",
    )(rows, taps, grad_latent)


def body(latent, cotangent, conv_weight, query_weight, key_weight, value_weight, out_weight):
    sums = whole(
        latent.reshape(128, 640), cotangent.reshape(128, 640), out_weight, key_weight.T, value_weight.T,
        query_weight.T, conv_weight.reshape(9, 640, 640),
    )
    taps, grad_latent, query, key, value, out = hand_out(*sums)
    return (grad_latent.reshape(latent.shape), taps.reshape(3, 3, 20, 640), query.T, key.T, value.T, out)


def solution(mesh):
    placed = (P("dp", "patch", None, None), P("dp", "patch", None, None), P(), P(), P(), P(), P())
    return jax.shard_map(
        body,
        mesh=mesh,
        in_specs=placed,
        out_specs=(P("dp", "patch", None, None), P(None, None, "patch", None), P(), P(), P(), P()),
        check_vma=False,
    )
```

```python
import functools
import jax
import jax.numpy as jnp
from jax import lax
from jax.experimental import pallas as pl
from jax.experimental.pallas import tpu as pltpu
from jax.sharding import PartitionSpec as P

NH = 5
HD = 64
AW = 320
MESH = pl.DeviceIdType.MESH
F32 = jnp.float32
BF16 = jnp.bfloat16


def place():
    p = lax.axis_index("patch")
    return lax.axis_index("dp"), p // 16, lax.rem(p, 16) // 2, lax.rem(p, 2)


def send(src, dst, send_sem, recv_sem, device):
    copy = pltpu.make_async_remote_copy(
        src_ref=src, dst_ref=dst, send_sem=send_sem, recv_sem=recv_sem,
        device_id=device, device_id_type=MESH,
    )
    copy.start()
    return copy


NT = (((1,), (1,)), ((), ()))
LOG2E = 1.4426950408889634


def remote(src, dst, send_sem, recv_sem, device):
    return pltpu.make_async_remote_copy(
        src_ref=src, dst_ref=dst, send_sem=send_sem, recv_sem=recv_sem,
        device_id=device, device_id_type=MESH,
    )


def attend_kernel(windows, queries, lhs_ref, x_ref, out_ref, kv, kvt, qd, qs, gs, q4, g4, gt, gt4, scores, slope, pb, sb,
                  top, low, att, delta, dq, top4, low4, att4, delta4, dq4, part, box_up, box_down, ahead, behind,
                  mix, mix_in, stat, own4, stage, res,
                  kv_s, kv_r, qd_s, qd_r, up_s, up_r, down_s, down_r, rup_s, rup_r, rdown_s, rdown_r,
                  mix_s, mix_r, stat_s, stat_r, g_s, g_r):
    dp, xlo, z, core = place()
    j = xlo * 2 + core

    def at_z(step):
        return (dp, xlo * 16 + lax.rem(z + step + 8, 8) * 2 + core)

    def in_quad(step):
        m = lax.rem(j + step, 4)
        return m, (dp, (m // 2) * 16 + z * 2 + lax.rem(m, 2))

    def rows(m):
        return pl.ds(pl.multiple_of(m * 128, 128), 128)

    first, second = [], []
    for s in range(1, 4):
        m, device = in_quad(s)
        first.append(send(x_ref.at[2 * m], kv.at[z, rows(j), :], kv_s.at[s], kv_r.at[s], device))
    queries()
    for s in range(1, 4):
        m, device = in_quad(s)
        second.append(send(x_ref.at[2 * m + 1], qd.at[0, rows(j), :], qd_s.at[0, s], qd_r.at[0, s], device))
        second.append(send(x_ref.at[8], qd.at[1, rows(j), :], qd_s.at[1, s], qd_r.at[1, s], device))
    kv[z, rows(j), :] = x_ref[2 * j]
    kv[z, 512:640] = x_ref[9]
    qd[0, rows(j), :] = x_ref[2 * j + 1]
    qd[1, rows(j), :] = x_ref[8]
    lane = lax.broadcasted_iota(jnp.int32, (128, 128), 1)
    left = lane < 64
    for ref in (top, top4):
        ref[...] = jnp.full(ref.shape, -jnp.inf, F32)
    for ref in (low, low4, att, att4, dq, dq4):
        ref[...] = jnp.zeros(ref.shape, F32)

    cuts = (slice(0, 320), slice(320, 640))

    def ring_up(s, i):
        ref = kv.at[lax.rem(z + 8 - s, 8), cuts[i]]
        return remote(ref, ref, up_s.at[s, i], up_r.at[s, i], at_z(1))

    def ring_down(s, i):
        ref = kv.at[lax.rem(z + s, 8), cuts[i]]
        return remote(ref, ref, down_s.at[s, i], down_r.at[s, i], at_z(-1))

    for copy in first:
        copy.wait()
    for i in range(2):
        ring_up(0, i).start()
        ring_down(0, i).start()
    windows(lhs_ref)
    for copy in second:
        copy.wait()
    for m in range(4):
        r = slice(m * 128, m * 128 + 128)
        for i, (a, b, bt) in enumerate(((qs, gs, gt), (q4, g4, gt4))):
            pair = qd[i, r].astype(F32)
            a[r] = jnp.where(left, pair, 0.0).astype(BF16)
            b[r] = jnp.where(left, 0.0, pair).astype(BF16)
            bt[:, r] = pair.T[64:128]

    def soften(b, keys, q, top, low, att):
        s = scores[b, keys, q]
        old = top[:, q]
        new = jnp.maximum(old, jnp.max(s, axis=0, keepdims=True))
        p = jnp.exp2(s - new)
        fade = jnp.exp2(old - new)
        low[:, q] = low[:, q] * fade + jnp.sum(p, axis=0, keepdims=True)
        top[:, q] = new
        att[:, q] = att[:, q] * fade
        pb[keys, q] = p.astype(BF16)

    main, side = slice(0, 512), slice(512, 640)
    quarters = [slice(128 * i, 128 * i + 128) for i in range(4)]

    def pass_one(t, carry):
        for s in range(3):
            @pl.when(t == 2 * s + 1)
            def _():
                for i in range(2):
                    ring_up(s, i).wait_recv()
                    if s < 2 or i == 0:
                        ring_up(s + 1, i).start()
                    ring_down(s, i).wait_recv()
                    if s < 2 or i == 1:
                        ring_down(s + 1, i).start()

        @pl.when(t == 7)
        def _():
            ring_up(3, 0).wait_recv()
            ring_down(3, 1).wait_recv()

        offset = jnp.where(lax.rem(t, 2) == 1, 8 - (t + 1) // 2, t // 2)
        b = lax.rem(z + offset, 8)
        scores[b, main] = lax.dot_general(kv[b, main], qs[...], NT, preferred_element_type=F32) * LOG2E
        scores[b, side] = lax.dot_general(kv[b, side], q4[...], NT, preferred_element_type=F32) * LOG2E
        for i in range(5):
            c = slice(128 * i, 128 * i + 128)
            kvt[b, :, c] = kv[b, c].astype(F32).T.astype(BF16)
        for q in quarters:
            soften(b, main, q, top, low, att)
            soften(b, side, q, top4, low4, att4)
        att[...] += jnp.dot(kvt[b, 64:128, main], pb[main], preferred_element_type=F32)
        att4[...] += jnp.dot(kvt[b, 64:128, side], pb[side], preferred_element_type=F32)
        return carry

    lax.fori_loop(0, 8, pass_one, 0)
    for m in range(4):
        q = quarters[m]
        mix[m, 0:64] = att4[:, q]
        mix[m, 64:65] = top4[:, q]
        mix[m, 65:66] = low4[:, q]
        mix[m, 66:72] = jnp.zeros((6, 128), F32)
    mixing = []
    for s in range(1, 4):
        m, device = in_quad(s)
        mixing.append(send(mix.at[m], mix_in.at[s], mix_s.at[s], mix_r.at[s], device))
    mix_in[0] = mix[j]
    att[...] = att[...] / low[...]
    top[...] = top[...] + jnp.log2(low[...])
    delta[...] = jnp.sum(att[...] * gt[...], axis=0, keepdims=True)

    def stat_copy(s):
        return remote(stat.at[j], stat.at[j], stat_s.at[s], stat_r.at[s], in_quad(s)[1])

    late = []
    for q in quarters:
        stage[1, q] = jnp.concatenate([att[:, q], jnp.zeros((64, 128), F32)], axis=0).T.astype(BF16)
    for s in range(1, 4):
        m, device = in_quad(s)
        late.append(send(stage.at[1, rows(m), :], res.at[j, 1], g_s.at[2, s], g_r.at[2, s], device))
    def sum_up(s, i):
        return remote(box_up.at[s, cuts[i]], ahead.at[s, cuts[i]], rup_s.at[s, i], rup_r.at[s, i], at_z(1))

    def sum_down(s, i):
        return remote(
            box_down.at[s, cuts[i]], behind.at[s, cuts[i]], rdown_s.at[s, i], rdown_r.at[s, i], at_z(-1)
        )

    def pass_on(box, landed, step, s, i):
        c = cuts[i]
        step(s, i).wait_recv()
        box[s + 1, c] = (part[c] + landed[s, c].astype(F32)).astype(BF16)
        step(s + 1, i).start()

    def slopes(b, keys, q, top, delta):
        p = jnp.exp2(scores[b, keys, q] - top[:, q])
        pb[keys, q] = p.astype(BF16)
        sb[keys, q] = (p * (slope[keys, q] - delta[:, q])).astype(BF16)

    def merge():
        for copy in mixing:
            copy.wait()
        tops = [mix_in[s, 64:65] for s in range(4)]
        best = jnp.maximum(jnp.maximum(tops[0], tops[1]), jnp.maximum(tops[2], tops[3]))
        total, blend = jnp.zeros((1, 128), F32), jnp.zeros((64, 128), F32)
        for s in range(4):
            weight = jnp.exp2(tops[s] - best)
            total = total + mix_in[s, 65:66] * weight
            blend = blend + mix_in[s, 0:64] * weight
        blend = blend / total
        own4[0:64] = blend
        own4[64:128] = jnp.zeros((64, 128), F32)
        stat[j, 0:1] = best + jnp.log2(total)
        stat[j, 1:2] = jnp.sum(blend * gt4[:, rows(j)], axis=0, keepdims=True)
        stat[j, 2:8] = jnp.zeros((6, 128), F32)
        for s in range(1, 4):
            stat_copy(s).start()

    def main_part(b):
        slope[main] = lax.dot_general(kv[b, main], gs[...], NT, preferred_element_type=F32)
        for q in quarters:
            slopes(b, main, q, top, delta)
        part[main] = jnp.dot(sb[main], qs[...], preferred_element_type=F32) + jnp.dot(
            pb[main], gs[...], preferred_element_type=F32
        )

    def main_dq(b):
        dq[...] += jnp.dot(kvt[b, 0:64, main], sb[main], preferred_element_type=F32)

    def side_part(b):
        slope[side] = lax.dot_general(kv[b, side], g4[...], NT, preferred_element_type=F32)
        for q in quarters:
            slopes(b, side, q, top4, delta4)
        part[side] = jnp.dot(sb[side], q4[...], preferred_element_type=F32) + jnp.dot(
            pb[side], g4[...], preferred_element_type=F32
        )

    def side_dq(b):
        dq4[...] += jnp.dot(kvt[b, 0:64, side], sb[side], preferred_element_type=F32)

    edge = lax.rem(z + 4, 8)
    main_part(edge)
    box_up[0, cuts[0]] = part[cuts[0]].astype(BF16)
    sum_up(0, 0).start()
    box_down[0, 320:512] = part[320:512].astype(BF16)
    main_dq(edge)
    merge()

    def pass_two(t, carry):
        offset = jnp.where(lax.rem(t, 2) == 0, 4 + t // 2, 4 - (t + 1) // 2)
        b = lax.rem(z + offset, 8)
        main_part(b)

        @pl.when(t == 1)
        def _():
            for s in range(1, 4):
                stat_copy(s).wait()
            for m in range(4):
                top4[:, quarters[m]] = stat[m, 0:1]
                delta4[:, quarters[m]] = stat[m, 1:2]
            side_part(edge)
            box_down[0, side] = part[side].astype(BF16)
            sum_down(0, 1).start()
            side_dq(edge)

        side_part(b)

        @pl.when(t == 1)
        def _():
            box_up[1, cuts[1]] = part[cuts[1]].astype(BF16)
            sum_up(1, 1).start()
            pass_on(box_up, ahead, sum_up, 0, 0)

        @pl.when(t == 2)
        def _():
            box_down[1, cuts[0]] = part[cuts[0]].astype(BF16)
            sum_down(1, 0).start()
            pass_on(box_down, behind, sum_down, 0, 1)

        for s in range(1, 3):
            @pl.when(t == 2 * s + 1)
            def _():
                pass_on(box_up, ahead, sum_up, s, 1)
                pass_on(box_up, ahead, sum_up, s, 0)

            @pl.when(t == 2 * s + 2)
            def _():
                pass_on(box_down, behind, sum_down, s, 0)
                pass_on(box_down, behind, sum_down, s, 1)

        main_dq(b)
        side_dq(b)
        return carry

    lax.fori_loop(1, 8, pass_two, 0)
    for q in quarters:
        both = jnp.concatenate([dq[:, q], dq4[:, q]], axis=0) * HD ** -0.5
        stage[0, q] = both.T.astype(BF16)
    for s in range(1, 4):
        m, device = in_quad(s)
        late.append(send(stage.at[0, rows(m), :], res.at[j, 0], g_s.at[0, s], g_r.at[0, s], device))
    for i in range(2):
        sum_up(3, i).wait_recv()
        sum_down(3, i).wait_recv()
    stage[2] = (part[main] + ahead[3, main].astype(F32) + behind[3, main].astype(F32)).astype(BF16)
    for s in range(1, 4):
        m, device = in_quad(s)
        late.append(send(stage.at[2, rows(m), :], res.at[j, 2], g_s.at[1, s], g_r.at[1, s], device))
    own = part[side] + ahead[3, side].astype(F32) + behind[3, side].astype(F32)
    for t in range(3):
        res[j, t] = stage[t, rows(j), :]
    for s in range(4):
        for i in range(2):
            if s < 3 or i == 0:
                ring_up(s, i).wait_send()
            if s < 3 or i == 1:
                ring_down(s, i).wait_send()
            if s > 0 or i == 0:
                sum_up(s, i).wait_send()
            if s > 0 or i == 1:
                sum_down(s, i).wait_send()
    for copy in late:
        copy.wait()

    def swap(a):
        return pltpu.roll(a, 64, axis=1)

    for t, source, high in ((0, 1, False), (1, 0, False), (2, 2, False), (3, 2, True)):
        for i in range(2):
            a, b = res[2 * i, source].astype(F32), res[2 * i + 1, source].astype(F32)
            pair = jnp.where(left, swap(a), b) if high else jnp.where(left, a, swap(b))
            out_ref[t, :, 128 * i : 128 * i + 128] = pair.astype(BF16)
    last4 = (
        own4[...].T,
        swap(sum(res[m, 0].astype(F32) for m in range(4))),
        own,
        swap(own),
    )
    for t in range(4):
        out_ref[t, :, 256:384] = jnp.where(left, last4[t], 0.0).astype(BF16)


def shifted(rows, j):
    before = jnp.where(j == 0, 0.0, pltpu.roll(rows, 1, axis=0))
    after = jnp.where(j == 63, 0.0, pltpu.roll(rows, 63, axis=0))
    return before, rows, after


def first_kernel(hbm, lat_ref, cot_ref, wq_ref, wk_ref, wv_ref, wo_ref, w, hid_ref, x_ref, load_sem, w_sem,
                 halo, turned, sbuf, share, sh, acc, tmp, kept, halo_s, halo_r, share_s, share_r, rim_s, rim_r):
    dp, xlo, z, core = place()
    p = lax.axis_index("patch")
    spot = dp * 2 + xlo
    index = lax.rem(p, 16)

    def at(step):
        other = lax.rem(p + step + 32, 32)
        return (dp, other)

    local = (lat_ref, cot_ref, wo_ref, wk_ref, wv_ref, wq_ref)
    inputs = []
    for i, ref in enumerate(local):
        copy = pltpu.make_async_copy(hbm[i], ref, load_sem.at[i])
        copy.start()
        inputs.append(copy)
    loads = [pltpu.make_async_copy(hbm[6].at[t], w.at[t], w_sem.at[t]) for t in range(9)]
    for t in (3, 4, 5, 0, 1, 2, 6, 7, 8):
        loads[t].start()
    barrier = pltpu.get_barrier_semaphore()

    def hello(s, carry):
        pl.semaphore_signal(barrier, inc=1, device_id=at(s), device_id_type=MESH)
        return carry

    def hello_plane(s, carry):
        other = lax.rem(spot + s, 16)
        device = (other // 2, lax.rem(other, 2) * 16 + index)
        pl.semaphore_signal(barrier, inc=1, device_id=device, device_id_type=MESH)
        return carry

    lax.fori_loop(1, 32, hello, 0)
    lax.fori_loop(1, 16, hello_plane, 0)
    inputs[0].wait()
    turned[0:640] = lat_ref[...].astype(F32).T
    turned[640:656] = jnp.zeros((16, 128), F32)
    for k in range(32):
        sbuf[k % 16, k // 16] = turned[20 * k : 20 * k + 32].astype(BF16)
    share[jnp.where(xlo == 0, 0, 17)] = jnp.zeros((2, 32, 128), BF16)
    share[index + 1] = sbuf[index]
    pl.semaphore_wait(barrier, 46)
    near = [
        send(lat_ref.at[64:128], halo.at[0], halo_s.at[0], halo_r.at[0], at(1)),
        send(lat_ref.at[0:64], halo.at[1], halo_s.at[1], halo_r.at[1], at(-1)),
    ]

    def share_copy(s):
        other = lax.rem(index + s, 16)
        return remote(sbuf.at[other], share.at[index + 1], share_s.at[s], share_r.at[s], (dp, xlo * 16 + other))

    rim = index == jnp.where(xlo == 0, 15, 0)
    rim_slot = jnp.where(xlo == 0, 0, 17)

    def rim_copy(s):
        return remote(sbuf.at[s], share.at[rim_slot], rim_s.at[s], rim_r.at[0], (dp, (1 - xlo) * 16 + s))

    def share_start(s, carry):
        share_copy(s).start()
        return carry

    def rim_start(s, carry):
        rim_copy(s).start()
        return carry

    lax.fori_loop(1, 16, share_start, 0)

    @pl.when(rim)
    def _():
        lax.fori_loop(0, 16, rim_start, 0)

    lane = lax.broadcasted_iota(jnp.int32, (128, 128), 1)
    left = lane < 64

    def pack(low_value, high_value, first_slot, last_slot):
        for n in range(3):
            c = slice(128 * n, min(128 * n + 128, AW))
            width = c.stop - c.start
            tmp[0, :, 0:width] = low_value[:, c]
            tmp[1, :, 0:width] = high_value[:, c]
            a, b = tmp[0], tmp[1]
            even = jnp.where(left, a, pltpu.roll(b, 64, axis=1)).astype(BF16)
            if n == 2:
                x_ref[last_slot] = even
            else:
                x_ref[4 * n + first_slot] = even
                x_ref[4 * n + 2 + first_slot] = jnp.where(left, pltpu.roll(a, 64, axis=1), b).astype(BF16)

    inputs[1].wait()
    inputs[2].wait()
    out_grad = lax.dot_general(cot_ref[...], wo_ref[...], NT, preferred_element_type=F32)
    tmp[...] = jnp.zeros(tmp.shape, F32)
    j = lax.broadcasted_iota(jnp.int32, (64, 640), 0)

    def lay(r, value):
        for b, moved in enumerate(shifted(value, j)):
            sh[b, 64 * r : 64 * r + 64] = moved.astype(BF16)

    lay(1, lat_ref[0:64].astype(F32))
    lay(2, lat_ref[64:128].astype(F32))
    for t in (3, 4, 5, 0, 1, 2, 6, 7, 8):
        a, b = t // 3, t % 3
        if t == 0:
            for copy in near:
                copy.wait()
            lay(0, jnp.where(p > 0, halo[0].astype(F32), 0.0))
            lay(3, jnp.where(p < 31, halo[1].astype(F32), 0.0))
        loads[t].wait()
        term = jnp.dot(sh[b, 64 * a : 64 * a + 128], w[t], preferred_element_type=F32)
        if t == 3:
            acc[...] = term
        else:
            acc[...] += term
    hid_ref[...] = acc[...].astype(BF16)
    for copy in inputs[3:]:
        copy.wait()

    def project(ref):
        value = lax.dot_general(hid_ref[...], ref[...], NT, preferred_element_type=F32)
        return value.astype(BF16).astype(F32)

    pack(project(wk_ref), project(wv_ref), 0, 9)
    kept[...] = out_grad

    def queries():
        pack(project(wq_ref) * HD ** -0.5, kept[...], 1, 8)

    def windows(lhs_ref):
        def share_end(s, carry):
            share_copy(s).wait()
            return carry

        def rim_end(s, carry):
            rim_copy(s).wait_send()
            return carry

        lax.fori_loop(1, 16, share_end, 0)
        rim_copy(0).wait_recv()

        @pl.when(rim)
        def _():
            lax.fori_loop(0, 16, rim_end, 0)

        col = lax.broadcasted_iota(jnp.int32, (32, 128), 1)
        near_side = col < 64
        col = lax.rem(col, 64)

        def one(q, carry):
            lanes = pl.ds(pl.multiple_of(lax.rem(q, 2) * 128, 128), 128)
            for c in range(2):
                here = share[q + 1, c].astype(F32)
                turn = pltpu.roll(here, 64, axis=1)
                above = jnp.where(near_side, pltpu.roll(share[q, c].astype(F32), 64, axis=1), turn)
                below = jnp.where(near_side, turn, pltpu.roll(share[q + 2, c].astype(F32), 64, axis=1))
                for a, value in enumerate((above, here, below)):
                    three = (
                        jnp.where(col == 0, 0.0, pltpu.roll(value, 1, axis=1)),
                        value,
                        jnp.where(col == 63, 0.0, pltpu.roll(value, 127, axis=1)),
                    )
                    for b in range(3):
                        row = 288 * c + 32 * (3 * a + b)
                        lhs_ref[q // 2, row : row + 32, lanes] = three[b].astype(BF16)
            return carry

        lax.fori_loop(0, 16, one, 0)

    return windows, queries


def finish_kernel(rows_hbm, rows_sem, parts_ref, both_ref, wq_ref, wk_ref, wv_ref, lhs_ref, w, out_ref, taps_ref, lat_ref,
                  gh, halo, sh, acc, prod, small, turned, xs, half, ra, rb, rc, rd,
                  plane, xin, xsum, zin, zfull, pfull, tb, tin, tfull, halo_s, halo_r, up_s, down_s, sib_s, own_r, sib_r,
                  pair_s, pair_r, y_s, y_r, x_s, x_r, z_s, z_r, zb_s, zb_r, xb_s, xb_r, yb_s, yb_r, fin_s, fin_r,
                  t_s, t_r, u_s, u_r):
    dp, xlo, z, core = place()
    p = lax.axis_index("patch")
    xhi, y = dp // 4, lax.rem(dp, 4)
    x = xhi * 2 + xlo
    sib = (dp, xlo * 16 + z * 2 + 1 - core)

    def at_z(s):
        other = lax.rem(z + s + 8, 8)
        return other, (dp, xlo * 16 + other * 2 + core)

    def at_y(s):
        other = lax.rem(y + s + 4, 4)
        return other, (xhi * 4 + other, p)

    def at_x(s):
        other = lax.rem(x + s + 4, 4)
        return other, (other // 2 * 4 + y, lax.rem(other, 2) * 16 + z * 2 + core)

    spot = dp * 2 + xlo

    def at_spot(s):
        other = lax.rem(spot + s, 16)
        return other, (other // 2, lax.rem(other, 2) * 16 + z * 2 + core)

    def at_dp(s):
        other = lax.rem(dp + s, 8)
        return other, (other, p)

    def at_p(s):
        return (dp, lax.rem(p + s + 32, 32))

    mine = pl.ds(pl.multiple_of(core * 128, 128), 128)
    sent = []

    value = both_ref[1].astype(F32)
    for t, ref in ((1, wq_ref), (2, wk_ref), (3, wv_ref)):
        value = value + jnp.dot(parts_ref[t, :, 0:AW], ref[...], preferred_element_type=F32)
    gh[z, mine, :] = value.astype(BF16)

    ways = {"up": (up_s, at_z(1)[1]), "down": (down_s, at_z(-1)[1]), "sib": (sib_s, sib)}
    count = {way: 0 for way in ways}
    low = pl.ds(pl.multiple_of(core * 128, 64), 64)
    high = pl.ds(pl.multiple_of(core * 128 + 64, 64), 64)

    def block(dz):
        return lax.rem(z + dz + 8, 8)

    def ship(dz, way, i):
        u = block(dz)
        sem, device = ways[way]
        if way == "sib":
            ref, recv = gh.at[u, mine, :], sib_r.at[u]
        else:
            ref, recv = gh.at[u, (low, high)[i], :], own_r.at[2 * u + i]
        sent.append(send(ref, ref, sem.at[count[way]], recv, device))
        count[way] += 1

    def arrive(dz):
        u = block(dz)
        for i in range(2):
            ref = gh.at[u, (low, high)[i], :]
            remote(ref, ref, up_s.at[0], own_r.at[2 * u + i], sib).wait_recv()
        ship(dz, "sib", 0)

    def arrive_both(dz):
        for i in range(2):
            for d, way in ((-dz, "up"), (dz, "down")):
                u = block(d)
                ref = gh.at[u, (low, high)[i], :]
                remote(ref, ref, up_s.at[0], own_r.at[2 * u + i], sib).wait_recv()
                if dz < 3 or i == (0 if way == "up" else 1):
                    ship(d, way, i)
        ship(-dz, "sib", 0)
        ship(dz, "sib", 0)

    edge = gh.at[z]
    near = [
        send(edge.at[high, :], halo.at[0], halo_s.at[0], halo_r.at[0], at_p(1)),
        send(edge.at[low, :], halo.at[1], halo_s.at[1], halo_r.at[1], at_p(-1)),
    ]
    for i in range(2):
        ship(0, "up", i)
        ship(0, "down", i)
    ship(0, "sib", 0)

    first_at, second_at = (at_y, at_x), (at_x, at_y)
    first_index, second_index = (y, x), (x, y)
    halves = range(2)

    def part(c, h, k):
        return pl.ds(pl.multiple_of(c * 640 + h * 320 + k * 80, 16), 80)

    def low_of(c, h, k):
        return pl.ds(pl.multiple_of(c * 640 + h * 320 + k * 80, 16), 48)

    def high_of(c, h, k):
        return pl.ds(pl.multiple_of(c * 640 + h * 320 + k * 80 + 48, 16), 32)

    pair = []
    for i in range(4):
        k = lax.rem(2 * (1 - core) + i, 4)
        t = lax.rem(k + 1, 4)
        turned[...] = parts_ref[t].astype(F32).T.astype(BF16)
        r = pl.ds(pl.multiple_of(k * AW, 16), AW)
        right = both_ref[jnp.where(t == 0, 1, 0)]
        xs[r] = jnp.dot(turned[0:AW], right, preferred_element_type=F32).astype(BF16)
        if i < 2:
            pair.append(send(xs.at[r], half.at[pl.ds(320 * i, 320)], pair_s.at[i], pair_r.at[i], sib))
    arrive_both(1)
    up, down, far = [], [], []
    for h in halves:
        up.append(first_at[h](1))
        down.append(first_at[h](-1))
        far.append(lax.rem(first_index[h] + 2, 4))
        pair[h].wait()
        mine_rows = pl.ds(pl.multiple_of(core * 640 + h * 320, 16), 320)
        r = slice(320 * h, 320 * h + 320)
        half[r] = (half[r].astype(F32) + xs[mine_rows].astype(F32)).astype(BF16)
        sent.append(send(half.at[low_of(0, h, far[h])], ra.at[h], y_s.at[h, 0], y_r.at[h, 0], up[h][1]))
        sent.append(send(half.at[high_of(0, h, far[h])], rb.at[h], y_s.at[h, 1], y_r.at[h, 1], down[h][1]))

    for copy in near:
        copy.wait()
    j = lax.broadcasted_iota(jnp.int32, (64, 640), 0)
    rows = (
        jnp.where(p > 0, halo[0].astype(F32), 0.0),
        gh[z, low, :].astype(F32),
        gh[z, high, :].astype(F32),
        jnp.where(p < 31, halo[1].astype(F32), 0.0),
    )
    for r in range(4):
        moved = shifted(rows[r], j)
        for b in range(3):
            sh[2 - b, 64 * r : 64 * r + 64] = moved[b].astype(BF16)

    def tap(t):
        a, b = t // 3, t % 3
        start = 64 * (2 - a)
        term = lax.dot_general(sh[b, start : start + 128], w[t], NT, preferred_element_type=F32)
        if t:
            acc[...] += term
        else:
            acc[...] = term

    def gain(dz, start=False):
        u = block(dz)
        ref = gh.at[u, pl.ds(pl.multiple_of((1 - core) * 128, 128), 128), :]
        remote(ref, ref, up_s.at[0], sib_r.at[u], sib).wait_recv()
        term = jnp.dot(lhs_ref[u], gh[u], preferred_element_type=F32)
        if start:
            prod[...] = term
        else:
            prod[...] += term

    tap(0)
    arrive_both(2)
    for h in halves:
        remote(half.at[low_of(0, h, 0)], ra.at[h], y_s.at[h, 0], y_r.at[h, 0], sib).wait_recv()
        remote(half.at[high_of(0, h, 0)], rb.at[h], y_s.at[h, 1], y_r.at[h, 1], sib).wait_recv()
        r = low_of(0, h, up[h][0])
        half[r] = (half[r].astype(F32) + ra[h].astype(F32)).astype(BF16)
        r = high_of(0, h, down[h][0])
        half[r] = (half[r].astype(F32) + rb[h].astype(F32)).astype(BF16)
        sent.append(send(half.at[part(0, h, up[h][0])], rc.at[h], y_s.at[h, 2], y_r.at[h, 2], up[h][1]))
        sent.append(send(half.at[part(0, h, down[h][0])], rd.at[h], y_s.at[h, 3], y_r.at[h, 3], down[h][1]))
    tap(1)
    gain(0, True)
    arrive_both(3)
    tap(2)
    def quarter(k):
        return pl.ds(pl.multiple_of(k * 128, 128), 128)

    def slot(k):
        return pl.ds(pl.multiple_of(k * 16, 16), 16)

    crossing = []
    for h in halves:
        remote(half.at[part(0, h, 0)], rc.at[h], y_s.at[h, 2], y_r.at[h, 2], sib).wait_recv()
        remote(half.at[part(0, h, 0)], rd.at[h], y_s.at[h, 3], y_r.at[h, 3], sib).wait_recv()
        whole = half[part(0, h, first_index[h])].astype(F32) + rc[h].astype(F32) + rd[h].astype(F32)
        for n in range(5):
            plane[h, 80 * n : 80 * n + 80] = whole[:, 128 * n : 128 * n + 128].astype(BF16)
        plane[h, 400:512] = jnp.zeros((112, 128), BF16)
        for s in range(1, 4):
            other, device = second_at[h](s)
            crossing.append(send(plane.at[h, quarter(other)], xin.at[h, s], x_s.at[h, s], x_r.at[h, s], device))
    gain(-1)
    gain(1)
    arrive(4)
    gain(-2)
    gain(2)
    for copy in crossing:
        copy.wait()
    for h in halves:
        whole = plane[h, quarter(second_index[h])].astype(F32)
        for s in range(1, 4):
            whole = whole + xin[h, s].astype(F32)
        xsum[h] = whole.astype(BF16)
    along = []
    for s in range(1, 8):
        other, device = at_z(s)
        along.append(send(xsum.at[:, slot(other), :], zin.at[s], z_s.at[s], z_r.at[s], device))
    gain(-3)
    gain(3)
    gain(4)
    whole = xsum[:, slot(z), :].astype(F32)
    for s in range(1, 8):
        along[s - 1].wait()
        whole = whole + zin[s].astype(F32)
    zfull[:, slot(z), :] = whole.astype(BF16)
    zback = []
    for s in range(1, 8):
        ref = zfull.at[:, slot(z), :]
        zback.append(send(ref, ref, zb_s.at[s], zb_r.at[s], at_z(s)[1]))
    places = [(n, i, 192 * n + 16 * i) for n in range(5) for i in range(12)]
    small[180:192] = jnp.zeros((12, 640), F32)
    for c in range(2):
        for t in range(9):
            small[20 * t : 20 * t + 20] = prod[288 * c + 32 * t : 288 * c + 32 * t + 20]
        for n, i, f in places:
            piece = small[16 * i : 16 * i + 16, 128 * n : 128 * n + 128].astype(BF16)
            tb[c, f // 128, f % 128 : f % 128 + 16] = piece
        tb[c, 7, 64:128] = jnp.zeros((64, 128), BF16)
    there = []
    for s in range(1, 16):
        other, device = at_spot(s)
        there.append(send(tb.at[lax.rem(other, 2), other // 2], tin.at[s], t_s.at[s], t_r.at[s], device))
    for copy in zback:
        copy.wait()
    xback = []
    for h in halves:
        pfull[h, quarter(second_index[h])] = zfull[h]
        for s in range(1, 4):
            ref = pfull.at[h, quarter(second_index[h])]
            xback.append(send(ref, ref, xb_s.at[h, s], xb_r.at[h, s], second_at[h](s)[1]))
    tap(3)
    tap(4)
    for copy in xback:
        copy.wait()
    fin = []
    for h in halves:
        for n in range(5):
            out_ref[part(core, h, first_index[h]), 128 * n : 128 * n + 128] = pfull[h, 80 * n : 80 * n + 80]

    def forward(rows, send_sem, recv_sem, device):
        return send(out_ref.at[rows], out_ref.at[rows], send_sem, recv_sem, device)

    def landed(rows, h, i):
        remote(out_ref.at[rows], out_ref.at[rows], yb_s.at[h, i], yb_r.at[h, i], sib).wait_recv()

    for h in halves:
        rows = part(core, h, first_index[h])
        sent.append(forward(rows, yb_s.at[h, 0], yb_r.at[h, 0], up[h][1]))
        sent.append(forward(rows, yb_s.at[h, 1], yb_r.at[h, 1], down[h][1]))
        fin.append(forward(rows, fin_s.at[h, 0], fin_r.at[h, 0], sib))
    tap(5)
    tap(6)
    for h in halves:
        landed(part(core, h, down[h][0]), h, 0)
        landed(part(core, h, up[h][0]), h, 1)
        sent.append(forward(low_of(core, h, down[h][0]), yb_s.at[h, 2], yb_r.at[h, 2], up[h][1]))
        sent.append(forward(high_of(core, h, up[h][0]), yb_s.at[h, 3], yb_r.at[h, 3], down[h][1]))
        fin.append(forward(part(core, h, down[h][0]), fin_s.at[h, 1], fin_r.at[h, 1], sib))
        fin.append(forward(part(core, h, up[h][0]), fin_s.at[h, 2], fin_r.at[h, 2], sib))
    tap(7)
    whole = tb[xlo, dp].astype(F32)
    for s in range(1, 16):
        there[s - 1].wait()
        whole = whole + tin[s].astype(F32)
    tfull[dp] = whole.astype(BF16)
    tback = []
    for s in range(1, 8):
        ref = tfull.at[dp]
        tback.append(send(ref, ref, u_s.at[s], u_r.at[s], at_dp(s)[1]))
    for h in halves:
        landed(low_of(core, h, far[h]), h, 2)
        landed(high_of(core, h, far[h]), h, 3)
        fin.append(forward(part(core, h, far[h]), fin_s.at[h, 3], fin_r.at[h, 3], sib))

    def write(c, i):
        r = pl.ds(pl.multiple_of(c * 640, 16), 640)
        copy = pltpu.make_async_copy(out_ref.at[r], rows_hbm.at[r], rows_sem.at[i])
        copy.start()
        return copy

    written = [write(core, 0)]
    tap(8)
    lat_ref[...] = acc[...].astype(BF16)
    for copy in fin:
        copy.wait()
    written.append(write(1 - core, 1))
    for copy in tback:
        copy.wait()
    for n, i, f in places:
        small[16 * i : 16 * i + 16, 128 * n : 128 * n + 128] = tfull[f // 128, f % 128 : f % 128 + 16].astype(F32)
    for t in range(9):
        taps_ref[t] = small[20 * t : 20 * t + 20]
    for copy in sent:
        copy.wait_send()
    for copy in written:
        copy.wait()


ATTEND = 52


def whole_kernel(*refs):
    hbm, (rows_ref, taps_ref, lat_ref), scratch = refs[:7], refs[7:10], refs[10:]
    shared, scratch = scratch[:10], scratch[10:]
    latent, wq, wk, wv, wo, w, both, packed, lhs, parts = shared
    hidden, cot = both.at[0], both.at[1]
    one, two, three = scratch[:16], scratch[16 : 16 + ATTEND], scratch[16 + ATTEND :]
    windows, queries = first_kernel(hbm, latent, cot, wq, wk, wv, wo, w, hidden, packed, *one)
    attend_kernel(windows, queries, lhs, packed, parts, *two)
    rows_v, rows_sem, three = three[0], three[1], three[2:]
    finish_kernel(rows_ref, rows_sem, parts, both, wq, wk, wv, lhs, w, rows_v, taps_ref, lat_ref, *three)


def whole(*args):
    dma = pltpu.SemaphoreType.DMA
    vmem = pl.BlockSpec(memory_space=pltpu.VMEM)

    def b16(*shape):
        return pltpu.VMEM(shape, BF16)

    def f32(*shape):
        return pltpu.VMEM(shape, F32)

    shared = [
        b16(128, 640), b16(320, 640), b16(320, 640), b16(320, 640), b16(320, 640),
        b16(9, 640, 640), b16(2, 128, 640), b16(10, 128, 128), b16(8, 576, 256), b16(4, 128, 384),
    ]
    one = [
        dma((6,)), dma((9,)), b16(2, 64, 640), f32(656, 128), b16(16, 2, 32, 128), b16(18, 2, 32, 128),
        b16(3, 256, 640), f32(128, 640), f32(2, 128, 128), f32(128, 320),
        dma((2,)), dma((2,)), dma((16,)), dma((16,)), dma((16,)), dma((1,)),
    ]
    two = [
        b16(8, 640, 128), b16(8, 128, 640), b16(2, 512, 128), b16(512, 128), b16(512, 128), b16(512, 128), b16(512, 128),
        f32(64, 512), f32(64, 512),
        f32(8, 640, 512), f32(640, 512), b16(640, 512), b16(640, 512),
        f32(1, 512), f32(1, 512), f32(64, 512), f32(1, 512), f32(64, 512),
        f32(1, 512), f32(1, 512), f32(64, 512), f32(1, 512), f32(64, 512),
        f32(640, 128), b16(4, 640, 128), b16(4, 640, 128), b16(4, 640, 128), b16(4, 640, 128),
        f32(4, 72, 128), f32(4, 72, 128), f32(4, 8, 128), f32(128, 128), b16(3, 512, 128), b16(4, 3, 128, 128),
        dma((4,)), dma((4,)), dma((2, 4)), dma((2, 4)),
        dma((4, 2)), dma((4, 2)), dma((4, 2)), dma((4, 2)), dma((4, 2)), dma((4, 2)), dma((4, 2)), dma((4, 2)),
        dma((4,)), dma((4,)), dma((4,)), dma((4,)), dma((3, 4)), dma((3, 4)),
    ]
    three = [
        b16(1280, 640), dma((2,)),
        b16(8, 256, 640), b16(2, 64, 640), b16(3, 256, 640), f32(128, 640),
        f32(576, 640), f32(192, 640), b16(384, 128),
        b16(1280, 640), b16(640, 640), b16(2, 48, 640), b16(2, 32, 640), b16(2, 80, 640), b16(2, 80, 640),
        b16(2, 512, 128), b16(2, 4, 128, 128), b16(2, 128, 128), b16(8, 2, 16, 128), b16(2, 128, 128), b16(2, 512, 128),
        b16(2, 8, 128, 128), b16(16, 128, 128), b16(8, 128, 128),
        dma((2,)), dma((2,)), dma((7,)), dma((7,)), dma((8,)), dma((16,)), dma((8,)),
        dma((2,)), dma((2,)), dma((2, 4)), dma((2, 4)), dma((2, 4)), dma((2, 4)), dma((8,)), dma((8,)),
        dma((8,)), dma((8,)), dma((2, 4)), dma((2, 4)), dma((2, 4)), dma((2, 4)), dma((2, 4)), dma((2, 4)),
        dma((16,)), dma((16,)), dma((8,)), dma((8,)),
    ]
    return pl.pallas_call(
        whole_kernel,
        out_shape=(
            jax.ShapeDtypeStruct((1280, 640), BF16),
            jax.ShapeDtypeStruct((9, 20, 640), F32),
            jax.ShapeDtypeStruct((128, 640), BF16),
        ),
        in_specs=[pl.BlockSpec(memory_space=pl.ANY)] * 7,
        out_specs=(pl.BlockSpec(memory_space=pl.ANY), vmem, vmem),
        scratch_shapes=shared + one + two + three,
        compiler_params=pltpu.CompilerParams(
            collective_id=0, has_side_effects=True, vmem_limit_bytes=60 * 1024 * 1024
        ),
        name="whole",
    )(*args)


def hand_kernel(rows_ref, taps_ref, lat_ref, taps_out, lat_out, *rest):
    outs, (rows, wide, taps, lat, in_sem, out_sem) = rest[:4], rest[4:]
    step = AW // 2
    loads = [
        pltpu.make_async_copy(rows_ref.at[step * i : step * i + step], rows.at[i], in_sem.at[i]) for i in range(8)
    ]
    loads.append(pltpu.make_async_copy(taps_ref, taps, in_sem.at[8]))
    loads.append(pltpu.make_async_copy(lat_ref, lat, in_sem.at[9]))
    for copy in loads:
        copy.start()
    stores = []
    for i in range(10):
        loads[i].wait()
        if i < 8:
            wide[i] = rows[i].astype(F32)
            place = outs[i // 2].at[step * (i % 2) : step * (i % 2) + step]
            copy = pltpu.make_async_copy(wide.at[i], place, out_sem.at[i])
        elif i == 8:
            copy = pltpu.make_async_copy(taps, taps_out, out_sem.at[i])
        else:
            copy = pltpu.make_async_copy(lat, lat_out, out_sem.at[i])
        copy.start()
        stores.append(copy)
    for copy in stores:
        copy.wait()


def hand_out(rows, taps, grad_latent):
    anywhere = pl.BlockSpec(memory_space=pl.ANY)
    return pl.pallas_call(
        hand_kernel,
        out_shape=(
            jax.ShapeDtypeStruct(taps.shape, F32),
            jax.ShapeDtypeStruct(grad_latent.shape, BF16),
        )
        + (jax.ShapeDtypeStruct((AW, 640), F32),) * 4,
        in_specs=[anywhere] * 3,
        out_specs=(anywhere,) * 6,
        scratch_shapes=[
            pltpu.VMEM((8, AW // 2, 640), BF16),
            pltpu.VMEM((8, AW // 2, 640), F32),
            pltpu.VMEM(taps.shape, F32),
            pltpu.VMEM(grad_latent.shape, BF16),
            pltpu.SemaphoreType.DMA((10,)),
            pltpu.SemaphoreType.DMA((10,)),
        ],
        compiler_params=pltpu.CompilerParams(vmem_limit_bytes=60 * 1024 * 1024),
        name="hand_out",
    )(rows, taps, grad_latent)


def body(latent, cotangent, conv_weight, query_weight, key_weight, value_weight, out_weight):
    sums = whole(
        latent.reshape(128, 640), cotangent.reshape(128, 640), out_weight, key_weight.T, value_weight.T,
        query_weight.T, conv_weight.reshape(9, 640, 640),
    )
    taps, grad_latent, query, key, value, out = hand_out(*sums)
    return (grad_latent.reshape(latent.shape), taps.reshape(3, 3, 20, 640), query.T, key.T, value.T, out)


def solution(mesh):
    placed = (P("dp", "patch", None, None), P("dp", "patch", None, None), P(), P(), P(), P(), P())
    return jax.shard_map(
        body,
        mesh=mesh,
        in_specs=placed,
        out_specs=(P("dp", "patch", None, None), P(None, None, "patch", None), P(), P(), P(), P()),
        check_vma=False,
    )
```
